32 devices in a mesh: kv: 4 (over y, x), blk: 8 (over z, core).
Axes of the slice: x: 2, y: 2, z: 4, core: 2. Of those that a mesh axis runs over, the one named last changes fastest.
Arguments:
- prefix_pool: bfloat16 [4, 192, 64, 512], P('kv', 'blk'), may hold values from -6 to 6
- slot_page: int32 [192], P('blk'), may hold values from 0 to 191, as said below
- prompt_len: int32 [3], replicated, may hold values from 1 to 6048, 12096 in all
- request_ids: int32 [48], replicated, may hold values from 0 to 47, each once
- tail_len: int32 [48], P('blk'), may hold values from 1 to 128, 3072 in all
- tail_cache: bfloat16 [4, 48, 128, 512], P('kv', 'blk'), may hold values from -6 to 6
- queries: bfloat16 [48, 2, 2048], P('blk', None, 'kv'), may hold values from -120 to 120
- new_kv: bfloat16 [4, 48, 2, 512], P('kv', 'blk'), may hold values from -5.1 to 5.1
- hidden: bfloat16 [48, 2, 2048], P('blk'), may hold values from -4 to 4
- out_weight: bfloat16 [2048, 2048], P('kv'), may hold values from -0.125 to 0.125
- norm_gain: float32 [2048], replicated, may hold values from 0.1 to 1.9
- score_weight: float32 [2048], replicated, may hold values from -0.125 to 0.125
Outputs:
- hidden_out: bfloat16 [48, 2, 2048], P('blk')
- scores_out: float32 [48], P('blk')
The draws below stay inside these ranges and needn't reach their ends.
Inputs may be any that keep to these rules, and one draw needn't show every extreme that they name: `slot_page`: the pages of all prompts fit the pool; every logical page number appears once. Request slot r serves sample request_ids[r] % 16 of prompt request_ids[r] // 16; every pair once.
All inputs are finite; a program needn't handle non-finite values. No bound on the sum of `tail_len` on one device may be relied on, other than what follows from the above.
Results may differ from the reference program's by a relative error of at most 0.02.
Values may be sent and summed in bfloat16 or wider, within the bound.
No kernel may reach another device: no remote copies, remote signals or barrier semaphores. Data moves between devices by JAX's collectives and lax.ppermute only.
A program may use at most 64 MiB of HBM per device.

```python
import math
import jax
import jax.numpy as jnp
import numpy as np
from jax import lax

D = 2048
HEAD = 256
KVHEADS = 4
GROUP = 2
QHEADS = 8
SAMPLES = 16
DRAFT = 2
PAGE = 64
TAIL = 128
REQS = 48
PROMPTS = 3
PAGES = 192
PREFIX_TOTAL = 12096
PROMPT_MOST = 6048
TAIL_TOTAL = 3072


def draw_slot_page(key, part):
    base = jax.random.fold_in(key, 57)
    key_move, key_dest = jax.random.split(base, 2)
    order = jnp.arange(PAGES, dtype=jnp.int32)
    mover = (jax.random.randint(key_move, (PAGES,), 0, 8) == 0).astype(jnp.int32)
    target = jax.random.randint(key_dest, (PAGES,), 0, PAGES)
    place = jnp.where(mover == 1, target, order)
    score = (place * 2 + mover) * PAGES + order
    return jnp.argsort(score, stable=True).astype(jnp.int32)


def draw_joint(key):
    base = jax.random.fold_in(key, 31)
    key_query, key_pairs = jax.random.split(base, 2)
    queries = jnp.clip(jax.random.normal(key_query, (REQS, DRAFT, QHEADS * HEAD), jnp.float32), -5.0, 5.0)
    fresh = jnp.clip(jax.random.normal(key_pairs, (KVHEADS, REQS, DRAFT, 2 * HEAD), jnp.float32), -5.0, 5.0)
    return (queries, fresh)


def draw_queries(key, part):
    return draw_joint(key)[0].astype(jnp.bfloat16)


def draw_new_kv(key, part):
    return draw_joint(key)[1].astype(jnp.bfloat16)


def shard_levels(rng, extent, cuts, least, high):
    level = 1.0
    for dim, parts in cuts:
        steps = jax.random.uniform(jax.random.fold_in(jax.random.fold_in(rng, 6), dim), (parts,), jnp.float32, least / len(cuts), high / len(cuts))
        level = level * jnp.repeat(jnp.exp(steps), extent[dim] // parts).reshape((-1,) + (1,) * (len(extent) - 1 - dim))
    return level


def length_profile(amount, total, bound, slope):
    portions = [(1 << 20) // math.isqrt(standing ** slope) + 1 for standing in range(2, amount + 1)]
    rest, given = total - bound - (amount - 1), [1] * (amount - 1)
    while rest > 0:
        candidates = [i for i in range(amount - 1) if given[i] < bound]
        mass, remaining = sum([portions[i] for i in candidates]), rest
        for i in candidates:
            extra = min(bound - given[i], max(1, remaining * portions[i] // mass), rest)
            given[i] = given[i] + extra
            rest = rest - extra
    return np.array([bound] + given)


def ragged_sizes(own_key, number_of, total, most, lean):
    if number_of == 2:
        one = jax.random.randint(own_key, (), max(1, total - most), min(most, total - 1) + 1)
        return jnp.stack([one, total - one])
    tallies = jnp.asarray(length_profile(number_of, total, most, lean), jnp.int32)
    pairs = (number_of - 1) // 2
    donor, sink = tallies[1:1 + 2 * pairs:2], tallies[2:2 + 2 * pairs:2]
    slack = jnp.minimum(donor - 1, most - sink)
    shifted = jax.random.randint(jax.random.fold_in(own_key, 1), (pairs,), 0, 1 << 20) % (slack + 1)
    tallies = tallies.at[1:1 + 2 * pairs:2].set(donor - shifted).at[2:2 + 2 * pairs:2].set(sink + shifted)
    return tallies[jax.random.permutation(jax.random.fold_in(own_key, 2), number_of)]


def centred(own_key, shape, scale, reach, cuts=(), kind=jnp.bfloat16):
    result = scale * jax.random.normal(own_key, shape, jnp.float32)
    if cuts:
        result = result * shard_levels(own_key, shape, cuts, -0.22, 0.18)
    return jnp.clip(result, -reach, reach).astype(kind)


def setup_inputs(seed: int = 0) -> dict:
    key_list = jax.random.split(jax.random.key(seed), 13)
    return {
        "prefix_pool": centred(key_list[0], (KVHEADS, PAGES, PAGE, 2 * HEAD), 1.0, 6.0, ((0, 4), (1, 8))),
        "slot_page": draw_slot_page(jax.random.fold_in(key_list[12], 71), 0),
        "prompt_len": ragged_sizes(key_list[2], PROMPTS, PREFIX_TOTAL, PROMPT_MOST, 2).astype(jnp.int32),
        "request_ids": jax.random.permutation(key_list[3], REQS).astype(jnp.int32),
        "tail_len": ragged_sizes(key_list[4], REQS, TAIL_TOTAL, TAIL, 2).astype(jnp.int32),
        "tail_cache": centred(key_list[5], (KVHEADS, REQS, TAIL, 2 * HEAD), 1.0, 6.0, ((0, 4), (1, 8))),
        "queries": draw_queries(jax.random.fold_in(key_list[12], 71), 0),
        "new_kv": draw_new_kv(jax.random.fold_in(key_list[12], 71), 0),
        "hidden": centred(key_list[8], (REQS, DRAFT, D), 0.5, 4.0, ((0, 8),)),
        "out_weight": centred(key_list[9], (QHEADS * HEAD, D), (QHEADS * HEAD) ** -0.5, 0.125, ((0, 4),)),
        "norm_gain": jnp.clip(1.0 + 0.18 * jax.random.normal(key_list[10], (D,), jnp.float32), 0.1, 1.9),
        "score_weight": centred(key_list[11], (D,), D ** -0.5, 0.125, (), jnp.float32),
    }


NEG_FLOOR = -1e+30

def page_layout(slot_page, prompt_len, page_tokens):
    needed = (prompt_len + page_tokens - 1) // page_tokens
    page_ends = jnp.cumsum(needed).astype(jnp.int32)
    page_starts = page_ends - needed
    page_owner = lax.optimization_barrier(jnp.sum((slot_page[:, None] >= page_ends[None, :]).astype(jnp.int32), axis=1))
    in_use = page_owner < prompt_len.shape[0]
    page_owner = jnp.minimum(page_owner, prompt_len.shape[0] - 1)
    offset = slot_page - page_starts[page_owner]
    position = offset[:, None] * page_tokens + jnp.arange(page_tokens, dtype=jnp.int32)[None, :]
    live_keys = in_use[:, None] & (position < prompt_len[page_owner][:, None])
    return (page_owner, live_keys)

def home_slots(request_ids):
    total_count = request_ids.shape[0]
    return jnp.zeros((total_count,), jnp.int32).at[request_ids].set(jnp.arange(total_count, dtype=jnp.int32))

def prefix_sums(all_queries, page_pool, slot_rows, live_keys, total_count):
    page_count = page_pool.shape[0]
    score_scale = HEAD ** (-0.5)
    row_count = DRAFT * GROUP
    picked = all_queries[slot_rows].reshape(page_count, -1, HEAD).astype(jnp.float32)
    logits = jnp.einsum('prh,pkh->prk', picked, page_pool[:, :, :HEAD].astype(jnp.float32)) * score_scale
    logits = jnp.where(live_keys[:, None, :], logits, NEG_FLOOR)
    flat_rows = slot_rows.reshape(-1)
    slot_peak = lax.optimization_barrier(jnp.max(logits, axis=2)).reshape(-1, row_count)
    prefix_peak = jnp.full((total_count, row_count), NEG_FLOOR, jnp.float32).at[flat_rows].max(slot_peak)
    ref_peak = prefix_peak[slot_rows].reshape(page_count, -1)
    weights = jnp.where(live_keys[:, None, :], jnp.exp(logits - ref_peak[:, :, None]), 0.0)
    slot_den = lax.optimization_barrier(jnp.sum(weights, axis=2)).reshape(-1, row_count)
    rounded = lax.optimization_barrier(weights.astype(jnp.bfloat16)).astype(jnp.float32)
    slot_num = jnp.einsum('prk,pkh->prh', rounded, page_pool[:, :, HEAD:].astype(jnp.float32)).reshape(-1, row_count, HEAD)
    prefix_num = jnp.zeros((total_count, row_count, HEAD), jnp.float32).at[flat_rows].add(slot_num)
    prefix_den = jnp.zeros((total_count, row_count), jnp.float32).at[flat_rows].add(slot_den)
    return (prefix_peak, prefix_num, prefix_den)

def own_attention(own_queries, tail_block, fresh_block, tail_len, prefix_peak, prefix_num, prefix_den):
    req_count = own_queries.shape[0]
    row_count = DRAFT * GROUP
    score_scale = HEAD ** (-0.5)
    flat_queries = own_queries.reshape(req_count, row_count, HEAD).astype(jnp.float32)
    tail_logits = jnp.einsum('rqh,rkh->rqk', flat_queries, tail_block[:, :, :HEAD].astype(jnp.float32)) * score_scale
    tail_live = (jnp.arange(tail_block.shape[1], dtype=jnp.int32)[None, :] < tail_len[:, None])[:, None, :]
    tail_logits = jnp.where(tail_live, tail_logits, NEG_FLOOR)
    fresh_logits = jnp.einsum('rqh,rkh->rqk', flat_queries, fresh_block[:, :, :HEAD].astype(jnp.float32)) * score_scale
    fresh_live = (jnp.arange(DRAFT, dtype=jnp.int32)[None, :] <= (jnp.arange(row_count, dtype=jnp.int32) // GROUP)[:, None])[None]
    fresh_logits = jnp.where(fresh_live, fresh_logits, NEG_FLOOR)
    own_peak = jnp.maximum(lax.optimization_barrier(jnp.max(tail_logits, axis=2)), lax.optimization_barrier(jnp.max(fresh_logits, axis=2)))
    top_peak = jnp.maximum(prefix_peak, own_peak)
    tail_weights = jnp.where(tail_live, jnp.exp(tail_logits - top_peak[:, :, None]), 0.0)
    fresh_weights = jnp.where(fresh_live, jnp.exp(fresh_logits - top_peak[:, :, None]), 0.0)
    carried = jnp.exp(prefix_peak - top_peak)
    tail_round = lax.optimization_barrier(tail_weights.astype(jnp.bfloat16)).astype(jnp.float32)
    fresh_round = lax.optimization_barrier(fresh_weights.astype(jnp.bfloat16)).astype(jnp.float32)
    numer = prefix_num * carried[:, :, None]
    numer = numer + jnp.einsum('rqk,rkh->rqh', tail_round, tail_block[:, :, HEAD:].astype(jnp.float32))
    numer = numer + jnp.einsum('rqk,rkh->rqh', fresh_round, fresh_block[:, :, HEAD:].astype(jnp.float32))
    denom = prefix_den * carried + lax.optimization_barrier(jnp.sum(tail_weights, axis=2)) + lax.optimization_barrier(jnp.sum(fresh_weights, axis=2))
    return (numer / denom[:, :, None]).astype(jnp.bfloat16).reshape(req_count, DRAFT, GROUP * HEAD)

def reference(prefix_pool, slot_page, prompt_len, request_ids, tail_len, tail_cache, queries, new_kv, hidden, out_weight, norm_gain, score_weight):
    page_owner, live_keys = page_layout(slot_page, prompt_len, PAGE)
    home_rows = home_slots(request_ids)
    slot_rows = home_rows[page_owner[:, None] * SAMPLES + jnp.arange(SAMPLES, dtype=jnp.int32)[None, :]]
    head_width = GROUP * HEAD
    heads_out = []
    for head_index in range(KVHEADS):
        head_queries = queries[:, :, head_index * head_width:(head_index + 1) * head_width]
        prefix_peak, prefix_num, prefix_den = prefix_sums(head_queries, prefix_pool[head_index], slot_rows, live_keys, REQS)
        heads_out.append(own_attention(head_queries, tail_cache[head_index], new_kv[head_index], tail_len, prefix_peak, prefix_num, prefix_den))
    attention = jnp.concatenate(heads_out, axis=2)
    projected = jnp.dot(attention.reshape(-1, QHEADS * HEAD), out_weight, preferred_element_type=jnp.float32)
    hidden_out = (hidden.astype(jnp.float32) + projected.reshape(hidden.shape)).astype(jnp.bfloat16)
    last_hidden = hidden_out[:, -1, :].astype(jnp.float32)
    normed = last_hidden * lax.rsqrt(lax.optimization_barrier(jnp.mean(last_hidden * last_hidden, axis=-1, keepdims=True)) + 1e-06) * norm_gain
    scores_out = lax.optimization_barrier(jnp.sum(normed * score_weight, axis=-1))
    return (hidden_out, scores_out)
```

```python
import functools

import jax
import jax.numpy as jnp
from jax import lax
from jax.experimental import pallas as pl
from jax.experimental.pallas import tpu as pltpu
from jax.sharding import PartitionSpec as P

SAMPLES = 16
LANES = 128
FLOOR = -(2.0**100)
LOG2E = 1.4426950408889634
VMEM = pl.BlockSpec(memory_space=pltpu.VMEM)
SMEM = pl.BlockSpec(memory_space=pltpu.SMEM)


def round_up(value, unit):
    return (value + unit - 1) // unit * unit


def iota(shape, dim):
    return lax.broadcasted_iota(jnp.int32, shape, dim)


def rounded_peak(peak):
    return peak.astype(jnp.bfloat16).astype(jnp.float32)


def softmax_parts(logits):
    peak = rounded_peak(jnp.max(logits, axis=1, keepdims=True))
    weights = jnp.exp2(logits - peak)
    return peak, weights, jnp.sum(weights, axis=1, keepdims=True)


def pack_stats(peak, den):
    high = den.astype(jnp.bfloat16).astype(jnp.float32)
    lane = iota((peak.shape[0], LANES), 1)
    stats = jnp.where(lane == 0, peak, jnp.where(lane == 1, high, den - high))
    return jnp.where(lane < 3, stats, 0.0)


def unpack_stats(stats):
    stats = stats.astype(jnp.float32)
    return stats[:, 0:1], stats[:, 1:2] + stats[:, 2:3]


def spread_rows(dest, base, block, heads, head_size, rows):
    reqs, drafts, _ = block.shape
    pad = rows - reqs * drafts
    for c in range(heads):
        cols = pl.ds(c * head_size, head_size)
        for r in range(reqs):
            dest[pl.ds(base + c * rows + r * drafts, drafts), :] = block[r, :, cols]
        if pad:
            dest[pl.ds(base + c * rows + reqs * drafts, pad), :] = jnp.zeros((pad, head_size), dest.dtype)


def layout_kernel(device_of, slots, local, rows, heads, drafts, page_tokens,
                  ids_ref, len_ref, page_ref, low_ref, high_ref, key_ref, start_ref):
    me = lax.axis_index("blk")
    prompts = len_ref.shape[0]

    def place(p, start):
        start_ref[p] = start
        return start + (len_ref[p] + page_tokens - 1) // page_tokens * page_tokens

    lax.fori_loop(0, prompts, place, jnp.int32(0))
    request = iota((rows, LANES), 0) // drafts

    def one(j, _):
        device = device_of(j, me)
        low = jnp.zeros((rows, LANES), jnp.int32)
        high = low
        for r in range(local):
            prompt = ids_ref[device * local + r] // SAMPLES
            start = start_ref[prompt]
            low = jnp.where(request == r, start, low)
            high = jnp.where(request == r, start + len_ref[prompt], high)
        for c in range(heads):
            place_at = pl.ds(pl.multiple_of((j * heads + c) * rows, rows), rows)
            low_ref[place_at, :] = low
            high_ref[place_at, :] = high
        return 0

    lax.fori_loop(0, slots, one, 0, unroll=slots <= 8)
    lane = iota((8, page_tokens), 1)
    for s in range(page_ref.shape[0]):
        key_ref[:, pl.ds(s * page_tokens, page_tokens)] = lane + page_ref[s] * page_tokens


def prefix_kernel(heads, rows, scale, q_ref, low_ref, high_ref, key_ref, pool_ref, *rest):
    out_ref, q_rows = rest
    slots = q_ref.shape[0]
    head_size = pool_ref.shape[2] // 2
    keys = pool_ref.shape[0] * pool_ref.shape[1]
    for j in range(slots):
        spread_rows(q_rows, j * heads * rows, q_ref.at[j], heads, head_size, rows)
    logits = lax.dot_general(
        q_rows[...], pool_ref[:, :, :head_size].reshape(keys, head_size),
        (((1,), (1,)), ((), ())), preferred_element_type=jnp.float32,
    )
    low, high = low_ref[...], high_ref[...]
    parts = []
    for k in range(0, keys, LANES):
        key = key_ref[0:1, k:k + LANES]
        live = (key >= low) & (key < high)
        parts.append(jnp.where(live, logits[:, k:k + LANES] * scale, FLOOR))
    peak, weights, den = softmax_parts(jnp.concatenate(parts, axis=1))
    num = jnp.dot(
        weights.astype(jnp.bfloat16), pool_ref[:, :, head_size:].reshape(keys, head_size),
        preferred_element_type=jnp.float32,
    )
    per = heads * rows
    out_ref[:, :, :head_size] = num.reshape(slots, per, head_size).astype(out_ref.dtype)
    out_ref[:, :, head_size:] = pack_stats(peak, den).reshape(slots, per, LANES).astype(out_ref.dtype)


def own_kernel(heads, rows, scale, len_ref, q_ref, tail_ref, fresh_ref, out_ref, q_rows, f_rows):
    reqs, drafts, _ = q_ref.shape
    tail = tail_ref.shape[1]
    head_size = tail_ref.shape[2] // 2
    spread_rows(q_rows, 0, q_ref, heads, head_size, rows)
    spread_rows(f_rows, 0, fresh_ref, 2, head_size, rows)
    queries = q_rows[...]
    contract = (((1,), (1,)), ((), ()))
    logits = lax.dot_general(
        queries, tail_ref[:, :, :head_size].reshape(reqs * tail, head_size),
        contract, preferred_element_type=jnp.float32,
    )
    total = heads * rows
    row = iota((total, tail), 0) % rows
    lane = iota((total, tail), 1)
    parts = []
    for r in range(reqs):
        live = (row // drafts == r) & (lane < len_ref[r])
        parts.append(jnp.where(live, logits[:, r * tail:(r + 1) * tail] * scale, FLOOR))
    fresh = lax.dot_general(
        queries, f_rows[0:rows, :], contract, preferred_element_type=jnp.float32
    )
    row = iota((total, rows), 0) % rows
    key = iota((total, rows), 1)
    live = (row // drafts == key // drafts) & (key % drafts <= row % drafts)
    fresh = jnp.where(live, fresh * scale, FLOOR)
    logits = jnp.concatenate(parts, axis=1)
    peak = jnp.maximum(
        jnp.max(logits, axis=1, keepdims=True), jnp.max(fresh, axis=1, keepdims=True)
    )
    peak = rounded_peak(peak)
    weights = jnp.exp2(logits - peak)
    fresh = jnp.exp2(fresh - peak)
    den = jnp.sum(weights, axis=1, keepdims=True) + jnp.sum(fresh, axis=1, keepdims=True)
    num = jnp.dot(
        weights.astype(jnp.bfloat16), tail_ref[:, :, head_size:].reshape(reqs * tail, head_size),
        preferred_element_type=jnp.float32,
    )
    num = num + jnp.dot(
        fresh.astype(jnp.bfloat16), f_rows[rows:2 * rows, :], preferred_element_type=jnp.float32
    )
    out_ref[:, :head_size] = num
    out_ref[:, head_size:] = pack_stats(peak, den)


def summed_parts(blocks, head_size):
    nums = [b[:, :head_size].astype(jnp.float32) for b in blocks]
    stats = [unpack_stats(b[:, head_size:]) for b in blocks]
    peak = functools.reduce(jnp.maximum, [s[0] for s in stats])
    factors = [jnp.exp2(s[0] - peak) for s in stats]
    num = sum(n * f for n, f in zip(nums, factors))
    den = sum(s[1] * f for s, f in zip(stats, factors))
    return num, peak, den


def merge_kernel(head_size, a_ref, b_ref, *out_refs):
    for j, out_ref in enumerate(out_refs):
        num, peak, den = summed_parts([a_ref[j], b_ref[j]], head_size)
        out_ref[:, :head_size] = num.astype(out_ref.dtype)
        out_ref[:, head_size:] = pack_stats(peak, den).astype(out_ref.dtype)


def project(num, den, weight_ref, out_ref, heads, rows):
    reqs, drafts, _ = out_ref.shape
    attention = (num / den).astype(jnp.bfloat16)
    head_size = attention.shape[1]
    value = sum(
        jnp.dot(
            attention[c * rows:(c + 1) * rows, :], weight_ref[c * head_size:(c + 1) * head_size, :],
            preferred_element_type=jnp.float32,
        )
        for c in range(heads)
    ).astype(out_ref.dtype)
    for r in range(reqs):
        out_ref[r] = value[r * drafts:(r + 1) * drafts, :]


def combine_kernel(heads, rows, head_size, *refs):
    *block_refs, weight_ref, out_ref = refs
    num, _, den = summed_parts([b[...] for b in block_refs], head_size)
    project(num, den, weight_ref, out_ref, heads, rows)


def combine_many_kernel(heads, rows, head_size, own_ref, many_ref, weight_ref, out_ref):
    def one(j, carry):
        num, peak, den = carry
        block = many_ref[j]
        next_peak, next_den = unpack_stats(block[:, head_size:])
        top = jnp.maximum(peak, next_peak)
        old, new = jnp.exp2(peak - top), jnp.exp2(next_peak - top)
        return num * old + block[:, :head_size].astype(jnp.float32) * new, top, den * old + next_den * new

    own = own_ref[...]
    carry = (own[:, :head_size], *unpack_stats(own[:, head_size:]))
    num, _, den = lax.fori_loop(0, many_ref.shape[0], one, carry)
    project(num, den, weight_ref, out_ref, heads, rows)


def final_kernel(*refs):
    *part_refs, hidden_ref, gain_ref, score_ref, out_ref, scores_ref = refs
    reqs, drafts, width = hidden_ref.shape
    mix = gain_ref[...] * score_ref[...]
    lane = iota((1, LANES), 1)
    scores = jnp.zeros((1, LANES), jnp.float32)
    for r in range(reqs):
        total = sum(p[r].astype(jnp.float32) for p in part_refs)
        value = (hidden_ref[r].astype(jnp.float32) + total).astype(out_ref.dtype)
        out_ref[r] = value
        last = value.astype(jnp.float32)[drafts - 1:drafts, :]
        square = jnp.sum(last * last, axis=1, keepdims=True) / width
        score = jnp.sum(last * mix, axis=1, keepdims=True) * lax.rsqrt(square + 1e-06)
        scores = jnp.where(lane == r, score, scores)
    scores_ref[...] = scores


def body(sizes, prefix_pool, slot_page, prompt_len, request_ids, tail_len, tail_cache, queries, new_kv, hidden,
         out_weight, norm_gain, score_weight):
    blk, kv = sizes
    pool = prefix_pool[0]
    page_count, page_tokens, head_pair = pool.shape
    head_size = head_pair // 2
    local, drafts, head_width = queries.shape
    heads = head_width // head_size
    rows = round_up(local * drafts, 16)
    per = heads * rows
    keys = page_count * page_tokens
    width = hidden.shape[2]
    scale = head_size ** (-0.5) * LOG2E
    paired = blk in (2, 4, 8)
    half = blk // 2

    def swap(x, axis, size, mask):
        return lax.ppermute(x, axis, [(i, i ^ mask) for i in range(size)])

    def device_of(j, me):
        if not paired:
            return j
        return me ^ (j * 2) if isinstance(j, int) and j < half else me ^ (j % half * 2 + j // half)

    low, high, key = pl.pallas_call(
        functools.partial(layout_kernel, device_of, blk, local, rows, heads, drafts, page_tokens),
        out_shape=(
            jax.ShapeDtypeStruct((blk * per, LANES), jnp.int32),
            jax.ShapeDtypeStruct((blk * per, LANES), jnp.int32),
            jax.ShapeDtypeStruct((8, keys), jnp.int32),
        ),
        in_specs=[SMEM] * 3,
        out_specs=(VMEM,) * 3,
        scratch_shapes=[pltpu.SMEM(prompt_len.shape, jnp.int32)],
        name="key_ranges",
    )(request_ids, prompt_len, slot_page)

    own = pl.pallas_call(
        functools.partial(own_kernel, heads, rows, scale),
        out_shape=jax.ShapeDtypeStruct((per, head_size + LANES), jnp.float32),
        in_specs=[SMEM] + [VMEM] * 3,
        out_specs=VMEM,
        scratch_shapes=[
            pltpu.VMEM((per, head_size), jnp.bfloat16),
            pltpu.VMEM((2 * rows, head_size), jnp.bfloat16),
        ],
        name="own_keys",
    )(tail_len, queries, tail_cache[0], new_kv[0])

    def prefix(block, first):
        slots = block.shape[0]
        step = min(slots, 4)
        grid = slots // step
        offset = first // step
        return pl.pallas_call(
            functools.partial(prefix_kernel, heads, rows, scale),
            out_shape=jax.ShapeDtypeStruct((slots, per, head_size + LANES), jnp.bfloat16),
            grid=(grid,),
            in_specs=[
                pl.BlockSpec((step, local, drafts, head_width), lambda i: (i, 0, 0, 0)),
                pl.BlockSpec((step * per, LANES), lambda i: (i + offset, 0)),
                pl.BlockSpec((step * per, LANES), lambda i: (i + offset, 0)),
                pl.BlockSpec((8, keys), lambda i: (0, 0)),
                pl.BlockSpec((page_count, page_tokens, head_pair), lambda i: (0, 0, 0)),
            ],
            out_specs=pl.BlockSpec((step, per, head_size + LANES), lambda i: (i, 0, 0)),
            scratch_shapes=[pltpu.VMEM((step * per, head_size), jnp.bfloat16)],
            compiler_params=pltpu.CompilerParams(vmem_limit_bytes=32 * 1024 * 1024),
            name="prefix_keys",
        )(block, low, high, key, pool)

    partial_shape = jax.ShapeDtypeStruct((local, drafts, width), jnp.bfloat16)
    limit = pltpu.CompilerParams(vmem_limit_bytes=32 * 1024 * 1024)
    if paired:
        column = [queries] + [swap(queries, "blk", blk, 2 * j) for j in range(1, half)]
        mine = jnp.stack(column)
        theirs = swap(mine, "blk", blk, 1)
        sums_mine = prefix(mine, 0)
        sums_theirs = prefix(theirs, half)
        back = swap(sums_theirs, "blk", blk, 1)
        block_shape = jax.ShapeDtypeStruct((per, head_size + LANES), jnp.bfloat16)
        merged = pl.pallas_call(
            functools.partial(merge_kernel, head_size),
            out_shape=(block_shape,) * half,
            in_specs=[VMEM] * 2,
            out_specs=(VMEM,) * half,
            name="merge_cores",
        )(sums_mine, back)
        blocks = [merged[0]] + [swap(merged[j], "blk", blk, 2 * j) for j in range(1, half)]
        share = pl.pallas_call(
            functools.partial(combine_kernel, heads, rows, head_size),
            out_shape=partial_shape,
            in_specs=[VMEM] * (half + 2),
            out_specs=VMEM,
            compiler_params=limit,
            name="combine_project",
        )(own, *blocks, out_weight)
    else:
        gathered = lax.all_gather(queries, "blk", axis=0)
        blocks = lax.all_to_all(prefix(gathered, 0), "blk", 0, 0)
        share = pl.pallas_call(
            functools.partial(combine_many_kernel, heads, rows, head_size),
            out_shape=partial_shape,
            in_specs=[VMEM] * 3,
            out_specs=VMEM,
            compiler_params=limit,
            name="combine_project",
        )(own, blocks, out_weight)
    if kv in (2, 4):
        shares = [share] + [swap(share, "kv", kv, j) for j in range(1, kv)]
    else:
        shares = [lax.psum(share, "kv")]
    hidden_out, scores = pl.pallas_call(
        final_kernel,
        out_shape=(
            jax.ShapeDtypeStruct(hidden.shape, hidden.dtype),
            jax.ShapeDtypeStruct((1, LANES), jnp.float32),
        ),
        in_specs=[VMEM] * (len(shares) + 3),
        out_specs=(VMEM, VMEM),
        name="residual_scores",
    )(*shares, hidden, norm_gain.reshape(1, width), score_weight.reshape(1, width))
    return hidden_out, scores[0, :local]


def solution(mesh):
    in_specs = (
        P("kv", "blk", None, None),
        P("blk"),
        P(),
        P(),
        P("blk"),
        P("kv", "blk", None, None),
        P("blk", None, "kv"),
        P("kv", "blk", None, None),
        P("blk", None, None),
        P("kv", None),
        P(),
        P(),
    )
    out_specs = (P("blk", None, None), P("blk"))
    sizes = (mesh.shape["blk"], mesh.shape["kv"])
    return jax.shard_map(
        functools.partial(body, sizes), mesh=mesh, in_specs=in_specs, out_specs=out_specs, check_vma=False
    )
```

```python
import functools

import jax
import jax.numpy as jnp
from jax import lax
from jax.experimental import pallas as pl
from jax.experimental.pallas import tpu as pltpu
from jax.sharding import PartitionSpec as P

SAMPLES = 16
LANES = 128
FLOOR = -(2.0**100)
LOG2E = 1.4426950408889634
VMEM = pl.BlockSpec(memory_space=pltpu.VMEM)
SMEM = pl.BlockSpec(memory_space=pltpu.SMEM)


def round_up(value, unit):
    return (value + unit - 1) // unit * unit


def cost(flops, size):
    return pl.CostEstimate(flops=flops, bytes_accessed=size, transcendentals=0)


def vmem(mebibytes):
    return pltpu.CompilerParams(vmem_limit_bytes=mebibytes * 1024 * 1024)


def iota(shape, dim):
    return lax.broadcasted_iota(jnp.int32, shape, dim)


def rounded_peak(peak):
    return peak.astype(jnp.bfloat16).astype(jnp.float32)


def softmax_parts(logits):
    peak = rounded_peak(jnp.max(logits, axis=1, keepdims=True))
    weights = jnp.exp2(logits - peak)
    return peak, weights, jnp.sum(weights, axis=1, keepdims=True)


def pack_stats(peak, den):
    high = den.astype(jnp.bfloat16).astype(jnp.float32)
    lane = iota((peak.shape[0], LANES), 1)
    stats = jnp.where(lane == 0, peak, jnp.where(lane == 1, high, den - high))
    return jnp.where(lane < 3, stats, 0.0)


def unpack_stats(stats):
    stats = stats.astype(jnp.float32)
    return stats[:, 0:1], stats[:, 1:2] + stats[:, 2:3]


def spread_rows(dest, base, block, heads, head_size, rows):
    reqs, drafts, _ = block.shape
    pad = rows - reqs * drafts
    for c in range(heads):
        cols = pl.ds(c * head_size, head_size)
        for r in range(reqs):
            dest[pl.ds(base + c * rows + r * drafts, drafts), :] = block[r, :, cols]
        if pad:
            dest[pl.ds(base + c * rows + reqs * drafts, pad), :] = jnp.zeros((pad, head_size), dest.dtype)


def layout_kernel(device_of, slots, local, rows, heads, drafts, page_tokens,
                  ids_ref, len_ref, page_ref, low_ref, high_ref, key_ref, start_ref):
    me = lax.axis_index("blk")
    prompts = len_ref.shape[0]

    def place(p, start):
        start_ref[p] = start
        return start + (len_ref[p] + page_tokens - 1) // page_tokens * page_tokens

    lax.fori_loop(0, prompts, place, jnp.int32(0))
    request = iota((rows, LANES), 0) // drafts

    def one(j, _):
        device = device_of(j, me)
        low = jnp.zeros((rows, LANES), jnp.int32)
        high = low
        for r in range(local):
            prompt = ids_ref[device * local + r] // SAMPLES
            start = start_ref[prompt]
            low = jnp.where(request == r, start, low)
            high = jnp.where(request == r, start + len_ref[prompt], high)
        for c in range(heads):
            place_at = pl.ds(pl.multiple_of((j * heads + c) * rows, rows), rows)
            low_ref[place_at, :] = low
            high_ref[place_at, :] = high
        return 0

    lax.fori_loop(0, slots, one, 0, unroll=slots <= 8)
    lane = iota((8, page_tokens), 1)
    for s in range(page_ref.shape[0]):
        key_ref[:, pl.ds(s * page_tokens, page_tokens)] = lane + page_ref[s] * page_tokens


def prefix_kernel(heads, rows, scale, q_ref, low_ref, high_ref, key_ref, pool_ref, *rest):
    out_ref, q_rows = rest
    slots = q_ref.shape[0]
    head_size = pool_ref.shape[2] // 2
    keys = pool_ref.shape[0] * pool_ref.shape[1]
    for j in range(slots):
        spread_rows(q_rows, j * heads * rows, q_ref.at[j], heads, head_size, rows)
    logits = lax.dot_general(
        q_rows[...], pool_ref[:, :, :head_size].reshape(keys, head_size),
        (((1,), (1,)), ((), ())), preferred_element_type=jnp.float32,
    )
    low, high = low_ref[...], high_ref[...]
    parts = []
    for k in range(0, keys, LANES):
        key = key_ref[0:1, k:k + LANES]
        live = (key >= low) & (key < high)
        parts.append(jnp.where(live, logits[:, k:k + LANES] * scale, FLOOR))
    peak, weights, den = softmax_parts(jnp.concatenate(parts, axis=1))
    num = jnp.dot(
        weights.astype(jnp.bfloat16), pool_ref[:, :, head_size:].reshape(keys, head_size),
        preferred_element_type=jnp.float32,
    )
    per = heads * rows
    out_ref[:, :, :head_size] = num.reshape(slots, per, head_size).astype(out_ref.dtype)
    out_ref[:, :, head_size:] = pack_stats(peak, den).reshape(slots, per, LANES).astype(out_ref.dtype)


def own_kernel(heads, rows, scale, len_ref, q_ref, tail_ref, fresh_ref, out_ref, q_rows, f_rows):
    reqs, drafts, _ = q_ref.shape
    tail = tail_ref.shape[1]
    head_size = tail_ref.shape[2] // 2
    spread_rows(q_rows, 0, q_ref, heads, head_size, rows)
    spread_rows(f_rows, 0, fresh_ref, 2, head_size, rows)
    queries = q_rows[...]
    contract = (((1,), (1,)), ((), ()))
    logits = lax.dot_general(
        queries, tail_ref[:, :, :head_size].reshape(reqs * tail, head_size),
        contract, preferred_element_type=jnp.float32,
    )
    total = heads * rows
    row = iota((total, tail), 0) % rows
    lane = iota((total, tail), 1)
    parts = []
    for r in range(reqs):
        live = (row // drafts == r) & (lane < len_ref[r])
        parts.append(jnp.where(live, logits[:, r * tail:(r + 1) * tail] * scale, FLOOR))
    fresh = lax.dot_general(
        queries, f_rows[0:rows, :], contract, preferred_element_type=jnp.float32
    )
    row = iota((total, rows), 0) % rows
    key = iota((total, rows), 1)
    live = (row // drafts == key // drafts) & (key % drafts <= row % drafts)
    fresh = jnp.where(live, fresh * scale, FLOOR)
    logits = jnp.concatenate(parts, axis=1)
    peak = jnp.maximum(
        jnp.max(logits, axis=1, keepdims=True), jnp.max(fresh, axis=1, keepdims=True)
    )
    peak = rounded_peak(peak)
    weights = jnp.exp2(logits - peak)
    fresh = jnp.exp2(fresh - peak)
    den = jnp.sum(weights, axis=1, keepdims=True) + jnp.sum(fresh, axis=1, keepdims=True)
    num = jnp.dot(
        weights.astype(jnp.bfloat16), tail_ref[:, :, head_size:].reshape(reqs * tail, head_size),
        preferred_element_type=jnp.float32,
    )
    num = num + jnp.dot(
        fresh.astype(jnp.bfloat16), f_rows[rows:2 * rows, :], preferred_element_type=jnp.float32
    )
    out_ref[:, :head_size] = num
    out_ref[:, head_size:] = pack_stats(peak, den)


def summed_parts(blocks, head_size):
    nums = [b[:, :head_size].astype(jnp.float32) for b in blocks]
    stats = [unpack_stats(b[:, head_size:]) for b in blocks]
    peak = functools.reduce(jnp.maximum, [s[0] for s in stats])
    factors = [jnp.exp2(s[0] - peak) for s in stats]
    num = sum(n * f for n, f in zip(nums, factors))
    den = sum(s[1] * f for s, f in zip(stats, factors))
    return num, peak, den


def merge_kernel(head_size, a_ref, b_ref, *out_refs):
    for j, out_ref in enumerate(out_refs):
        num, peak, den = summed_parts([a_ref[j], b_ref[j]], head_size)
        out_ref[:, :head_size] = num.astype(out_ref.dtype)
        out_ref[:, head_size:] = pack_stats(peak, den).astype(out_ref.dtype)


def project(num, den, weight_ref, out_ref, heads, rows):
    reqs, drafts, _ = out_ref.shape
    attention = (num / den).astype(jnp.bfloat16)
    head_size = attention.shape[1]
    value = sum(
        jnp.dot(
            attention[c * rows:(c + 1) * rows, :], weight_ref[c * head_size:(c + 1) * head_size, :],
            preferred_element_type=jnp.float32,
        )
        for c in range(heads)
    ).astype(out_ref.dtype)
    for r in range(reqs):
        out_ref[r] = value[r * drafts:(r + 1) * drafts, :]


def combine_kernel(heads, rows, head_size, *refs):
    *block_refs, weight_ref, out_ref = refs
    num, _, den = summed_parts([b[...] for b in block_refs], head_size)
    project(num, den, weight_ref, out_ref, heads, rows)


def combine_many_kernel(heads, rows, head_size, own_ref, many_ref, weight_ref, out_ref):
    def one(j, carry):
        num, peak, den = carry
        block = many_ref[j]
        next_peak, next_den = unpack_stats(block[:, head_size:])
        top = jnp.maximum(peak, next_peak)
        old, new = jnp.exp2(peak - top), jnp.exp2(next_peak - top)
        return num * old + block[:, :head_size].astype(jnp.float32) * new, top, den * old + next_den * new

    own = own_ref[...]
    carry = (own[:, :head_size], *unpack_stats(own[:, head_size:]))
    num, _, den = lax.fori_loop(0, many_ref.shape[0], one, carry)
    project(num, den, weight_ref, out_ref, heads, rows)


def final_kernel(*refs):
    *part_refs, hidden_ref, gain_ref, score_ref, out_ref, scores_ref = refs
    reqs, drafts, width = hidden_ref.shape
    mix = gain_ref[...] * score_ref[...]
    lane = iota((1, LANES), 1)
    scores = jnp.zeros((1, LANES), jnp.float32)
    for r in range(reqs):
        total = sum(p[r].astype(jnp.float32) for p in part_refs)
        value = (hidden_ref[r].astype(jnp.float32) + total).astype(out_ref.dtype)
        out_ref[r] = value
        last = value.astype(jnp.float32)[drafts - 1:drafts, :]
        square = jnp.sum(last * last, axis=1, keepdims=True) / width
        score = jnp.sum(last * mix, axis=1, keepdims=True) * lax.rsqrt(square + 1e-06)
        scores = jnp.where(lane == r, score, scores)
    scores_ref[...] = scores[0, :reqs]


def body(sizes, prefix_pool, slot_page, prompt_len, request_ids, tail_len, tail_cache, queries, new_kv, hidden,
         out_weight, norm_gain, score_weight):
    blk, kv = sizes
    pool = prefix_pool[0]
    page_count, page_tokens, head_pair = pool.shape
    head_size = head_pair // 2
    local, drafts, head_width = queries.shape
    heads = head_width // head_size
    rows = round_up(local * drafts, 16)
    per = heads * rows
    keys = page_count * page_tokens
    width = hidden.shape[2]
    scale = head_size ** (-0.5) * LOG2E
    paired = blk in (2, 4, 8)
    half = blk // 2

    def swap(x, axis, size, mask):
        return lax.ppermute(x, axis, [(i, i ^ mask) for i in range(size)])

    def device_of(j, me):
        if not paired:
            return j
        return me ^ (j * 2) if isinstance(j, int) and j < half else me ^ (j % half * 2 + j // half)

    low, high, key = pl.pallas_call(
        functools.partial(layout_kernel, device_of, blk, local, rows, heads, drafts, page_tokens),
        out_shape=(
            jax.ShapeDtypeStruct((blk * per, LANES), jnp.int32),
            jax.ShapeDtypeStruct((blk * per, LANES), jnp.int32),
            jax.ShapeDtypeStruct((8, keys), jnp.int32),
        ),
        in_specs=[SMEM] * 3,
        out_specs=(VMEM,) * 3,
        scratch_shapes=[pltpu.SMEM(prompt_len.shape, jnp.int32)],
        compiler_params=vmem(8),
        cost_estimate=cost(1, 2 * blk * per * LANES * 4),
        name="key_ranges",
    )(request_ids, prompt_len, slot_page)

    own = pl.pallas_call(
        functools.partial(own_kernel, heads, rows, scale),
        out_shape=jax.ShapeDtypeStruct((per, head_size + LANES), jnp.float32),
        in_specs=[SMEM] + [VMEM] * 3,
        out_specs=VMEM,
        scratch_shapes=[
            pltpu.VMEM((per, head_size), jnp.bfloat16),
            pltpu.VMEM((2 * rows, head_size), jnp.bfloat16),
        ],
        compiler_params=vmem(8),
        cost_estimate=cost(4 * per * local * tail_cache.shape[2] * head_size, 2 * tail_cache.size),
        name="own_keys",
    )(tail_len, queries, tail_cache[0], new_kv[0])

    def prefix(block, first):
        slots = block.shape[0]
        step = min(slots, 4)
        grid = slots // step
        offset = first // step
        return pl.pallas_call(
            functools.partial(prefix_kernel, heads, rows, scale),
            out_shape=jax.ShapeDtypeStruct((slots, per, head_size + LANES), jnp.bfloat16),
            grid=(grid,),
            in_specs=[
                pl.BlockSpec((step, local, drafts, head_width), lambda i: (i, 0, 0, 0)),
                pl.BlockSpec((step * per, LANES), lambda i: (i + offset, 0)),
                pl.BlockSpec((step * per, LANES), lambda i: (i + offset, 0)),
                pl.BlockSpec((8, keys), lambda i: (0, 0)),
                pl.BlockSpec((page_count, page_tokens, head_pair), lambda i: (0, 0, 0)),
            ],
            out_specs=pl.BlockSpec((step, per, head_size + LANES), lambda i: (i, 0, 0)),
            scratch_shapes=[pltpu.VMEM((step * per, head_size), jnp.bfloat16)],
            compiler_params=vmem(16),
            cost_estimate=cost(4 * slots * per * keys * head_size, 2 * pool.size),
            name="prefix_keys",
        )(block, low, high, key, pool)

    partial_shape = jax.ShapeDtypeStruct((local, drafts, width), jnp.bfloat16)
    if paired:
        column = [queries] + [swap(queries, "blk", blk, 2 * j) for j in range(1, half)]
        mine = jnp.stack(column)
        theirs = swap(mine, "blk", blk, 1)
        sums_mine = prefix(mine, 0)
        sums_theirs = prefix(theirs, half)
        back = swap(sums_theirs, "blk", blk, 1)
        block_shape = jax.ShapeDtypeStruct((per, head_size + LANES), jnp.bfloat16)
        merged = pl.pallas_call(
            functools.partial(merge_kernel, head_size),
            out_shape=(block_shape,) * half,
            in_specs=[VMEM] * 2,
            out_specs=(VMEM,) * half,
            compiler_params=vmem(8),
            cost_estimate=cost(1, 6 * half * per * head_size),
            name="merge_cores",
        )(sums_mine, back)
        blocks = [merged[0]] + [swap(merged[j], "blk", blk, 2 * j) for j in range(1, half)]
        share = pl.pallas_call(
            functools.partial(combine_kernel, heads, rows, head_size),
            out_shape=partial_shape,
            in_specs=[VMEM] * (half + 2),
            out_specs=VMEM,
            compiler_params=vmem(12),
            cost_estimate=cost(2 * per * head_size * width, 2 * out_weight.size),
            name="combine_project",
        )(own, *blocks, out_weight)
    else:
        gathered = lax.all_gather(queries, "blk", axis=0)
        blocks = lax.all_to_all(prefix(gathered, 0), "blk", 0, 0)
        share = pl.pallas_call(
            functools.partial(combine_many_kernel, heads, rows, head_size),
            out_shape=partial_shape,
            in_specs=[VMEM] * 3,
            out_specs=VMEM,
            compiler_params=vmem(12),
            cost_estimate=cost(2 * per * head_size * width, 2 * out_weight.size),
            name="combine_project",
        )(own, blocks, out_weight)
    if kv in (2, 4):
        shares = [share] + [swap(share, "kv", kv, j) for j in range(1, kv)]
    else:
        shares = [lax.psum(share, "kv")]
    hidden_out, scores = pl.pallas_call(
        final_kernel,
        out_shape=(
            jax.ShapeDtypeStruct(hidden.shape, hidden.dtype),
            jax.ShapeDtypeStruct((local,), jnp.float32),
        ),
        in_specs=[VMEM] * (len(shares) + 3),
        out_specs=(VMEM, VMEM),
        compiler_params=vmem(8),
        cost_estimate=cost(1, 2 * hidden.size * 6),
        name="residual_scores",
    )(*shares, hidden, norm_gain.reshape(1, width), score_weight.reshape(1, width))
    return hidden_out, scores


def solution(mesh):
    in_specs = (
        P("kv", "blk", None, None),
        P("blk"),
        P(),
        P(),
        P("blk"),
        P("kv", "blk", None, None),
        P("blk", None, "kv"),
        P("kv", "blk", None, None),
        P("blk", None, None),
        P("kv", None),
        P(),
        P(),
    )
    out_specs = (P("blk", None, None), P("blk"))
    sizes = (mesh.shape["blk"], mesh.shape["kv"])
    return jax.shard_map(
        functools.partial(body, sizes), mesh=mesh, in_specs=in_specs, out_specs=out_specs, check_vma=False
    )
```

```python
import functools

import jax
import jax.numpy as jnp
from jax import lax
from jax.experimental import pallas as pl
from jax.experimental.pallas import tpu as pltpu
from jax.sharding import PartitionSpec as P

SAMPLES = 16
LANES = 128
FLOOR = -(2.0**100)
LOG2E = 1.4426950408889634
ANY = pl.BlockSpec(memory_space=pl.ANY)
VMEM = pl.BlockSpec(memory_space=pltpu.VMEM)
SMEM = pl.BlockSpec(memory_space=pltpu.SMEM)


def round_up(value, unit):
    return (value + unit - 1) // unit * unit


def cost(flops, size):
    return pl.CostEstimate(flops=flops, bytes_accessed=size, transcendentals=0)


def vmem(mebibytes):
    return pltpu.CompilerParams(vmem_limit_bytes=mebibytes * 1024 * 1024)


def iota(shape, dim):
    return lax.broadcasted_iota(jnp.int32, shape, dim)


def rounded_peak(peak):
    return peak.astype(jnp.bfloat16).astype(jnp.float32)


def softmax_parts(logits):
    peak = rounded_peak(jnp.max(logits, axis=1, keepdims=True))
    weights = jnp.exp2(logits - peak)
    return peak, weights, jnp.sum(weights, axis=1, keepdims=True)


def pack_stats(peak, den):
    high = den.astype(jnp.bfloat16).astype(jnp.float32)
    lane = iota((peak.shape[0], LANES), 1)
    stats = jnp.where(lane == 0, peak, jnp.where(lane == 1, high, den - high))
    return jnp.where(lane < 3, stats, 0.0)


def unpack_stats(stats):
    stats = stats.astype(jnp.float32)
    return stats[:, 0:1], stats[:, 1:2] + stats[:, 2:3]


def spread_rows(dest, base, block, heads, head_size, rows):
    reqs, drafts, _ = block.shape
    pad = rows - reqs * drafts
    for c in range(heads):
        cols = pl.ds(c * head_size, head_size)
        for r in range(reqs):
            dest[pl.ds(base + c * rows + r * drafts, drafts), :] = block[r, :, cols]
        if pad:
            dest[pl.ds(base + c * rows + reqs * drafts, pad), :] = jnp.zeros((pad, head_size), dest.dtype)


def layout_kernel(device_of, slots, local, rows, heads, drafts, page_tokens,
                  ids_ref, len_ref, page_ref, q_ref, pool_ref,
                  low_ref, high_ref, key_ref, q_out_ref, pool_out_ref, start_ref, sems):
    copies = [
        pltpu.make_async_copy(q_ref, q_out_ref, sems.at[0]),
        pltpu.make_async_copy(pool_ref, pool_out_ref, sems.at[1]),
    ]
    for copy in copies:
        copy.start()
    me = lax.axis_index("blk")
    prompts = len_ref.shape[0]

    def place(p, start):
        start_ref[p] = start
        return start + (len_ref[p] + page_tokens - 1) // page_tokens * page_tokens

    lax.fori_loop(0, prompts, place, jnp.int32(0))
    request = iota((rows, LANES), 0) // drafts

    def one(j, _):
        device = device_of(j, me)
        low = jnp.zeros((rows, LANES), jnp.int32)
        high = low
        for r in range(local):
            prompt = ids_ref[device * local + r] // SAMPLES
            start = start_ref[prompt]
            low = jnp.where(request == r, start, low)
            high = jnp.where(request == r, start + len_ref[prompt], high)
        for c in range(heads):
            place_at = pl.ds(pl.multiple_of((j * heads + c) * rows, rows), rows)
            low_ref[place_at, :] = low
            high_ref[place_at, :] = high
        return 0

    lax.fori_loop(0, slots, one, 0, unroll=slots <= 8)
    lane = iota((8, page_tokens), 1)
    for s in range(page_ref.shape[0]):
        key_ref[:, pl.ds(s * page_tokens, page_tokens)] = lane + page_ref[s] * page_tokens
    for copy in copies:
        copy.wait()


def prefix_kernel(heads, rows, scale, q_ref, low_ref, high_ref, key_ref, pool_ref, *rest):
    out_ref, q_rows = rest
    slots = q_ref.shape[0]
    head_size = pool_ref.shape[2] // 2
    keys = pool_ref.shape[0] * pool_ref.shape[1]
    for j in range(slots):
        spread_rows(q_rows, j * heads * rows, q_ref.at[j], heads, head_size, rows)
    logits = lax.dot_general(
        q_rows[...], pool_ref[:, :, :head_size].reshape(keys, head_size),
        (((1,), (1,)), ((), ())), preferred_element_type=jnp.float32,
    )
    low, high = low_ref[...], high_ref[...]
    parts = []
    for k in range(0, keys, LANES):
        key = key_ref[0:1, k:k + LANES]
        live = (key >= low) & (key < high)
        parts.append(jnp.where(live, logits[:, k:k + LANES] * scale, FLOOR))
    peak, weights, den = softmax_parts(jnp.concatenate(parts, axis=1))
    num = jnp.dot(
        weights.astype(jnp.bfloat16), pool_ref[:, :, head_size:].reshape(keys, head_size),
        preferred_element_type=jnp.float32,
    )
    per = heads * rows
    out_ref[:, :, :head_size] = num.reshape(slots, per, head_size).astype(out_ref.dtype)
    out_ref[:, :, head_size:] = pack_stats(peak, den).reshape(slots, per, LANES).astype(out_ref.dtype)


def own_kernel(heads, rows, scale, len_ref, q_ref, tail_ref, fresh_ref, out_ref, q_rows, f_rows):
    reqs, drafts, _ = q_ref.shape
    tail = tail_ref.shape[1]
    head_size = tail_ref.shape[2] // 2
    spread_rows(q_rows, 0, q_ref, heads, head_size, rows)
    spread_rows(f_rows, 0, fresh_ref, 2, head_size, rows)
    queries = q_rows[...]
    contract = (((1,), (1,)), ((), ()))
    logits = lax.dot_general(
        queries, tail_ref[:, :, :head_size].reshape(reqs * tail, head_size),
        contract, preferred_element_type=jnp.float32,
    )
    total = heads * rows
    row = iota((total, tail), 0) % rows
    lane = iota((total, tail), 1)
    parts = []
    for r in range(reqs):
        live = (row // drafts == r) & (lane < len_ref[r])
        parts.append(jnp.where(live, logits[:, r * tail:(r + 1) * tail] * scale, FLOOR))
    fresh = lax.dot_general(
        queries, f_rows[0:rows, :], contract, preferred_element_type=jnp.float32
    )
    row = iota((total, rows), 0) % rows
    key = iota((total, rows), 1)
    live = (row // drafts == key // drafts) & (key % drafts <= row % drafts)
    fresh = jnp.where(live, fresh * scale, FLOOR)
    logits = jnp.concatenate(parts, axis=1)
    peak = jnp.maximum(
        jnp.max(logits, axis=1, keepdims=True), jnp.max(fresh, axis=1, keepdims=True)
    )
    peak = rounded_peak(peak)
    weights = jnp.exp2(logits - peak)
    fresh = jnp.exp2(fresh - peak)
    den = jnp.sum(weights, axis=1, keepdims=True) + jnp.sum(fresh, axis=1, keepdims=True)
    num = jnp.dot(
        weights.astype(jnp.bfloat16), tail_ref[:, :, head_size:].reshape(reqs * tail, head_size),
        preferred_element_type=jnp.float32,
    )
    num = num + jnp.dot(
        fresh.astype(jnp.bfloat16), f_rows[rows:2 * rows, :], preferred_element_type=jnp.float32
    )
    out_ref[:, :head_size] = num
    out_ref[:, head_size:] = pack_stats(peak, den)


def summed_parts(blocks, head_size):
    nums = [b[:, :head_size].astype(jnp.float32) for b in blocks]
    stats = [unpack_stats(b[:, head_size:]) for b in blocks]
    peak = functools.reduce(jnp.maximum, [s[0] for s in stats])
    factors = [jnp.exp2(s[0] - peak) for s in stats]
    num = sum(n * f for n, f in zip(nums, factors))
    den = sum(s[1] * f for s, f in zip(stats, factors))
    return num, peak, den


def merge_kernel(head_size, a_ref, b_ref, *out_refs):
    for j, out_ref in enumerate(out_refs):
        num, peak, den = summed_parts([a_ref[j], b_ref[j]], head_size)
        out_ref[:, :head_size] = num.astype(out_ref.dtype)
        out_ref[:, head_size:] = pack_stats(peak, den).astype(out_ref.dtype)


def project(num, den, weight_ref, out_ref, heads, rows):
    reqs, drafts, _ = out_ref.shape
    attention = (num / den).astype(jnp.bfloat16)
    head_size = attention.shape[1]
    value = sum(
        jnp.dot(
            attention[c * rows:(c + 1) * rows, :], weight_ref[c * head_size:(c + 1) * head_size, :],
            preferred_element_type=jnp.float32,
        )
        for c in range(heads)
    ).astype(out_ref.dtype)
    for r in range(reqs):
        out_ref[r] = value[r * drafts:(r + 1) * drafts, :]


def combine_kernel(heads, rows, head_size, *refs):
    *block_refs, weight_ref, out_ref = refs
    num, _, den = summed_parts([b[...] for b in block_refs], head_size)
    project(num, den, weight_ref, out_ref, heads, rows)


def combine_many_kernel(heads, rows, head_size, own_ref, many_ref, weight_ref, out_ref):
    def one(j, carry):
        num, peak, den = carry
        block = many_ref[j]
        next_peak, next_den = unpack_stats(block[:, head_size:])
        top = jnp.maximum(peak, next_peak)
        old, new = jnp.exp2(peak - top), jnp.exp2(next_peak - top)
        return num * old + block[:, :head_size].astype(jnp.float32) * new, top, den * old + next_den * new

    own = own_ref[...]
    carry = (own[:, :head_size], *unpack_stats(own[:, head_size:]))
    num, _, den = lax.fori_loop(0, many_ref.shape[0], one, carry)
    project(num, den, weight_ref, out_ref, heads, rows)


def final_kernel(*refs):
    *part_refs, hidden_ref, gain_ref, score_ref, out_ref, scores_ref = refs
    reqs, drafts, width = hidden_ref.shape
    mix = gain_ref[...] * score_ref[...]
    lane = iota((1, LANES), 1)
    scores = jnp.zeros((1, LANES), jnp.float32)
    for r in range(reqs):
        total = sum(p[r].astype(jnp.float32) for p in part_refs)
        value = (hidden_ref[r].astype(jnp.float32) + total).astype(out_ref.dtype)
        out_ref[r] = value
        last = value.astype(jnp.float32)[drafts - 1:drafts, :]
        square = jnp.sum(last * last, axis=1, keepdims=True) / width
        score = jnp.sum(last * mix, axis=1, keepdims=True) * lax.rsqrt(square + 1e-06)
        scores = jnp.where(lane == r, score, scores)
    scores_ref[...] = scores[0, :reqs]


def body(sizes, prefix_pool, slot_page, prompt_len, request_ids, tail_len, tail_cache, queries, new_kv, hidden,
         out_weight, norm_gain, score_weight):
    blk, kv = sizes
    pool = prefix_pool[0]
    page_count, page_tokens, head_pair = pool.shape
    head_size = head_pair // 2
    local, drafts, head_width = queries.shape
    heads = head_width // head_size
    rows = round_up(local * drafts, 16)
    per = heads * rows
    keys = page_count * page_tokens
    width = hidden.shape[2]
    scale = head_size ** (-0.5) * LOG2E
    paired = blk in (2, 4, 8)
    half = blk // 2

    def swap(x, axis, size, mask):
        return lax.ppermute(x, axis, [(i, i ^ mask) for i in range(size)])

    def device_of(j, me):
        if not paired:
            return j
        return me ^ (j * 2) if isinstance(j, int) and j < half else me ^ (j % half * 2 + j // half)

    in_hbm = functools.partial(pltpu.with_memory_space_constraint, memory_space=pltpu.HBM)
    low, high, key, near_queries, pool = pl.pallas_call(
        functools.partial(layout_kernel, device_of, blk, local, rows, heads, drafts, page_tokens),
        out_shape=(
            jax.ShapeDtypeStruct((blk * per, LANES), jnp.int32),
            jax.ShapeDtypeStruct((blk * per, LANES), jnp.int32),
            jax.ShapeDtypeStruct((8, keys), jnp.int32),
            jax.ShapeDtypeStruct(queries.shape, queries.dtype),
            jax.ShapeDtypeStruct(pool.shape, pool.dtype),
        ),
        in_specs=[SMEM] * 3 + [ANY] * 2,
        out_specs=(VMEM,) * 3 + (ANY,) * 2,
        scratch_shapes=[pltpu.SMEM(prompt_len.shape, jnp.int32), pltpu.SemaphoreType.DMA((2,))],
        compiler_params=vmem(8),
        cost_estimate=cost(1, 2 * blk * per * LANES * 4),
        name="key_ranges",
    )(*map(in_hbm, (request_ids, prompt_len, slot_page, queries, pool)))

    own = pl.pallas_call(
        functools.partial(own_kernel, heads, rows, scale),
        out_shape=jax.ShapeDtypeStruct((per, head_size + LANES), jnp.float32),
        in_specs=[SMEM] + [VMEM] * 3,
        out_specs=VMEM,
        scratch_shapes=[
            pltpu.VMEM((per, head_size), jnp.bfloat16),
            pltpu.VMEM((2 * rows, head_size), jnp.bfloat16),
        ],
        compiler_params=vmem(8),
        cost_estimate=cost(4 * per * local * tail_cache.shape[2] * head_size, 2 * tail_cache.size),
        name="own_keys",
    )(tail_len, queries, tail_cache[0], new_kv[0])

    def prefix(block, first):
        slots = block.shape[0]
        step = min(slots, 4)
        grid = slots // step
        offset = first // step
        return pl.pallas_call(
            functools.partial(prefix_kernel, heads, rows, scale),
            out_shape=jax.ShapeDtypeStruct((slots, per, head_size + LANES), jnp.bfloat16),
            grid=(grid,),
            in_specs=[
                pl.BlockSpec((step, local, drafts, head_width), lambda i: (i, 0, 0, 0)),
                pl.BlockSpec((step * per, LANES), lambda i: (i + offset, 0)),
                pl.BlockSpec((step * per, LANES), lambda i: (i + offset, 0)),
                pl.BlockSpec((8, keys), lambda i: (0, 0)),
                pl.BlockSpec((page_count, page_tokens, head_pair), lambda i: (0, 0, 0)),
            ],
            out_specs=pl.BlockSpec((step, per, head_size + LANES), lambda i: (i, 0, 0)),
            scratch_shapes=[pltpu.VMEM((step * per, head_size), jnp.bfloat16)],
            compiler_params=vmem(16),
            cost_estimate=cost(4 * slots * per * keys * head_size, 2 * pool.size),
            name="prefix_keys",
        )(block, low, high, key, pool)

    partial_shape = jax.ShapeDtypeStruct((local, drafts, width), jnp.bfloat16)
    if paired:
        column = [near_queries] + [swap(queries, "blk", blk, 2 * j) for j in range(1, half)]
        mine = jnp.stack(column)
        theirs = swap(mine, "blk", blk, 1)
        sums_mine = prefix(mine, 0)
        sums_theirs = prefix(theirs, half)
        back = swap(sums_theirs, "blk", blk, 1)
        block_shape = jax.ShapeDtypeStruct((per, head_size + LANES), jnp.bfloat16)
        merged = pl.pallas_call(
            functools.partial(merge_kernel, head_size),
            out_shape=(block_shape,) * half,
            in_specs=[VMEM] * 2,
            out_specs=(VMEM,) * half,
            compiler_params=vmem(8),
            cost_estimate=cost(1, 6 * half * per * head_size),
            name="merge_cores",
        )(sums_mine, back)
        blocks = [merged[0]] + [swap(merged[j], "blk", blk, 2 * j) for j in range(1, half)]
        share = pl.pallas_call(
            functools.partial(combine_kernel, heads, rows, head_size),
            out_shape=partial_shape,
            in_specs=[VMEM] * (half + 2),
            out_specs=VMEM,
            compiler_params=vmem(12),
            cost_estimate=cost(2 * per * head_size * width, 2 * out_weight.size),
            name="combine_project",
        )(own, *blocks, out_weight)
    else:
        gathered = lax.all_gather(queries, "blk", axis=0)
        blocks = lax.all_to_all(prefix(gathered, 0), "blk", 0, 0)
        share = pl.pallas_call(
            functools.partial(combine_many_kernel, heads, rows, head_size),
            out_shape=partial_shape,
            in_specs=[VMEM] * 3,
            out_specs=VMEM,
            compiler_params=vmem(12),
            cost_estimate=cost(2 * per * head_size * width, 2 * out_weight.size),
            name="combine_project",
        )(own, blocks, out_weight)
    if kv in (2, 4):
        shares = [share] + [swap(share, "kv", kv, j) for j in range(1, kv)]
    else:
        shares = [lax.psum(share, "kv")]
    hidden_out, scores = pl.pallas_call(
        final_kernel,
        out_shape=(
            jax.ShapeDtypeStruct(hidden.shape, hidden.dtype),
            jax.ShapeDtypeStruct((local,), jnp.float32),
        ),
        in_specs=[VMEM] * (len(shares) + 3),
        out_specs=(VMEM, VMEM),
        compiler_params=vmem(8),
        cost_estimate=cost(1, 2 * hidden.size * 6),
        name="residual_scores",
    )(*shares, hidden, norm_gain.reshape(1, width), score_weight.reshape(1, width))
    return hidden_out, scores


def solution(mesh):
    in_specs = (
        P("kv", "blk", None, None),
        P("blk"),
        P(),
        P(),
        P("blk"),
        P("kv", "blk", None, None),
        P("blk", None, "kv"),
        P("kv", "blk", None, None),
        P("blk", None, None),
        P("kv", None),
        P(),
        P(),
    )
    out_specs = (P("blk", None, None), P("blk"))
    sizes = (mesh.shape["blk"], mesh.shape["kv"])
    return jax.shard_map(
        functools.partial(body, sizes), mesh=mesh, in_specs=in_specs, out_specs=out_specs, check_vma=False
    )
```

```python
import functools

import jax
import jax.numpy as jnp
from jax import lax
from jax.experimental import pallas as pl
from jax.experimental.pallas import tpu as pltpu
from jax.sharding import PartitionSpec as P

SAMPLES = 16
ORDER_A = (2, 3, 1)
ORDER_B = (3, 2, 1)
ORDER_C = (1, 2, 3)
LANES = 128
FLOOR = -(2.0**100)
LOG2E = 1.4426950408889634
ANY = pl.BlockSpec(memory_space=pl.ANY)
VMEM = pl.BlockSpec(memory_space=pltpu.VMEM)
SMEM = pl.BlockSpec(memory_space=pltpu.SMEM)


def round_up(value, unit):
    return (value + unit - 1) // unit * unit


def cost(flops, size):
    return pl.CostEstimate(flops=flops, bytes_accessed=size, transcendentals=0)


def vmem(mebibytes):
    return pltpu.CompilerParams(vmem_limit_bytes=mebibytes * 1024 * 1024)


def iota(shape, dim):
    return lax.broadcasted_iota(jnp.int32, shape, dim)


def rounded_peak(peak):
    return peak.astype(jnp.bfloat16).astype(jnp.float32)


def softmax_parts(logits):
    peak = rounded_peak(jnp.max(logits, axis=1, keepdims=True))
    weights = jnp.exp2(logits - peak)
    return peak, weights, jnp.sum(weights, axis=1, keepdims=True)


def pack_stats(peak, den):
    high = den.astype(jnp.bfloat16).astype(jnp.float32)
    lane = iota((peak.shape[0], LANES), 1)
    stats = jnp.where(lane == 0, peak, jnp.where(lane == 1, high, den - high))
    return jnp.where(lane < 3, stats, 0.0)


def unpack_stats(stats):
    stats = stats.astype(jnp.float32)
    return stats[:, 0:1], stats[:, 1:2] + stats[:, 2:3]


def spread_rows(dest, base, block, heads, head_size, rows):
    reqs, drafts, _ = block.shape
    pad = rows - reqs * drafts
    for c in range(heads):
        cols = pl.ds(c * head_size, head_size)
        for r in range(reqs):
            dest[pl.ds(base + c * rows + r * drafts, drafts), :] = block[r, :, cols]
        if pad:
            dest[pl.ds(base + c * rows + reqs * drafts, pad), :] = jnp.zeros((pad, head_size), dest.dtype)


def write_keys(page_ref, key_ref, page_tokens):
    lane = iota((8, page_tokens), 1)
    for s in range(page_ref.shape[0]):
        key_ref[:, pl.ds(s * page_tokens, page_tokens)] = lane + page_ref[s] * page_tokens


def layout_kernel(device_of, slots, local, rows, heads, drafts, page_tokens,
                  ids_hbm, len_hbm, page_hbm, q_ref, pool_ref,
                  low_ref, high_ref, key_ref, q_out_ref, pool_out_ref,
                  ids_ref, len_ref, page_ref, start_ref, sems):
    pairs = [(ids_hbm, ids_ref), (len_hbm, len_ref), (page_hbm, page_ref), (pool_ref, pool_out_ref), (q_ref, q_out_ref)]
    copies = [pltpu.make_async_copy(a, b, sems.at[i]) for i, (a, b) in enumerate(pairs)]
    for copy in copies:
        copy.start()
    me = lax.axis_index("blk")
    prompts = len_ref.shape[0]
    shift = SAMPLES.bit_length() - 1
    for copy in copies[:3]:
        copy.wait()

    def place(p, start):
        start_ref[p] = start
        return start + lax.div(len_ref[p] + page_tokens - 1, page_tokens) * page_tokens

    lax.fori_loop(0, prompts, place, jnp.int32(0), unroll=prompts <= 4)
    request = iota((rows, LANES), 0) // drafts

    def one(j, _):
        device = device_of(j, me)
        low = jnp.zeros((rows, LANES), jnp.int32)
        high = low
        for r in range(local):
            prompt = lax.shift_right_logical(ids_ref[device * local + r], shift)
            start = start_ref[prompt]
            low = jnp.where(request == r, start, low)
            high = jnp.where(request == r, start + len_ref[prompt], high)
        for c in range(heads):
            place_at = pl.ds((j * heads + c) * rows, rows)
            low_ref[place_at, :] = low
            high_ref[place_at, :] = high
        return 0

    if slots <= 8:
        for j in range(slots):
            one(j, 0)
    else:
        lax.fori_loop(0, slots, one, 0)
    write_keys(page_ref, key_ref, page_tokens)
    for copy in copies[3:]:
        copy.wait()


def key_row(ref, at, page_tokens):
    if ref.shape[0] > 1:
        return ref[0:1, at:at + LANES]
    lane = iota((1, LANES), 1)
    first = at // page_tokens
    page = ref[:, first:first + 1]
    for n in range(1, LANES // page_tokens):
        page = jnp.where(lane >= n * page_tokens, ref[:, first + n:first + n + 1], page)
    return page * page_tokens + lane % page_tokens


def prefix_kernel(heads, rows, scale, q_ref, low_ref, high_ref, *rest):
    *both_refs, out_ref, q_rows = rest
    key_refs, pool_refs = both_refs[:len(both_refs) // 2], both_refs[len(both_refs) // 2:]
    slots = q_ref.shape[0]
    pages, page_tokens, head_pair = pool_refs[0].shape
    head_size = head_pair // 2
    keys = pages * page_tokens
    for j in range(slots):
        spread_rows(q_rows, j * heads * rows, q_ref.at[j], heads, head_size, rows)
    low, high = low_ref[...], high_ref[...]
    parts = []
    for key_ref, pool_ref in zip(key_refs, pool_refs):
        logits = lax.dot_general(
            q_rows[...], pool_ref[:, :, :head_size].reshape(keys, head_size),
            (((1,), (1,)), ((), ())), preferred_element_type=jnp.float32,
        )
        for k in range(0, keys, LANES):
            key = key_row(key_ref, k, page_tokens)
            live = (key >= low) & (key < high)
            parts.append(jnp.where(live, logits[:, k:k + LANES] * scale, FLOOR))
    peak, weights, den = softmax_parts(jnp.concatenate(parts, axis=1))
    weights = weights.astype(jnp.bfloat16)
    num = sum(
        jnp.dot(
            weights[:, n * keys:(n + 1) * keys], pool_ref[:, :, head_size:].reshape(keys, head_size),
            preferred_element_type=jnp.float32,
        )
        for n, pool_ref in enumerate(pool_refs)
    )
    per = heads * rows
    out_ref[:, :, :head_size] = num.reshape(slots, per, head_size).astype(out_ref.dtype)
    out_ref[:, :, head_size:] = pack_stats(peak, den).reshape(slots, per, LANES).astype(out_ref.dtype)


def own_kernel(heads, rows, scale, len_ref, q_ref, tail_ref, fresh_ref, out_ref, q_rows, f_rows):
    reqs, drafts, _ = q_ref.shape
    tail = tail_ref.shape[1]
    head_size = tail_ref.shape[2] // 2
    spread_rows(q_rows, 0, q_ref, heads, head_size, rows)
    spread_rows(f_rows, 0, fresh_ref, 2, head_size, rows)
    queries = q_rows[...]
    contract = (((1,), (1,)), ((), ()))
    logits = lax.dot_general(
        queries, tail_ref[:, :, :head_size].reshape(reqs * tail, head_size),
        contract, preferred_element_type=jnp.float32,
    )
    total = heads * rows
    row = iota((total, tail), 0) % rows
    lane = iota((total, tail), 1)
    parts = []
    for r in range(reqs):
        live = (row // drafts == r) & (lane < len_ref[r])
        parts.append(jnp.where(live, logits[:, r * tail:(r + 1) * tail] * scale, FLOOR))
    fresh = lax.dot_general(
        queries, f_rows[0:rows, :], contract, preferred_element_type=jnp.float32
    )
    row = iota((total, rows), 0) % rows
    key = iota((total, rows), 1)
    live = (row // drafts == key // drafts) & (key % drafts <= row % drafts)
    fresh = jnp.where(live, fresh * scale, FLOOR)
    logits = jnp.concatenate(parts, axis=1)
    peak = jnp.maximum(
        jnp.max(logits, axis=1, keepdims=True), jnp.max(fresh, axis=1, keepdims=True)
    )
    peak = rounded_peak(peak)
    weights = jnp.exp2(logits - peak)
    fresh = jnp.exp2(fresh - peak)
    den = jnp.sum(weights, axis=1, keepdims=True) + jnp.sum(fresh, axis=1, keepdims=True)
    num = jnp.dot(
        weights.astype(jnp.bfloat16), tail_ref[:, :, head_size:].reshape(reqs * tail, head_size),
        preferred_element_type=jnp.float32,
    )
    num = num + jnp.dot(
        fresh.astype(jnp.bfloat16), f_rows[rows:2 * rows, :], preferred_element_type=jnp.float32
    )
    out_ref[:, :head_size] = num
    out_ref[:, head_size:] = pack_stats(peak, den)


def summed_parts(blocks, head_size):
    nums = [b[:, :head_size].astype(jnp.float32) for b in blocks]
    stats = [unpack_stats(b[:, head_size:]) for b in blocks]
    peak = functools.reduce(jnp.maximum, [s[0] for s in stats])
    factors = [jnp.exp2(s[0] - peak) for s in stats]
    num = sum(n * f for n, f in zip(nums, factors))
    den = sum(s[1] * f for s, f in zip(stats, factors))
    return num, peak, den


def project(num, den, weight_ref, out_ref, heads, rows):
    reqs, drafts, _ = out_ref.shape
    attention = (num / den).astype(jnp.bfloat16)
    head_size = attention.shape[1]
    value = sum(
        jnp.dot(
            attention[c * rows:(c + 1) * rows, :], weight_ref[c * head_size:(c + 1) * head_size, :],
            preferred_element_type=jnp.float32,
        )
        for c in range(heads)
    ).astype(out_ref.dtype)
    for r in range(reqs):
        out_ref[r] = value[r * drafts:(r + 1) * drafts, :]


def combine_kernel(heads, rows, head_size, *refs):
    *block_refs, weight_ref, out_ref = refs
    num, _, den = summed_parts([b[...] for b in block_refs], head_size)
    project(num, den, weight_ref, out_ref, heads, rows)


def combine_many_kernel(heads, rows, head_size, own_ref, many_ref, weight_ref, out_ref):
    def one(j, carry):
        num, peak, den = carry
        block = many_ref[j]
        next_peak, next_den = unpack_stats(block[:, head_size:])
        top = jnp.maximum(peak, next_peak)
        old, new = jnp.exp2(peak - top), jnp.exp2(next_peak - top)
        return num * old + block[:, :head_size].astype(jnp.float32) * new, top, den * old + next_den * new

    own = own_ref[...]
    carry = (own[:, :head_size], *unpack_stats(own[:, head_size:]))
    num, _, den = lax.fori_loop(0, many_ref.shape[0], one, carry)
    project(num, den, weight_ref, out_ref, heads, rows)


def final_kernel(*refs):
    *part_refs, hidden_ref, gain_ref, score_ref, out_ref, scores_ref = refs
    reqs, drafts, width = hidden_ref.shape
    mix = gain_ref[...] * score_ref[...]
    lane = iota((1, LANES), 1)
    scores = jnp.zeros((1, LANES), jnp.float32)
    for r in range(reqs):
        total = sum(p[r].astype(jnp.float32) for p in part_refs)
        value = (hidden_ref[r].astype(jnp.float32) + total).astype(out_ref.dtype)
        out_ref[r] = value
        last = value.astype(jnp.float32)[drafts - 1:drafts, :]
        square = jnp.sum(last * last, axis=1, keepdims=True) / width
        score = jnp.sum(last * mix, axis=1, keepdims=True) * lax.rsqrt(square + 1e-06)
        scores = jnp.where(lane == r, score, scores)
    scores_ref[...] = scores[0, :reqs]


def body(sizes, prefix_pool, slot_page, prompt_len, request_ids, tail_len, tail_cache, queries, new_kv, hidden,
         out_weight, norm_gain, score_weight):
    blk, kv = sizes
    pool = prefix_pool[0]
    page_count, page_tokens, head_pair = pool.shape
    head_size = head_pair // 2
    local, drafts, head_width = queries.shape
    heads = head_width // head_size
    rows = round_up(local * drafts, 16)
    per = heads * rows
    keys = page_count * page_tokens
    width = hidden.shape[2]
    scale = head_size ** (-0.5) * LOG2E
    paired = blk in (2, 4, 8)
    half = blk // 2
    partners = [0] + [j for j in ORDER_A if j < half]

    def swap(x, axis, size, mask):
        return lax.ppermute(x, axis, [(i, i ^ mask) for i in range(size)])

    def device_of(j, me):
        return me ^ (partners[j] * 2) if paired else j

    slots = half if paired else blk
    pools = [pool]
    if paired:
        pools.append(swap(pool, "blk", blk, 1))
        far_pages = swap(slot_page, "blk", blk, 1)

    in_hbm = functools.partial(pltpu.with_memory_space_constraint, memory_space=pltpu.HBM)
    low, high, near_keys, near_queries, pools[0] = pl.pallas_call(
        functools.partial(layout_kernel, device_of, slots, local, rows, heads, drafts, page_tokens),
        out_shape=(
            jax.ShapeDtypeStruct((slots * per, LANES), jnp.int32),
            jax.ShapeDtypeStruct((slots * per, LANES), jnp.int32),
            jax.ShapeDtypeStruct((8, keys), jnp.int32),
            jax.ShapeDtypeStruct(queries.shape, queries.dtype),
            jax.ShapeDtypeStruct(pool.shape, pool.dtype),
        ),
        in_specs=[ANY] * 5,
        out_specs=(VMEM,) * 3 + (ANY,) * 2,
        scratch_shapes=[
            pltpu.SMEM(request_ids.shape, jnp.int32),
            pltpu.SMEM(prompt_len.shape, jnp.int32),
            pltpu.SMEM(slot_page.shape, jnp.int32),
            pltpu.SMEM(prompt_len.shape, jnp.int32),
            pltpu.SemaphoreType.DMA((5,)),
        ],
        compiler_params=vmem(8),
        cost_estimate=cost(1, 2 * slots * per * LANES * 4),
        name="key_ranges",
    )(*map(in_hbm, (request_ids, prompt_len, slot_page, queries, pool)))
    key_lists = [near_keys]
    if paired:
        key_lists.append(far_pages.reshape(1, page_count))

    own = pl.pallas_call(
        functools.partial(own_kernel, heads, rows, scale),
        out_shape=jax.ShapeDtypeStruct((per, head_size + LANES), jnp.float32),
        in_specs=[SMEM] + [VMEM] * 3,
        out_specs=VMEM,
        scratch_shapes=[
            pltpu.VMEM((per, head_size), jnp.bfloat16),
            pltpu.VMEM((2 * rows, head_size), jnp.bfloat16),
        ],
        compiler_params=vmem(8),
        cost_estimate=cost(4 * per * local * tail_cache.shape[2] * head_size, 2 * tail_cache.size),
        name="own_keys",
    )(tail_len, queries, tail_cache[0], new_kv[0])

    def prefix(block):
        slots = block.shape[0]
        step = min(slots, 4)
        return pl.pallas_call(
            functools.partial(prefix_kernel, heads, rows, scale),
            out_shape=jax.ShapeDtypeStruct((slots, per, head_size + LANES), jnp.bfloat16),
            grid=(slots // step,),
            in_specs=[
                pl.BlockSpec((step, local, drafts, head_width), lambda i: (i, 0, 0, 0)),
                pl.BlockSpec((step * per, LANES), lambda i: (i, 0)),
                pl.BlockSpec((step * per, LANES), lambda i: (i, 0)),
            ] + [pl.BlockSpec(k.shape, lambda i: (0, 0)) for k in key_lists] + [pl.BlockSpec((page_count, page_tokens, head_pair), lambda i: (0, 0, 0))] * len(pools),
            out_specs=pl.BlockSpec((step, per, head_size + LANES), lambda i: (i, 0, 0)),
            scratch_shapes=[pltpu.VMEM((step * per, head_size), jnp.bfloat16)],
            compiler_params=vmem(24),
            cost_estimate=cost(4 * slots * per * keys * len(pools) * head_size, 2 * pool.size * len(pools)),
            name="prefix_keys",
        )(block, low, high, *key_lists, *pools)

    partial_shape = jax.ShapeDtypeStruct((local, drafts, width), jnp.bfloat16)
    if paired:
        column = [near_queries] + [swap(queries, "blk", blk, 2 * j) for j in partners[1:]]
        sums = prefix(jnp.stack(column))
        blocks = [sums[0]] + [
            swap(sums[partners.index(j)], "blk", blk, 2 * j) for j in ORDER_B if j < half
        ]
        share = pl.pallas_call(
            functools.partial(combine_kernel, heads, rows, head_size),
            out_shape=partial_shape,
            in_specs=[VMEM] * (half + 2),
            out_specs=VMEM,
            compiler_params=vmem(12),
            cost_estimate=cost(2 * per * head_size * width, 2 * out_weight.size),
            name="combine_project",
        )(own, *blocks, out_weight)
    else:
        gathered = lax.all_gather(queries, "blk", axis=0)
        blocks = lax.all_to_all(prefix(gathered), "blk", 0, 0)
        share = pl.pallas_call(
            functools.partial(combine_many_kernel, heads, rows, head_size),
            out_shape=partial_shape,
            in_specs=[VMEM] * 3,
            out_specs=VMEM,
            compiler_params=vmem(12),
            cost_estimate=cost(2 * per * head_size * width, 2 * out_weight.size),
            name="combine_project",
        )(own, blocks, out_weight)
    if kv in (2, 4):
        shares = [share] + [swap(share, "kv", kv, j) for j in ORDER_C if j < kv]
    else:
        shares = [lax.psum(share, "kv")]
    hidden_out, scores = pl.pallas_call(
        final_kernel,
        out_shape=(
            jax.ShapeDtypeStruct(hidden.shape, hidden.dtype),
            jax.ShapeDtypeStruct((local,), jnp.float32),
        ),
        in_specs=[VMEM] * (len(shares) + 3),
        out_specs=(VMEM, VMEM),
        compiler_params=vmem(8),
        cost_estimate=cost(1, 2 * hidden.size * 6),
        name="residual_scores",
    )(*shares, hidden, norm_gain.reshape(1, width), score_weight.reshape(1, width))
    return hidden_out, scores


def solution(mesh):
    in_specs = (
        P("kv", "blk", None, None),
        P("blk"),
        P(),
        P(),
        P("blk"),
        P("kv", "blk", None, None),
        P("blk", None, "kv"),
        P("kv", "blk", None, None),
        P("blk", None, None),
        P("kv", None),
        P(),
        P(),
    )
    out_specs = (P("blk", None, None), P("blk"))
    sizes = (mesh.shape["blk"], mesh.shape["kv"])
    return jax.shard_map(
        functools.partial(body, sizes), mesh=mesh, in_specs=in_specs, out_specs=out_specs, check_vma=False
    )
```

```python
import functools

import jax
import jax.numpy as jnp
from jax import lax
from jax.experimental import pallas as pl
from jax.experimental.pallas import tpu as pltpu
from jax.sharding import PartitionSpec as P

SAMPLES = 16
CHUNK = 6
ORDER_A = (2, 3, 1)
ORDER_B = (3, 1, 2)
ORDER_C = (1, 2, 3)
LANES = 128
FLOOR = -(2.0**100)
LOG2E = 1.4426950408889634
ANY = pl.BlockSpec(memory_space=pl.ANY)
VMEM = pl.BlockSpec(memory_space=pltpu.VMEM)
SMEM = pl.BlockSpec(memory_space=pltpu.SMEM)


def round_up(value, unit):
    return (value + unit - 1) // unit * unit


def cost(flops, size):
    return pl.CostEstimate(flops=flops, bytes_accessed=size, transcendentals=0)


def vmem(mebibytes):
    return pltpu.CompilerParams(vmem_limit_bytes=mebibytes * 1024 * 1024)


def iota(shape, dim):
    return lax.broadcasted_iota(jnp.int32, shape, dim)


def rounded_peak(peak):
    return peak.astype(jnp.bfloat16).astype(jnp.float32)


def pack_stats(peak, den):
    high = den.astype(jnp.bfloat16).astype(jnp.float32)
    lane = iota((peak.shape[0], LANES), 1)
    stats = jnp.where(lane == 0, peak, jnp.where(lane == 1, high, den - high))
    return jnp.where(lane < 3, stats, 0.0)


def unpack_stats(stats):
    stats = stats.astype(jnp.float32)
    return stats[:, 0:1], stats[:, 1:2] + stats[:, 2:3]


def spread_rows(dest, base, block, heads, head_size, rows):
    reqs, drafts, _ = block.shape
    pad = rows - reqs * drafts
    for c in range(heads):
        cols = pl.ds(c * head_size, head_size)
        for r in range(reqs):
            dest[pl.ds(base + c * rows + r * drafts, drafts), :] = block[r, :, cols]
        if pad:
            dest[pl.ds(base + c * rows + reqs * drafts, pad), :] = jnp.zeros((pad, head_size), dest.dtype)


def write_keys(page_ref, key_ref, page_tokens):
    lane = iota((8, page_tokens), 1)
    for s in range(page_ref.shape[0]):
        key_ref[:, pl.ds(s * page_tokens, page_tokens)] = lane + page_ref[s] * page_tokens


def layout_kernel(device_of, slots, local, rows, heads, drafts, page_tokens,
                  ids_hbm, len_hbm, page_hbm, q_ref, pool_ref,
                  low_ref, high_ref, key_ref, q_out_ref, pool_out_ref,
                  ids_ref, len_ref, page_ref, start_ref, sems):
    pairs = [(ids_hbm, ids_ref), (len_hbm, len_ref), (page_hbm, page_ref), (pool_ref, pool_out_ref), (q_ref, q_out_ref)]
    copies = [pltpu.make_async_copy(a, b, sems.at[i]) for i, (a, b) in enumerate(pairs)]
    for copy in copies:
        copy.start()
    me = lax.axis_index("blk")
    prompts = len_ref.shape[0]
    shift = SAMPLES.bit_length() - 1
    for copy in copies[:3]:
        copy.wait()

    def place(p, start):
        start_ref[p] = start
        return start + lax.div(len_ref[p] + page_tokens - 1, page_tokens) * page_tokens

    lax.fori_loop(0, prompts, place, jnp.int32(0), unroll=prompts <= 4)
    request = iota((rows, LANES), 0) // drafts

    def one(j, _):
        device = device_of(j, me)
        low = jnp.zeros((rows, LANES), jnp.int32)
        high = low
        for r in range(local):
            prompt = lax.shift_right_logical(ids_ref[device * local + r], shift)
            start = start_ref[prompt]
            low = jnp.where(request == r, start, low)
            high = jnp.where(request == r, start + len_ref[prompt], high)
        for c in range(heads):
            place_at = pl.ds((j * heads + c) * rows, rows)
            low_ref[place_at, :] = low
            high_ref[place_at, :] = high
        return 0

    if slots <= 8:
        for j in range(slots):
            one(j, 0)
    else:
        lax.fori_loop(0, slots, one, 0)
    write_keys(page_ref, key_ref, page_tokens)
    for copy in copies[3:]:
        copy.wait()


def key_row(ref, at, page_tokens):
    if ref.shape[0] > 1:
        return ref[0:1, at:at + LANES]
    lane = iota((1, LANES), 1)
    first = at // page_tokens
    page = ref[:, first:first + 1]
    for n in range(1, LANES // page_tokens):
        page = jnp.where(lane >= n * page_tokens, ref[:, first + n:first + n + 1], page)
    return page * page_tokens + lane % page_tokens


def prefix_kernel(heads, rows, scale, sources, parts_out, *refs):
    q_refs, refs = refs[:sources], refs[sources:]
    (low_ref, high_ref), refs = refs[:2], refs[2:]
    both_refs, out_refs, q_rows = refs[:-parts_out - 1], refs[-parts_out - 1:-1], refs[-1]
    key_refs, pool_refs = both_refs[:len(both_refs) // 2], both_refs[len(both_refs) // 2:]
    blocks = list(q_refs) if len(q_refs[0].shape) == 3 else [q_refs[0].at[j] for j in range(q_refs[0].shape[0])]
    slots = len(blocks)
    pages, page_tokens, head_pair = pool_refs[0].shape
    head_size = head_pair // 2
    for j, block in enumerate(blocks):
        spread_rows(q_rows, j * heads * rows, block, heads, head_size, rows)
    low, high = low_ref[...], high_ref[...]
    queries = q_rows[...]
    chunk = CHUNK if pages % CHUNK == 0 else pages
    masked = []
    for key_ref, pool_ref in zip(key_refs, pool_refs):
        for first in range(0, pages, chunk):
            keys = pool_ref[first:first + chunk, :, :head_size].reshape(chunk * page_tokens, head_size)
            logits = lax.dot_general(queries, keys, (((1,), (1,)), ((), ())), preferred_element_type=jnp.float32)
            parts = []
            for k in range(0, chunk * page_tokens, LANES):
                key = key_row(key_ref, first * page_tokens + k, page_tokens)
                live = (key >= low) & (key < high)
                parts.append(jnp.where(live, logits[:, k:k + LANES] * scale, FLOOR))
            masked.append((pool_ref, first, jnp.concatenate(parts, axis=1)))
    num = den = peak = None
    for pool_ref, first, logits in masked:
        top = rounded_peak(jnp.max(logits, axis=1, keepdims=True))
        if peak is not None:
            top = jnp.maximum(top, peak)
        weights = jnp.exp2(logits - top)
        chunk_den = jnp.sum(weights, axis=1, keepdims=True)
        values = pool_ref[first:first + chunk, :, head_size:].reshape(chunk * page_tokens, head_size)
        chunk_num = jnp.dot(weights.astype(jnp.bfloat16), values, preferred_element_type=jnp.float32)
        if peak is None:
            num, den = chunk_num, chunk_den
        else:
            kept = jnp.exp2(peak - top)
            num, den = num * kept + chunk_num, den * kept + chunk_den
        peak = top
    per = heads * rows
    stats = pack_stats(peak, den)
    outs = list(out_refs) if len(out_refs[0].shape) == 2 else [out_refs[0].at[j] for j in range(slots)]
    for j, out_ref in enumerate(outs):
        out_ref[:, :head_size] = num[j * per:(j + 1) * per].astype(out_ref.dtype)
        out_ref[:, head_size:] = stats[j * per:(j + 1) * per].astype(out_ref.dtype)


def own_kernel(heads, rows, scale, len_ref, q_ref, tail_ref, fresh_ref, out_ref, q_rows, f_rows):
    reqs, drafts, _ = q_ref.shape
    tail = tail_ref.shape[1]
    head_size = tail_ref.shape[2] // 2
    spread_rows(q_rows, 0, q_ref, heads, head_size, rows)
    spread_rows(f_rows, 0, fresh_ref, 2, head_size, rows)
    queries = q_rows[...]
    contract = (((1,), (1,)), ((), ()))
    logits = lax.dot_general(
        queries, tail_ref[:, :, :head_size].reshape(reqs * tail, head_size),
        contract, preferred_element_type=jnp.float32,
    )
    total = heads * rows
    row = iota((total, tail), 0) % rows
    lane = iota((total, tail), 1)
    parts = []
    for r in range(reqs):
        live = (row // drafts == r) & (lane < len_ref[r])
        parts.append(jnp.where(live, logits[:, r * tail:(r + 1) * tail] * scale, FLOOR))
    fresh = lax.dot_general(
        queries, f_rows[0:rows, :], contract, preferred_element_type=jnp.float32
    )
    row = iota((total, rows), 0) % rows
    key = iota((total, rows), 1)
    live = (row // drafts == key // drafts) & (key % drafts <= row % drafts)
    fresh = jnp.where(live, fresh * scale, FLOOR)
    logits = jnp.concatenate(parts, axis=1)
    peak = jnp.maximum(
        jnp.max(logits, axis=1, keepdims=True), jnp.max(fresh, axis=1, keepdims=True)
    )
    peak = rounded_peak(peak)
    weights = jnp.exp2(logits - peak)
    fresh = jnp.exp2(fresh - peak)
    den = jnp.sum(weights, axis=1, keepdims=True) + jnp.sum(fresh, axis=1, keepdims=True)
    num = jnp.dot(
        weights.astype(jnp.bfloat16), tail_ref[:, :, head_size:].reshape(reqs * tail, head_size),
        preferred_element_type=jnp.float32,
    )
    num = num + jnp.dot(
        fresh.astype(jnp.bfloat16), f_rows[rows:2 * rows, :], preferred_element_type=jnp.float32
    )
    out_ref[:, :head_size] = num
    out_ref[:, head_size:] = pack_stats(peak, den)


def summed_parts(blocks, head_size):
    nums = [b[:, :head_size].astype(jnp.float32) for b in blocks]
    stats = [unpack_stats(b[:, head_size:]) for b in blocks]
    peak = functools.reduce(jnp.maximum, [s[0] for s in stats])
    factors = [jnp.exp2(s[0] - peak) for s in stats]
    num = sum(n * f for n, f in zip(nums, factors))
    den = sum(s[1] * f for s, f in zip(stats, factors))
    return num, peak, den


def project(num, den, weight_ref, out_ref, heads, rows):
    reqs, drafts, _ = out_ref.shape
    attention = (num / den).astype(jnp.bfloat16)
    head_size = attention.shape[1]
    value = sum(
        jnp.dot(
            attention[c * rows:(c + 1) * rows, :], weight_ref[c * head_size:(c + 1) * head_size, :],
            preferred_element_type=jnp.float32,
        )
        for c in range(heads)
    ).astype(out_ref.dtype)
    for r in range(reqs):
        out_ref[r] = value[r * drafts:(r + 1) * drafts, :]


def combine_kernel(heads, rows, head_size, *refs):
    *block_refs, weight_ref, out_ref = refs
    num, _, den = summed_parts([b[...] for b in block_refs], head_size)
    project(num, den, weight_ref, out_ref, heads, rows)


def combine_many_kernel(heads, rows, head_size, own_ref, many_ref, weight_ref, out_ref):
    def one(j, carry):
        num, peak, den = carry
        block = many_ref[j]
        next_peak, next_den = unpack_stats(block[:, head_size:])
        top = jnp.maximum(peak, next_peak)
        old, new = jnp.exp2(peak - top), jnp.exp2(next_peak - top)
        return num * old + block[:, :head_size].astype(jnp.float32) * new, top, den * old + next_den * new

    own = own_ref[...]
    carry = (own[:, :head_size], *unpack_stats(own[:, head_size:]))
    num, _, den = lax.fori_loop(0, many_ref.shape[0], one, carry)
    project(num, den, weight_ref, out_ref, heads, rows)


def final_kernel(*refs):
    *part_refs, hidden_ref, gain_ref, score_ref, out_ref, scores_ref = refs
    reqs, drafts, width = hidden_ref.shape
    mix = gain_ref[...] * score_ref[...]
    lane = iota((1, LANES), 1)
    scores = jnp.zeros((1, LANES), jnp.float32)
    for r in range(reqs):
        total = sum(p[r].astype(jnp.float32) for p in part_refs)
        value = (hidden_ref[r].astype(jnp.float32) + total).astype(out_ref.dtype)
        out_ref[r] = value
        last = value.astype(jnp.float32)[drafts - 1:drafts, :]
        square = jnp.sum(last * last, axis=1, keepdims=True) / width
        score = jnp.sum(last * mix, axis=1, keepdims=True) * lax.rsqrt(square + 1e-06)
        scores = jnp.where(lane == r, score, scores)
    scores_ref[...] = scores[0, :reqs]


def body(sizes, prefix_pool, slot_page, prompt_len, request_ids, tail_len, tail_cache, queries, new_kv, hidden,
         out_weight, norm_gain, score_weight):
    blk, kv = sizes
    pool = prefix_pool[0]
    page_count, page_tokens, head_pair = pool.shape
    head_size = head_pair // 2
    local, drafts, head_width = queries.shape
    heads = head_width // head_size
    rows = round_up(local * drafts, 16)
    per = heads * rows
    keys = page_count * page_tokens
    width = hidden.shape[2]
    scale = head_size ** (-0.5) * LOG2E
    paired = blk in (2, 4, 8)
    half = blk // 2
    partners = [0] + [j for j in ORDER_A if j < half]
    masks = [0] + [2 * j + 1 for j in partners[1:]]

    def swap(x, axis, size, mask):
        return lax.ppermute(x, axis, [(i, i ^ mask) for i in range(size)])

    def device_of(j, me):
        return me ^ masks[j] if paired else j

    slots = half if paired else blk
    pools = [pool]
    if paired:
        pools.append(swap(pool, "blk", blk, 1))
        far_pages = swap(slot_page, "blk", blk, 1)

    in_hbm = functools.partial(pltpu.with_memory_space_constraint, memory_space=pltpu.HBM)
    low, high, near_keys, near_queries, pools[0] = pl.pallas_call(
        functools.partial(layout_kernel, device_of, slots, local, rows, heads, drafts, page_tokens),
        out_shape=(
            jax.ShapeDtypeStruct((slots * per, LANES), jnp.int32),
            jax.ShapeDtypeStruct((slots * per, LANES), jnp.int32),
            jax.ShapeDtypeStruct((8, keys), jnp.int32),
            jax.ShapeDtypeStruct(queries.shape, queries.dtype),
            jax.ShapeDtypeStruct(pool.shape, pool.dtype),
        ),
        in_specs=[ANY] * 5,
        out_specs=(VMEM,) * 3 + (ANY,) * 2,
        scratch_shapes=[
            pltpu.SMEM(request_ids.shape, jnp.int32),
            pltpu.SMEM(prompt_len.shape, jnp.int32),
            pltpu.SMEM(slot_page.shape, jnp.int32),
            pltpu.SMEM(prompt_len.shape, jnp.int32),
            pltpu.SemaphoreType.DMA((5,)),
        ],
        compiler_params=vmem(8),
        cost_estimate=cost(1, 2 * slots * per * LANES * 4),
        name="key_ranges",
    )(*map(in_hbm, (request_ids, prompt_len, slot_page, queries, pool)))
    key_lists = [near_keys]
    if paired:
        key_lists.append(far_pages.reshape(1, page_count))

    own = pl.pallas_call(
        functools.partial(own_kernel, heads, rows, scale),
        out_shape=jax.ShapeDtypeStruct((per, head_size + LANES), jnp.float32),
        in_specs=[SMEM] + [VMEM] * 3,
        out_specs=VMEM,
        scratch_shapes=[
            pltpu.VMEM((per, head_size), jnp.bfloat16),
            pltpu.VMEM((2 * rows, head_size), jnp.bfloat16),
        ],
        compiler_params=vmem(8),
        cost_estimate=cost(4 * per * local * tail_cache.shape[2] * head_size, 2 * tail_cache.size),
        name="own_keys",
    )(tail_len, queries, tail_cache[0], new_kv[0])

    block_shape = jax.ShapeDtypeStruct((per, head_size + LANES), jnp.bfloat16)
    scratch = [pltpu.VMEM((min(slots, 4) * per, head_size), jnp.bfloat16)]
    price = cost(4 * slots * per * keys * len(pools) * head_size, 2 * pool.size * len(pools))

    def prefix_column(blocks):
        return pl.pallas_call(
            functools.partial(prefix_kernel, heads, rows, scale, slots, slots),
            out_shape=(block_shape,) * slots,
            in_specs=[VMEM] * (slots + 2 + 2 * len(pools)),
            out_specs=(VMEM,) * slots,
            scratch_shapes=scratch,
            compiler_params=vmem(24),
            cost_estimate=price,
            name="prefix_keys",
        )(*blocks, low, high, *key_lists, *pools)

    def prefix_many(block):
        step = min(slots, 4)
        return pl.pallas_call(
            functools.partial(prefix_kernel, heads, rows, scale, 1, 1),
            out_shape=jax.ShapeDtypeStruct((slots,) + block_shape.shape, jnp.bfloat16),
            grid=(slots // step,),
            in_specs=[
                pl.BlockSpec((step, local, drafts, head_width), lambda i: (i, 0, 0, 0)),
                pl.BlockSpec((step * per, LANES), lambda i: (i, 0)),
                pl.BlockSpec((step * per, LANES), lambda i: (i, 0)),
                pl.BlockSpec((8, keys), lambda i: (0, 0)),
                pl.BlockSpec((page_count, page_tokens, head_pair), lambda i: (0, 0, 0)),
            ],
            out_specs=pl.BlockSpec((step,) + block_shape.shape, lambda i: (i, 0, 0)),
            scratch_shapes=scratch,
            compiler_params=vmem(24),
            cost_estimate=price,
            name="prefix_keys",
        )(block, low, high, *key_lists, *pools)

    partial_shape = jax.ShapeDtypeStruct((local, drafts, width), jnp.bfloat16)
    if paired:
        column = [near_queries] + [swap(queries, "blk", blk, mask) for mask in masks[1:]]
        sums = prefix_column(column)
        blocks = [sums[0]] + [
            swap(sums[partners.index(j)], "blk", blk, 2 * j + 1) for j in ORDER_B if j < half
        ]
        share = pl.pallas_call(
            functools.partial(combine_kernel, heads, rows, head_size),
            out_shape=partial_shape,
            in_specs=[VMEM] * (half + 2),
            out_specs=VMEM,
            compiler_params=vmem(12),
            cost_estimate=cost(2 * per * head_size * width, 2 * out_weight.size),
            name="combine_project",
        )(own, *blocks, out_weight)
    else:
        gathered = lax.all_gather(queries, "blk", axis=0)
        blocks = lax.all_to_all(prefix_many(gathered), "blk", 0, 0)
        share = pl.pallas_call(
            functools.partial(combine_many_kernel, heads, rows, head_size),
            out_shape=partial_shape,
            in_specs=[VMEM] * 3,
            out_specs=VMEM,
            compiler_params=vmem(12),
            cost_estimate=cost(2 * per * head_size * width, 2 * out_weight.size),
            name="combine_project",
        )(own, blocks, out_weight)
    if kv in (2, 4):
        shares = [share] + [swap(share, "kv", kv, j) for j in ORDER_C if j < kv]
    else:
        shares = [lax.psum(share, "kv")]
    hidden_out, scores = pl.pallas_call(
        final_kernel,
        out_shape=(
            jax.ShapeDtypeStruct(hidden.shape, hidden.dtype),
            jax.ShapeDtypeStruct((local,), jnp.float32),
        ),
        in_specs=[VMEM] * (len(shares) + 3),
        out_specs=(VMEM, VMEM),
        compiler_params=vmem(8),
        cost_estimate=cost(1, 2 * hidden.size * 6),
        name="residual_scores",
    )(*shares, hidden, norm_gain.reshape(1, width), score_weight.reshape(1, width))
    return hidden_out, scores


def solution(mesh):
    in_specs = (
        P("kv", "blk", None, None),
        P("blk"),
        P(),
        P(),
        P("blk"),
        P("kv", "blk", None, None),
        P("blk", None, "kv"),
        P("kv", "blk", None, None),
        P("blk", None, None),
        P("kv", None),
        P(),
        P(),
    )
    out_specs = (P("blk", None, None), P("blk"))
    sizes = (mesh.shape["blk"], mesh.shape["kv"])
    return jax.shard_map(
        functools.partial(body, sizes), mesh=mesh, in_specs=in_specs, out_specs=out_specs, check_vma=False
    )
```

```python
import functools

import jax
import jax.numpy as jnp
from jax import lax
from jax.experimental import pallas as pl
from jax.experimental.pallas import tpu as pltpu
from jax.sharding import PartitionSpec as P

SAMPLES = 16
CHUNK = 8
ORDER_A = (2, 3, 1)
ORDER_B = (3, 1, 2)
ORDER_C = (1, 2, 3)
LANES = 128
FLOOR = -(2.0**100)
LOG2E = 1.4426950408889634
ANY = pl.BlockSpec(memory_space=pl.ANY)
VMEM = pl.BlockSpec(memory_space=pltpu.VMEM)
SMEM = pl.BlockSpec(memory_space=pltpu.SMEM)


def round_up(value, unit):
    return (value + unit - 1) // unit * unit


def cost(flops, size):
    return pl.CostEstimate(flops=flops, bytes_accessed=size, transcendentals=0)


def vmem(mebibytes):
    return pltpu.CompilerParams(vmem_limit_bytes=mebibytes * 1024 * 1024)


def iota(shape, dim):
    return lax.broadcasted_iota(jnp.int32, shape, dim)


def rounded_peak(peak):
    return peak.astype(jnp.bfloat16).astype(jnp.float32)


def pack_stats(peak, den):
    high = den.astype(jnp.bfloat16).astype(jnp.float32)
    lane = iota((peak.shape[0], LANES), 1)
    stats = jnp.where(lane == 0, peak, jnp.where(lane == 1, high, den - high))
    return jnp.where(lane < 3, stats, 0.0)


def unpack_stats(stats):
    stats = stats.astype(jnp.float32)
    return stats[:, 0:1], stats[:, 1:2] + stats[:, 2:3]


def spread_rows(dest, base, block, heads, head_size, rows):
    reqs, drafts, _ = block.shape
    pad = rows - reqs * drafts
    for c in range(heads):
        cols = pl.ds(c * head_size, head_size)
        for r in range(reqs):
            dest[pl.ds(base + c * rows + r * drafts, drafts), :] = block[r, :, cols]
        if pad:
            dest[pl.ds(base + c * rows + reqs * drafts, pad), :] = jnp.zeros((pad, head_size), dest.dtype)


def write_keys(page_ref, key_ref, page_tokens):
    lane = iota((8, page_tokens), 1)
    for s in range(page_ref.shape[0]):
        key_ref[:, pl.ds(s * page_tokens, page_tokens)] = lane + page_ref[s] * page_tokens


def layout_kernel(device_of, slots, local, rows, heads, drafts, page_tokens,
                  ids_hbm, len_hbm, page_hbm, q_ref,
                  low_ref, high_ref, key_ref, q_out_ref,
                  ids_ref, len_ref, page_ref, start_ref, sems):
    pairs = [(ids_hbm, ids_ref), (len_hbm, len_ref), (page_hbm, page_ref), (q_ref, q_out_ref)]
    copies = [pltpu.make_async_copy(a, b, sems.at[i]) for i, (a, b) in enumerate(pairs)]
    for copy in copies:
        copy.start()
    me = lax.axis_index("blk")
    prompts = len_ref.shape[0]
    shift = SAMPLES.bit_length() - 1
    for copy in copies[:3]:
        copy.wait()

    def place(p, start):
        start_ref[p] = start
        return start + lax.div(len_ref[p] + page_tokens - 1, page_tokens) * page_tokens

    lax.fori_loop(0, prompts, place, jnp.int32(0), unroll=prompts <= 4)
    request = iota((rows, LANES), 0) // drafts

    def one(j, _):
        device = device_of(j, me)
        low = jnp.zeros((rows, LANES), jnp.int32)
        high = low
        for r in range(local):
            prompt = lax.shift_right_logical(ids_ref[device * local + r], shift)
            start = start_ref[prompt]
            low = jnp.where(request == r, start, low)
            high = jnp.where(request == r, start + len_ref[prompt], high)
        for c in range(heads):
            place_at = pl.ds((j * heads + c) * rows, rows)
            low_ref[place_at, :] = low
            high_ref[place_at, :] = high
        return 0

    if slots <= 8:
        for j in range(slots):
            one(j, 0)
    else:
        lax.fori_loop(0, slots, one, 0)
    write_keys(page_ref, key_ref, page_tokens)
    for copy in copies[3:]:
        copy.wait()


def flip_kernel(page_tokens, *refs):
    pools = 2 if len(refs) == 6 else 1
    page_refs, pool_refs, key_refs, flip_refs = refs[:pools - 1], refs[pools - 1:2 * pools - 1], refs[2 * pools - 1:-pools], refs[-pools:]
    for page_ref, key_ref in zip(page_refs, key_refs):
        write_keys(page_ref, key_ref, page_tokens)
    for pool_ref, flip_ref in zip(pool_refs, flip_refs):
        pages, tokens, head_pair = pool_ref.shape
        keys = pool_ref[:, :, :head_pair // 2].reshape(pages * tokens, head_pair // 2)
        flip_ref[...] = keys.T


def prefix_kernel(heads, rows, scale, sources, parts_out, *refs):
    q_refs, refs = refs[:sources], refs[sources:]
    (low_ref, high_ref), refs = refs[:2], refs[2:]
    both_refs, out_refs, q_rows = refs[:-parts_out - 1], refs[-parts_out - 1:-1], refs[-1]
    count = len(both_refs) // 3
    key_refs, flip_refs, pool_refs = both_refs[:count], both_refs[count:2 * count], both_refs[2 * count:]
    blocks = list(q_refs) if len(q_refs[0].shape) == 3 else [q_refs[0].at[j] for j in range(q_refs[0].shape[0])]
    slots = len(blocks)
    pages, page_tokens, head_pair = pool_refs[0].shape
    head_size = head_pair // 2
    for j, block in enumerate(blocks):
        spread_rows(q_rows, j * heads * rows, block, heads, head_size, rows)
    low, high = low_ref[...], high_ref[...]
    queries = q_rows[...]
    chunk = CHUNK if pages % CHUNK == 0 else pages
    masked = []
    for key_ref, flip_ref, pool_ref in zip(key_refs, flip_refs, pool_refs):
        for first in range(0, pages, chunk):
            at = first * page_tokens
            logits = jnp.dot(queries, flip_ref[:, at:at + chunk * page_tokens], preferred_element_type=jnp.float32)
            parts = []
            for k in range(0, chunk * page_tokens, LANES):
                key = key_ref[0:1, at + k:at + k + LANES]
                live = (key >= low) & (key < high)
                parts.append(jnp.where(live, logits[:, k:k + LANES] * scale, FLOOR))
            masked.append((pool_ref, first, jnp.concatenate(parts, axis=1)))
    num = den = peak = None
    for pool_ref, first, logits in masked:
        top = rounded_peak(jnp.max(logits, axis=1, keepdims=True))
        if peak is not None:
            top = jnp.maximum(top, peak)
        weights = jnp.exp2(logits - top)
        chunk_den = jnp.sum(weights, axis=1, keepdims=True)
        values = pool_ref[first:first + chunk, :, head_size:].reshape(chunk * page_tokens, head_size)
        chunk_num = jnp.dot(weights.astype(jnp.bfloat16), values, preferred_element_type=jnp.float32)
        if peak is None:
            num, den = chunk_num, chunk_den
        else:
            kept = jnp.exp2(peak - top)
            num, den = num * kept + chunk_num, den * kept + chunk_den
        peak = top
    per = heads * rows
    stats = pack_stats(peak, den)
    outs = list(out_refs) if len(out_refs[0].shape) == 2 else [out_refs[0].at[j] for j in range(slots)]
    for j, out_ref in enumerate(outs):
        out_ref[:, :head_size] = num[j * per:(j + 1) * per].astype(out_ref.dtype)
        out_ref[:, head_size:] = stats[j * per:(j + 1) * per].astype(out_ref.dtype)


def own_kernel(heads, rows, scale, len_ref, q_ref, tail_ref, fresh_ref, out_ref, q_rows, f_rows):
    reqs, drafts, _ = q_ref.shape
    tail = tail_ref.shape[1]
    head_size = tail_ref.shape[2] // 2
    spread_rows(q_rows, 0, q_ref, heads, head_size, rows)
    spread_rows(f_rows, 0, fresh_ref, 2, head_size, rows)
    queries = q_rows[...]
    contract = (((1,), (1,)), ((), ()))
    logits = lax.dot_general(
        queries, tail_ref[:, :, :head_size].reshape(reqs * tail, head_size),
        contract, preferred_element_type=jnp.float32,
    )
    total = heads * rows
    row = iota((total, tail), 0) % rows
    lane = iota((total, tail), 1)
    parts = []
    for r in range(reqs):
        live = (row // drafts == r) & (lane < len_ref[r])
        parts.append(jnp.where(live, logits[:, r * tail:(r + 1) * tail] * scale, FLOOR))
    fresh = lax.dot_general(
        queries, f_rows[0:rows, :], contract, preferred_element_type=jnp.float32
    )
    row = iota((total, rows), 0) % rows
    key = iota((total, rows), 1)
    live = (row // drafts == key // drafts) & (key % drafts <= row % drafts)
    fresh = jnp.where(live, fresh * scale, FLOOR)
    logits = jnp.concatenate(parts, axis=1)
    peak = jnp.maximum(
        jnp.max(logits, axis=1, keepdims=True), jnp.max(fresh, axis=1, keepdims=True)
    )
    peak = rounded_peak(peak)
    weights = jnp.exp2(logits - peak)
    fresh = jnp.exp2(fresh - peak)
    den = jnp.sum(weights, axis=1, keepdims=True) + jnp.sum(fresh, axis=1, keepdims=True)
    num = jnp.dot(
        weights.astype(jnp.bfloat16), tail_ref[:, :, head_size:].reshape(reqs * tail, head_size),
        preferred_element_type=jnp.float32,
    )
    num = num + jnp.dot(
        fresh.astype(jnp.bfloat16), f_rows[rows:2 * rows, :], preferred_element_type=jnp.float32
    )
    out_ref[:, :head_size] = num
    out_ref[:, head_size:] = pack_stats(peak, den)


def summed_parts(blocks, head_size):
    nums = [b[:, :head_size].astype(jnp.float32) for b in blocks]
    stats = [unpack_stats(b[:, head_size:]) for b in blocks]
    peak = functools.reduce(jnp.maximum, [s[0] for s in stats])
    factors = [jnp.exp2(s[0] - peak) for s in stats]
    num = sum(n * f for n, f in zip(nums, factors))
    den = sum(s[1] * f for s, f in zip(stats, factors))
    return num, peak, den


def project(num, den, weight_ref, out_ref, heads, rows):
    reqs, drafts, _ = out_ref.shape
    attention = (num / den).astype(jnp.bfloat16)
    head_size = attention.shape[1]
    value = sum(
        jnp.dot(
            attention[c * rows:(c + 1) * rows, :], weight_ref[c * head_size:(c + 1) * head_size, :],
            preferred_element_type=jnp.float32,
        )
        for c in range(heads)
    ).astype(out_ref.dtype)
    for r in range(reqs):
        out_ref[r] = value[r * drafts:(r + 1) * drafts, :]


def combine_kernel(heads, rows, head_size, *refs):
    *block_refs, weight_ref, out_ref = refs
    num, _, den = summed_parts([b[...] for b in block_refs], head_size)
    project(num, den, weight_ref, out_ref, heads, rows)


def combine_many_kernel(heads, rows, head_size, own_ref, many_ref, weight_ref, out_ref):
    def one(j, carry):
        num, peak, den = carry
        block = many_ref[j]
        next_peak, next_den = unpack_stats(block[:, head_size:])
        top = jnp.maximum(peak, next_peak)
        old, new = jnp.exp2(peak - top), jnp.exp2(next_peak - top)
        return num * old + block[:, :head_size].astype(jnp.float32) * new, top, den * old + next_den * new

    own = own_ref[...]
    carry = (own[:, :head_size], *unpack_stats(own[:, head_size:]))
    num, _, den = lax.fori_loop(0, many_ref.shape[0], one, carry)
    project(num, den, weight_ref, out_ref, heads, rows)


def final_kernel(*refs):
    *part_refs, hidden_ref, gain_ref, score_ref, out_ref, scores_ref = refs
    reqs, drafts, width = hidden_ref.shape
    mix = gain_ref[...] * score_ref[...]
    lane = iota((1, LANES), 1)
    scores = jnp.zeros((1, LANES), jnp.float32)
    for r in range(reqs):
        total = sum(p[r].astype(jnp.float32) for p in part_refs)
        value = (hidden_ref[r].astype(jnp.float32) + total).astype(out_ref.dtype)
        out_ref[r] = value
        last = value.astype(jnp.float32)[drafts - 1:drafts, :]
        square = jnp.sum(last * last, axis=1, keepdims=True) / width
        score = jnp.sum(last * mix, axis=1, keepdims=True) * lax.rsqrt(square + 1e-06)
        scores = jnp.where(lane == r, score, scores)
    scores_ref[...] = scores[0, :reqs]


def body(sizes, prefix_pool, slot_page, prompt_len, request_ids, tail_len, tail_cache, queries, new_kv, hidden,
         out_weight, norm_gain, score_weight):
    blk, kv = sizes
    pool = prefix_pool[0]
    page_count, page_tokens, head_pair = pool.shape
    head_size = head_pair // 2
    local, drafts, head_width = queries.shape
    heads = head_width // head_size
    rows = round_up(local * drafts, 16)
    per = heads * rows
    keys = page_count * page_tokens
    width = hidden.shape[2]
    scale = head_size ** (-0.5) * LOG2E
    paired = blk in (2, 4, 8)
    half = blk // 2
    partners = [0] + [j for j in ORDER_A if j < half]
    masks = [0] + [2 * j + 1 for j in partners[1:]]

    def swap(x, axis, size, mask):
        return lax.ppermute(x, axis, [(i, i ^ mask) for i in range(size)])

    def device_of(j, me):
        return me ^ masks[j] if paired else j

    slots = half if paired else blk
    pools = [pool]
    if paired:
        pools.append(swap(pool, "blk", blk, 1))
        far_pages = swap(slot_page, "blk", blk, 1)

    in_hbm = functools.partial(pltpu.with_memory_space_constraint, memory_space=pltpu.HBM)
    low, high, near_keys, near_queries = pl.pallas_call(
        functools.partial(layout_kernel, device_of, slots, local, rows, heads, drafts, page_tokens),
        out_shape=(
            jax.ShapeDtypeStruct((slots * per, LANES), jnp.int32),
            jax.ShapeDtypeStruct((slots * per, LANES), jnp.int32),
            jax.ShapeDtypeStruct((8, keys), jnp.int32),
            jax.ShapeDtypeStruct(queries.shape, queries.dtype),
        ),
        in_specs=[ANY] * 4,
        out_specs=(VMEM,) * 3 + (ANY,),
        scratch_shapes=[
            pltpu.SMEM(request_ids.shape, jnp.int32),
            pltpu.SMEM(prompt_len.shape, jnp.int32),
            pltpu.SMEM(slot_page.shape, jnp.int32),
            pltpu.SMEM(prompt_len.shape, jnp.int32),
            pltpu.SemaphoreType.DMA((4,)),
        ],
        compiler_params=vmem(8),
        cost_estimate=cost(4 * 10**9, 2 * slots * per * LANES * 4),
        name="key_ranges",
    )(*map(in_hbm, (request_ids, prompt_len, slot_page, queries)))
    flipped = pl.pallas_call(
        functools.partial(flip_kernel, page_tokens),
        out_shape=(jax.ShapeDtypeStruct((8, keys), jnp.int32),) * (len(pools) - 1)
        + (jax.ShapeDtypeStruct((head_size, keys), pool.dtype),) * len(pools),
        in_specs=[SMEM] * (len(pools) - 1) + [VMEM] * len(pools),
        out_specs=(VMEM,) * (2 * len(pools) - 1),
        compiler_params=vmem(12),
        cost_estimate=cost(10**9, 4 * pool.size * len(pools)),
        name="flip_keys",
    )(*([far_pages] if paired else []), *pools)
    key_lists, flips = [near_keys, *flipped[:-len(pools)]], flipped[-len(pools):]

    own = pl.pallas_call(
        functools.partial(own_kernel, heads, rows, scale),
        out_shape=jax.ShapeDtypeStruct((per, head_size + LANES), jnp.float32),
        in_specs=[SMEM] + [VMEM] * 3,
        out_specs=VMEM,
        scratch_shapes=[
            pltpu.VMEM((per, head_size), jnp.bfloat16),
            pltpu.VMEM((2 * rows, head_size), jnp.bfloat16),
        ],
        compiler_params=vmem(8),
        cost_estimate=cost(4 * per * local * tail_cache.shape[2] * head_size, 2 * tail_cache.size),
        name="own_keys",
    )(tail_len, queries, tail_cache[0], new_kv[0])

    block_shape = jax.ShapeDtypeStruct((per, head_size + LANES), jnp.bfloat16)
    scratch = [pltpu.VMEM((min(slots, 4) * per, head_size), jnp.bfloat16)]
    price = cost(4 * slots * per * keys * len(pools) * head_size, 2 * pool.size * len(pools))

    def prefix_column(blocks):
        return pl.pallas_call(
            functools.partial(prefix_kernel, heads, rows, scale, slots, slots),
            out_shape=(block_shape,) * slots,
            in_specs=[VMEM] * (slots + 2 + 3 * len(pools)),
            out_specs=(VMEM,) * slots,
            scratch_shapes=scratch,
            compiler_params=vmem(24),
            cost_estimate=price,
            name="prefix_keys",
        )(*blocks, low, high, *key_lists, *flips, *pools)

    def prefix_many(block):
        step = min(slots, 4)
        return pl.pallas_call(
            functools.partial(prefix_kernel, heads, rows, scale, 1, 1),
            out_shape=jax.ShapeDtypeStruct((slots,) + block_shape.shape, jnp.bfloat16),
            grid=(slots // step,),
            in_specs=[
                pl.BlockSpec((step, local, drafts, head_width), lambda i: (i, 0, 0, 0)),
                pl.BlockSpec((step * per, LANES), lambda i: (i, 0)),
                pl.BlockSpec((step * per, LANES), lambda i: (i, 0)),
                pl.BlockSpec((8, keys), lambda i: (0, 0)),
                pl.BlockSpec((head_size, keys), lambda i: (0, 0)),
                pl.BlockSpec((page_count, page_tokens, head_pair), lambda i: (0, 0, 0)),
            ],
            out_specs=pl.BlockSpec((step,) + block_shape.shape, lambda i: (i, 0, 0)),
            scratch_shapes=scratch,
            compiler_params=vmem(24),
            cost_estimate=price,
            name="prefix_keys",
        )(block, low, high, *key_lists, *flips, *pools)

    partial_shape = jax.ShapeDtypeStruct((local, drafts, width), jnp.bfloat16)
    if paired:
        column = [near_queries] + [swap(queries, "blk", blk, mask) for mask in masks[1:]]
        sums = prefix_column(column)
        blocks = [sums[0]] + [
            swap(sums[partners.index(j)], "blk", blk, 2 * j + 1) for j in ORDER_B if j < half
        ]
        share = pl.pallas_call(
            functools.partial(combine_kernel, heads, rows, head_size),
            out_shape=partial_shape,
            in_specs=[VMEM] * (half + 2),
            out_specs=VMEM,
            compiler_params=vmem(12),
            cost_estimate=cost(2 * per * head_size * width, 2 * out_weight.size),
            name="combine_project",
        )(own, *blocks, out_weight)
    else:
        gathered = lax.all_gather(queries, "blk", axis=0)
        blocks = lax.all_to_all(prefix_many(gathered), "blk", 0, 0)
        share = pl.pallas_call(
            functools.partial(combine_many_kernel, heads, rows, head_size),
            out_shape=partial_shape,
            in_specs=[VMEM] * 3,
            out_specs=VMEM,
            compiler_params=vmem(12),
            cost_estimate=cost(2 * per * head_size * width, 2 * out_weight.size),
            name="combine_project",
        )(own, blocks, out_weight)
    if kv in (2, 4):
        shares = [share] + [swap(share, "kv", kv, j) for j in ORDER_C if j < kv]
    else:
        shares = [lax.psum(share, "kv")]
    hidden_out, scores = pl.pallas_call(
        final_kernel,
        out_shape=(
            jax.ShapeDtypeStruct(hidden.shape, hidden.dtype),
            jax.ShapeDtypeStruct((local,), jnp.float32),
        ),
        in_specs=[VMEM] * (len(shares) + 3),
        out_specs=(VMEM, VMEM),
        compiler_params=vmem(8),
        cost_estimate=cost(1, 2 * hidden.size * 6),
        name="residual_scores",
    )(*shares, hidden, norm_gain.reshape(1, width), score_weight.reshape(1, width))
    return hidden_out, scores


def solution(mesh):
    in_specs = (
        P("kv", "blk", None, None),
        P("blk"),
        P(),
        P(),
        P("blk"),
        P("kv", "blk", None, None),
        P("blk", None, "kv"),
        P("kv", "blk", None, None),
        P("blk", None, None),
        P("kv", None),
        P(),
        P(),
    )
    out_specs = (P("blk", None, None), P("blk"))
    sizes = (mesh.shape["blk"], mesh.shape["kv"])
    return jax.shard_map(
        functools.partial(body, sizes), mesh=mesh, in_specs=in_specs, out_specs=out_specs, check_vma=False
    )
```

```python
import functools

import jax
import jax.numpy as jnp
from jax import lax
from jax.experimental import pallas as pl
from jax.experimental.pallas import tpu as pltpu
from jax.sharding import PartitionSpec as P

SAMPLES = 16
CHUNK = 8
ORDER_A = (2, 3, 1)
ORDER_B = (3, 1, 2)
ORDER_C = (1, 2, 3)
LANES = 128
FLOOR = -(2.0**100)
LOG2E = 1.4426950408889634
ANY = pl.BlockSpec(memory_space=pl.ANY)
VMEM = pl.BlockSpec(memory_space=pltpu.VMEM)
SMEM = pl.BlockSpec(memory_space=pltpu.SMEM)


def round_up(value, unit):
    return (value + unit - 1) // unit * unit


def cost(flops, size):
    return pl.CostEstimate(flops=flops, bytes_accessed=size, transcendentals=0)


def vmem(mebibytes):
    return pltpu.CompilerParams(vmem_limit_bytes=mebibytes * 1024 * 1024)


def iota(shape, dim):
    return lax.broadcasted_iota(jnp.int32, shape, dim)


def rounded_peak(peak):
    return peak.astype(jnp.bfloat16).astype(jnp.float32)


def pack_stats(peak, den):
    high = den.astype(jnp.bfloat16).astype(jnp.float32)
    lane = iota((peak.shape[0], LANES), 1)
    stats = jnp.where(lane == 0, peak, jnp.where(lane == 1, high, den - high))
    return jnp.where(lane < 3, stats, 0.0)


def unpack_stats(stats):
    stats = stats.astype(jnp.float32)
    return stats[:, 0:1], stats[:, 1:2] + stats[:, 2:3]


def spread_rows(dest, base, block, heads, head_size, rows):
    reqs, drafts, _ = block.shape
    pad = rows - reqs * drafts
    for c in range(heads):
        cols = pl.ds(c * head_size, head_size)
        for r in range(reqs):
            dest[pl.ds(base + c * rows + r * drafts, drafts), :] = block[r, :, cols]
        if pad:
            dest[pl.ds(base + c * rows + reqs * drafts, pad), :] = jnp.zeros((pad, head_size), dest.dtype)


def write_keys(page_ref, key_ref, page_tokens):
    lane = iota((8, page_tokens), 1)
    for s in range(page_ref.shape[0]):
        key_ref[:, pl.ds(s * page_tokens, page_tokens)] = lane + page_ref[s] * page_tokens


def layout_kernel(device_of, slots, local, rows, heads, drafts, page_tokens,
                  ids_hbm, len_hbm, page_hbm, q_ref,
                  low_ref, high_ref, key_ref, q_out_ref,
                  ids_ref, len_ref, page_ref, start_ref, sems):
    pairs = [(ids_hbm, ids_ref), (len_hbm, len_ref), (page_hbm, page_ref), (q_ref, q_out_ref)]
    copies = [pltpu.make_async_copy(a, b, sems.at[i]) for i, (a, b) in enumerate(pairs)]
    for copy in copies:
        copy.start()
    me = lax.axis_index("blk")
    prompts = len_ref.shape[0]
    shift = SAMPLES.bit_length() - 1
    for copy in copies[:3]:
        copy.wait()

    def place(p, start):
        start_ref[p] = start
        return start + lax.div(len_ref[p] + page_tokens - 1, page_tokens) * page_tokens

    lax.fori_loop(0, prompts, place, jnp.int32(0), unroll=prompts <= 4)
    request = iota((rows, LANES), 0) // drafts

    def one(j, _):
        device = device_of(j, me)
        low = jnp.zeros((rows, LANES), jnp.int32)
        high = low
        for r in range(local):
            prompt = lax.shift_right_logical(ids_ref[device * local + r], shift)
            start = start_ref[prompt]
            low = jnp.where(request == r, start, low)
            high = jnp.where(request == r, start + len_ref[prompt], high)
        for c in range(heads):
            place_at = pl.ds((j * heads + c) * rows, rows)
            low_ref[place_at, :] = low
            high_ref[place_at, :] = high
        return 0

    if slots <= 8:
        for j in range(slots):
            one(j, 0)
    else:
        lax.fori_loop(0, slots, one, 0)
    write_keys(page_ref, key_ref, page_tokens)
    for copy in copies[3:]:
        copy.wait()


def flip_kernel(page_tokens, *refs):
    pools = 2 if len(refs) == 6 else 1
    page_refs, pool_refs, key_refs, flip_refs = refs[:pools - 1], refs[pools - 1:2 * pools - 1], refs[2 * pools - 1:-pools], refs[-pools:]
    for page_ref, key_ref in zip(page_refs, key_refs):
        write_keys(page_ref, key_ref, page_tokens)
    for pool_ref, flip_ref in zip(pool_refs, flip_refs):
        pages, tokens, head_pair = pool_ref.shape
        keys = pool_ref[:, :, :head_pair // 2].reshape(pages * tokens, head_pair // 2)
        flip_ref[...] = keys.T


def prefix_kernel(heads, rows, scale, sources, parts_out, first_slot, *refs):
    q_refs, refs = refs[:sources], refs[sources:]
    (low_ref, high_ref), refs = refs[:2], refs[2:]
    both_refs, out_refs, q_rows = refs[:-parts_out - 1], refs[-parts_out - 1:-1], refs[-1]
    count = len(both_refs) // 3
    key_refs, flip_refs, pool_refs = both_refs[:count], both_refs[count:2 * count], both_refs[2 * count:]
    blocks = list(q_refs) if len(q_refs[0].shape) == 3 else [q_refs[0].at[j] for j in range(q_refs[0].shape[0])]
    slots = len(blocks)
    pages, page_tokens, head_pair = pool_refs[0].shape
    head_size = head_pair // 2
    for j, block in enumerate(blocks):
        spread_rows(q_rows, j * heads * rows, block, heads, head_size, rows)
    ranges = pl.ds(first_slot * heads * rows, slots * heads * rows)
    low, high = low_ref[ranges, :], high_ref[ranges, :]
    queries = q_rows[...]
    chunk = CHUNK if pages % CHUNK == 0 else pages
    masked = []
    for key_ref, flip_ref, pool_ref in zip(key_refs, flip_refs, pool_refs):
        for first in range(0, pages, chunk):
            at = first * page_tokens
            logits = jnp.dot(queries, flip_ref[:, at:at + chunk * page_tokens], preferred_element_type=jnp.float32)
            parts = []
            for k in range(0, chunk * page_tokens, LANES):
                key = key_ref[0:1, at + k:at + k + LANES]
                live = (key >= low) & (key < high)
                parts.append(jnp.where(live, logits[:, k:k + LANES] * scale, FLOOR))
            masked.append((pool_ref, first, jnp.concatenate(parts, axis=1)))
    num = den = peak = None
    for pool_ref, first, logits in masked:
        top = rounded_peak(jnp.max(logits, axis=1, keepdims=True))
        if peak is not None:
            top = jnp.maximum(top, peak)
        weights = jnp.exp2(logits - top)
        chunk_den = jnp.sum(weights, axis=1, keepdims=True)
        values = pool_ref[first:first + chunk, :, head_size:].reshape(chunk * page_tokens, head_size)
        chunk_num = jnp.dot(weights.astype(jnp.bfloat16), values, preferred_element_type=jnp.float32)
        if peak is None:
            num, den = chunk_num, chunk_den
        else:
            kept = jnp.exp2(peak - top)
            num, den = num * kept + chunk_num, den * kept + chunk_den
        peak = top
    per = heads * rows
    stats = pack_stats(peak, den)
    outs = list(out_refs) if len(out_refs[0].shape) == 2 else [out_refs[0].at[j] for j in range(slots)]
    for j, out_ref in enumerate(outs):
        out_ref[:, :head_size] = num[j * per:(j + 1) * per].astype(out_ref.dtype)
        out_ref[:, head_size:] = stats[j * per:(j + 1) * per].astype(out_ref.dtype)


def own_kernel(heads, rows, scale, len_ref, q_ref, tail_ref, fresh_ref, weight_ref, out_ref, q_rows, f_rows):
    del weight_ref
    reqs, drafts, _ = q_ref.shape
    tail = tail_ref.shape[1]
    head_size = tail_ref.shape[2] // 2
    spread_rows(q_rows, 0, q_ref, heads, head_size, rows)
    spread_rows(f_rows, 0, fresh_ref, 2, head_size, rows)
    queries = q_rows[...]
    contract = (((1,), (1,)), ((), ()))
    logits = lax.dot_general(
        queries, tail_ref[:, :, :head_size].reshape(reqs * tail, head_size),
        contract, preferred_element_type=jnp.float32,
    )
    total = heads * rows
    row = iota((total, tail), 0) % rows
    lane = iota((total, tail), 1)
    parts = []
    for r in range(reqs):
        live = (row // drafts == r) & (lane < len_ref[r])
        parts.append(jnp.where(live, logits[:, r * tail:(r + 1) * tail] * scale, FLOOR))
    fresh = lax.dot_general(
        queries, f_rows[0:rows, :], contract, preferred_element_type=jnp.float32
    )
    row = iota((total, rows), 0) % rows
    key = iota((total, rows), 1)
    live = (row // drafts == key // drafts) & (key % drafts <= row % drafts)
    fresh = jnp.where(live, fresh * scale, FLOOR)
    logits = jnp.concatenate(parts, axis=1)
    peak = jnp.maximum(
        jnp.max(logits, axis=1, keepdims=True), jnp.max(fresh, axis=1, keepdims=True)
    )
    peak = rounded_peak(peak)
    weights = jnp.exp2(logits - peak)
    fresh = jnp.exp2(fresh - peak)
    den = jnp.sum(weights, axis=1, keepdims=True) + jnp.sum(fresh, axis=1, keepdims=True)
    num = jnp.dot(
        weights.astype(jnp.bfloat16), tail_ref[:, :, head_size:].reshape(reqs * tail, head_size),
        preferred_element_type=jnp.float32,
    )
    num = num + jnp.dot(
        fresh.astype(jnp.bfloat16), f_rows[rows:2 * rows, :], preferred_element_type=jnp.float32
    )
    out_ref[:, :head_size] = num
    out_ref[:, head_size:] = pack_stats(peak, den)


def summed_parts(blocks, head_size):
    nums = [b[:, :head_size].astype(jnp.float32) for b in blocks]
    stats = [unpack_stats(b[:, head_size:]) for b in blocks]
    peak = functools.reduce(jnp.maximum, [s[0] for s in stats])
    factors = [jnp.exp2(s[0] - peak) for s in stats]
    num = sum(n * f for n, f in zip(nums, factors))
    den = sum(s[1] * f for s, f in zip(stats, factors))
    return num, peak, den


def project(num, den, weight_ref, out_ref, heads, rows):
    reqs, drafts, _ = out_ref.shape
    attention = (num / den).astype(jnp.bfloat16)
    head_size = attention.shape[1]
    value = sum(
        jnp.dot(
            attention[c * rows:(c + 1) * rows, :], weight_ref[c * head_size:(c + 1) * head_size, :],
            preferred_element_type=jnp.float32,
        )
        for c in range(heads)
    ).astype(out_ref.dtype)
    for r in range(reqs):
        out_ref[r] = value[r * drafts:(r + 1) * drafts, :]


def combine_kernel(heads, rows, head_size, *refs):
    *block_refs, weight_ref, out_ref = refs
    num, _, den = summed_parts([b[...] for b in block_refs], head_size)
    project(num, den, weight_ref, out_ref, heads, rows)


def combine_many_kernel(heads, rows, head_size, own_ref, many_ref, weight_ref, out_ref):
    def one(j, carry):
        num, peak, den = carry
        block = many_ref[j]
        next_peak, next_den = unpack_stats(block[:, head_size:])
        top = jnp.maximum(peak, next_peak)
        old, new = jnp.exp2(peak - top), jnp.exp2(next_peak - top)
        return num * old + block[:, :head_size].astype(jnp.float32) * new, top, den * old + next_den * new

    own = own_ref[...]
    carry = (own[:, :head_size], *unpack_stats(own[:, head_size:]))
    num, _, den = lax.fori_loop(0, many_ref.shape[0], one, carry)
    project(num, den, weight_ref, out_ref, heads, rows)


def final_kernel(*refs):
    *part_refs, hidden_ref, gain_ref, score_ref, out_ref, scores_ref = refs
    reqs, drafts, width = hidden_ref.shape
    mix = gain_ref[...] * score_ref[...]
    lane = iota((1, LANES), 1)
    scores = jnp.zeros((1, LANES), jnp.float32)
    for r in range(reqs):
        total = sum(p[r].astype(jnp.float32) for p in part_refs)
        value = (hidden_ref[r].astype(jnp.float32) + total).astype(out_ref.dtype)
        out_ref[r] = value
        last = value.astype(jnp.float32)[drafts - 1:drafts, :]
        square = jnp.sum(last * last, axis=1, keepdims=True) / width
        score = jnp.sum(last * mix, axis=1, keepdims=True) * lax.rsqrt(square + 1e-06)
        scores = jnp.where(lane == r, score, scores)
    scores_ref[...] = scores[0, :reqs]


def body(sizes, prefix_pool, slot_page, prompt_len, request_ids, tail_len, tail_cache, queries, new_kv, hidden,
         out_weight, norm_gain, score_weight):
    blk, kv = sizes
    pool = prefix_pool[0]
    page_count, page_tokens, head_pair = pool.shape
    head_size = head_pair // 2
    local, drafts, head_width = queries.shape
    heads = head_width // head_size
    rows = round_up(local * drafts, 16)
    per = heads * rows
    keys = page_count * page_tokens
    width = hidden.shape[2]
    scale = head_size ** (-0.5) * LOG2E
    paired = blk in (2, 4, 8)
    half = blk // 2
    partners = [0] + [j for j in ORDER_A if j < half]
    masks = [0] + [2 * j + 1 for j in partners[1:]]

    def swap(x, axis, size, mask):
        return lax.ppermute(x, axis, [(i, i ^ mask) for i in range(size)])

    def device_of(j, me):
        return me ^ masks[j] if paired else j

    slots = half if paired else blk
    pools = [pool]
    if paired:
        pools.append(swap(pool, "blk", blk, 1))
        far_pages = swap(slot_page, "blk", blk, 1)

    in_hbm = functools.partial(pltpu.with_memory_space_constraint, memory_space=pltpu.HBM)
    low, high, near_keys, near_queries = pl.pallas_call(
        functools.partial(layout_kernel, device_of, slots, local, rows, heads, drafts, page_tokens),
        out_shape=(
            jax.ShapeDtypeStruct((slots * per, LANES), jnp.int32),
            jax.ShapeDtypeStruct((slots * per, LANES), jnp.int32),
            jax.ShapeDtypeStruct((8, keys), jnp.int32),
            jax.ShapeDtypeStruct(queries.shape, queries.dtype),
        ),
        in_specs=[ANY] * 4,
        out_specs=(VMEM,) * 3 + (ANY,),
        scratch_shapes=[
            pltpu.SMEM(request_ids.shape, jnp.int32),
            pltpu.SMEM(prompt_len.shape, jnp.int32),
            pltpu.SMEM(slot_page.shape, jnp.int32),
            pltpu.SMEM(prompt_len.shape, jnp.int32),
            pltpu.SemaphoreType.DMA((4,)),
        ],
        compiler_params=vmem(8),
        cost_estimate=cost(4 * 10**9, 2 * slots * per * LANES * 4),
        name="key_ranges",
    )(*map(in_hbm, (request_ids, prompt_len, slot_page, queries)))
    flipped = pl.pallas_call(
        functools.partial(flip_kernel, page_tokens),
        out_shape=(jax.ShapeDtypeStruct((8, keys), jnp.int32),) * (len(pools) - 1)
        + (jax.ShapeDtypeStruct((head_size, keys), pool.dtype),) * len(pools),
        in_specs=[SMEM] * (len(pools) - 1) + [VMEM] * len(pools),
        out_specs=(VMEM,) * (2 * len(pools) - 1),
        compiler_params=vmem(12),
        cost_estimate=cost(10**9, 4 * pool.size * len(pools)),
        name="flip_keys",
    )(*([far_pages] if paired else []), *pools)
    key_lists, flips = [near_keys, *flipped[:-len(pools)]], flipped[-len(pools):]

    own = pl.pallas_call(
        functools.partial(own_kernel, heads, rows, scale),
        out_shape=jax.ShapeDtypeStruct((per, head_size + LANES), jnp.float32),
        in_specs=[SMEM] + [VMEM] * 4,
        out_specs=VMEM,
        scratch_shapes=[
            pltpu.VMEM((per, head_size), jnp.bfloat16),
            pltpu.VMEM((2 * rows, head_size), jnp.bfloat16),
        ],
        compiler_params=vmem(8),
        cost_estimate=cost(4 * per * local * tail_cache.shape[2] * head_size, 2 * tail_cache.size),
        name="own_keys",
    )(tail_len, queries, tail_cache[0], new_kv[0], out_weight)

    block_shape = jax.ShapeDtypeStruct((per, head_size + LANES), jnp.bfloat16)
    scratch = [pltpu.VMEM((min(slots, 4) * per, head_size), jnp.bfloat16)]
    price = cost(4 * slots * per * keys * len(pools) * head_size, 2 * pool.size * len(pools))

    def prefix_column(blocks, first_slot):
        count = len(blocks)
        return pl.pallas_call(
            functools.partial(prefix_kernel, heads, rows, scale, count, count, first_slot),
            out_shape=(block_shape,) * count,
            in_specs=[VMEM] * (count + 2 + 3 * len(pools)),
            out_specs=(VMEM,) * count,
            scratch_shapes=[pltpu.VMEM((count * per, head_size), jnp.bfloat16)],
            compiler_params=vmem(24),
            cost_estimate=cost(price.flops // slots * count, price.bytes_accessed),
            name="prefix_keys",
        )(*blocks, low, high, *key_lists, *flips, *pools)

    def prefix_many(block):
        step = min(slots, 4)
        return pl.pallas_call(
            functools.partial(prefix_kernel, heads, rows, scale, 1, 1, 0),
            out_shape=jax.ShapeDtypeStruct((slots,) + block_shape.shape, jnp.bfloat16),
            grid=(slots // step,),
            in_specs=[
                pl.BlockSpec((step, local, drafts, head_width), lambda i: (i, 0, 0, 0)),
                pl.BlockSpec((step * per, LANES), lambda i: (i, 0)),
                pl.BlockSpec((step * per, LANES), lambda i: (i, 0)),
                pl.BlockSpec((8, keys), lambda i: (0, 0)),
                pl.BlockSpec((head_size, keys), lambda i: (0, 0)),
                pl.BlockSpec((page_count, page_tokens, head_pair), lambda i: (0, 0, 0)),
            ],
            out_specs=pl.BlockSpec((step,) + block_shape.shape, lambda i: (i, 0, 0)),
            scratch_shapes=scratch,
            compiler_params=vmem(24),
            cost_estimate=price,
            name="prefix_keys",
        )(block, low, high, *key_lists, *flips, *pools)

    partial_shape = jax.ShapeDtypeStruct((local, drafts, width), jnp.bfloat16)
    if paired:
        column = [near_queries] + [swap(queries, "blk", blk, mask) for mask in masks[1:]]
        sums = [None, *prefix_column(column[1:], 1)] if half > 1 else [None]
        sums[0] = prefix_column(column[:1], 0)[0]
        blocks = [sums[0]] + [
            swap(sums[partners.index(j)], "blk", blk, 2 * j + 1) for j in ORDER_B if j < half
        ]
        share = pl.pallas_call(
            functools.partial(combine_kernel, heads, rows, head_size),
            out_shape=partial_shape,
            in_specs=[VMEM] * (half + 2),
            out_specs=VMEM,
            compiler_params=vmem(12),
            cost_estimate=cost(2 * per * head_size * width, 2 * out_weight.size),
            name="combine_project",
        )(own, *blocks, out_weight)
    else:
        gathered = lax.all_gather(queries, "blk", axis=0)
        blocks = lax.all_to_all(prefix_many(gathered), "blk", 0, 0)
        share = pl.pallas_call(
            functools.partial(combine_many_kernel, heads, rows, head_size),
            out_shape=partial_shape,
            in_specs=[VMEM] * 3,
            out_specs=VMEM,
            compiler_params=vmem(12),
            cost_estimate=cost(2 * per * head_size * width, 2 * out_weight.size),
            name="combine_project",
        )(own, blocks, out_weight)
    if kv in (2, 4):
        shares = [share] + [swap(share, "kv", kv, j) for j in ORDER_C if j < kv]
    else:
        shares = [lax.psum(share, "kv")]
    hidden_out, scores = pl.pallas_call(
        final_kernel,
        out_shape=(
            jax.ShapeDtypeStruct(hidden.shape, hidden.dtype),
            jax.ShapeDtypeStruct((local,), jnp.float32),
        ),
        in_specs=[VMEM] * (len(shares) + 3),
        out_specs=(VMEM, VMEM),
        compiler_params=vmem(8),
        cost_estimate=cost(1, 2 * hidden.size * 6),
        name="residual_scores",
    )(*shares, hidden, norm_gain.reshape(1, width), score_weight.reshape(1, width))
    return hidden_out, scores


def solution(mesh):
    in_specs = (
        P("kv", "blk", None, None),
        P("blk"),
        P(),
        P(),
        P("blk"),
        P("kv", "blk", None, None),
        P("blk", None, "kv"),
        P("kv", "blk", None, None),
        P("blk", None, None),
        P("kv", None),
        P(),
        P(),
    )
    out_specs = (P("blk", None, None), P("blk"))
    sizes = (mesh.shape["blk"], mesh.shape["kv"])
    return jax.shard_map(
        functools.partial(body, sizes), mesh=mesh, in_specs=in_specs, out_specs=out_specs, check_vma=False
    )
```

```python
import functools

import jax
import jax.numpy as jnp
from jax import lax
from jax.experimental import pallas as pl
from jax.experimental.pallas import tpu as pltpu
from jax.sharding import PartitionSpec as P

SAMPLES = 16
CHUNK = 8
ORDER_A = (2, 3, 1)
ORDER_B = (3, 1, 2)
ORDER_C = (1, 2, 3)
LANES = 128
FLOOR = -(2.0**100)
LOG2E = 1.4426950408889634
ANY = pl.BlockSpec(memory_space=pl.ANY)
VMEM = pl.BlockSpec(memory_space=pltpu.VMEM)
SMEM = pl.BlockSpec(memory_space=pltpu.SMEM)


def round_up(value, unit):
    return (value + unit - 1) // unit * unit


def cost(flops, size):
    return pl.CostEstimate(flops=flops, bytes_accessed=size, transcendentals=0)


def vmem(mebibytes):
    return pltpu.CompilerParams(vmem_limit_bytes=mebibytes * 1024 * 1024)


def iota(shape, dim):
    return lax.broadcasted_iota(jnp.int32, shape, dim)


def rounded_peak(peak):
    return peak.astype(jnp.bfloat16).astype(jnp.float32)


def pack_stats(peak, den):
    high = den.astype(jnp.bfloat16).astype(jnp.float32)
    lane = iota((peak.shape[0], LANES), 1)
    stats = jnp.where(lane == 0, peak, jnp.where(lane == 1, high, den - high))
    return jnp.where(lane < 3, stats, 0.0)


def unpack_stats(stats):
    stats = stats.astype(jnp.float32)
    return stats[:, 0:1], stats[:, 1:2] + stats[:, 2:3]


def spread_rows(dest, base, block, heads, head_size, rows):
    reqs, drafts, _ = block.shape
    pad = rows - reqs * drafts
    for c in range(heads):
        cols = pl.ds(c * head_size, head_size)
        for r in range(reqs):
            dest[pl.ds(base + c * rows + r * drafts, drafts), :] = block[r, :, cols]
        if pad:
            dest[pl.ds(base + c * rows + reqs * drafts, pad), :] = jnp.zeros((pad, head_size), dest.dtype)


def write_keys(page_ref, key_ref, page_tokens):
    lane = iota((8, page_tokens), 1)
    for s in range(page_ref.shape[0]):
        key_ref[:, pl.ds(s * page_tokens, page_tokens)] = lane + page_ref[s] * page_tokens


def layout_kernel(device_of, slots, local, rows, heads, drafts, page_tokens,
                  ids_hbm, len_hbm, page_hbm, q_ref,
                  low_ref, high_ref, key_ref, q_out_ref,
                  ids_ref, len_ref, page_ref, start_ref, sems):
    pairs = [(ids_hbm, ids_ref), (len_hbm, len_ref), (page_hbm, page_ref), (q_ref, q_out_ref)]
    copies = [pltpu.make_async_copy(a, b, sems.at[i]) for i, (a, b) in enumerate(pairs)]
    for copy in copies:
        copy.start()
    me = lax.axis_index("blk")
    prompts = len_ref.shape[0]
    shift = SAMPLES.bit_length() - 1
    for copy in copies[:3]:
        copy.wait()

    def place(p, start):
        start_ref[p] = start
        return start + lax.div(len_ref[p] + page_tokens - 1, page_tokens) * page_tokens

    lax.fori_loop(0, prompts, place, jnp.int32(0), unroll=prompts <= 4)
    request = iota((heads * rows, LANES), 0) % rows // drafts

    def one(j, _):
        device = device_of(j, me)
        low = jnp.zeros((heads * rows, LANES), jnp.int32)
        high = low
        for r in range(local):
            prompt = lax.shift_right_logical(ids_ref[device * local + r], shift)
            start = start_ref[prompt]
            low = jnp.where(request == r, start, low)
            high = jnp.where(request == r, start + len_ref[prompt], high)
        place_at = pl.ds(j * heads * rows, heads * rows)
        low_ref[place_at, :] = low
        high_ref[place_at, :] = high
        return 0

    if slots <= 8:
        for j in range(slots):
            one(j, 0)
    else:
        lax.fori_loop(0, slots, one, 0)
    write_keys(page_ref, key_ref, page_tokens)
    for copy in copies[3:]:
        copy.wait()


def flip_kernel(page_tokens, *refs):
    pools = 2 if len(refs) == 6 else 1
    page_refs, pool_refs, key_refs, flip_refs = refs[:pools - 1], refs[pools - 1:2 * pools - 1], refs[2 * pools - 1:-pools], refs[-pools:]
    for page_ref, key_ref in zip(page_refs, key_refs):
        write_keys(page_ref, key_ref, page_tokens)
    for pool_ref, flip_ref in zip(pool_refs, flip_refs):
        pages, tokens, head_pair = pool_ref.shape
        keys = pool_ref[:, :, :head_pair // 2].reshape(pages * tokens, head_pair // 2)
        flip_ref[...] = keys.T


def prefix_kernel(heads, rows, scale, sources, parts_out, first_slot, *refs):
    q_refs, refs = refs[:sources], refs[sources:]
    (low_ref, high_ref), refs = refs[:2], refs[2:]
    both_refs, out_refs, q_rows = refs[:-parts_out - 1], refs[-parts_out - 1:-1], refs[-1]
    count = len(both_refs) // 3
    key_refs, flip_refs, pool_refs = both_refs[:count], both_refs[count:2 * count], both_refs[2 * count:]
    blocks = list(q_refs) if len(q_refs[0].shape) == 3 else [q_refs[0].at[j] for j in range(q_refs[0].shape[0])]
    slots = len(blocks)
    pages, page_tokens, head_pair = pool_refs[0].shape
    head_size = head_pair // 2
    for j, block in enumerate(blocks):
        spread_rows(q_rows, j * heads * rows, block, heads, head_size, rows)
    ranges = pl.ds(first_slot * heads * rows, slots * heads * rows)
    low, high = low_ref[ranges, :], high_ref[ranges, :]
    queries = q_rows[...]
    chunk = CHUNK if pages % CHUNK == 0 else pages
    masked = []
    for key_ref, flip_ref, pool_ref in zip(key_refs, flip_refs, pool_refs):
        for first in range(0, pages, chunk):
            at = first * page_tokens
            logits = jnp.dot(queries, flip_ref[:, at:at + chunk * page_tokens], preferred_element_type=jnp.float32)
            parts = []
            for k in range(0, chunk * page_tokens, LANES):
                key = key_ref[0:1, at + k:at + k + LANES]
                live = (key >= low) & (key < high)
                parts.append(jnp.where(live, logits[:, k:k + LANES] * scale, FLOOR))
            masked.append((pool_ref, first, jnp.concatenate(parts, axis=1)))
    num = den = peak = None
    for pool_ref, first, logits in masked:
        top = rounded_peak(jnp.max(logits, axis=1, keepdims=True))
        if peak is not None:
            top = jnp.maximum(top, peak)
        weights = jnp.exp2(logits - top)
        chunk_den = jnp.sum(weights, axis=1, keepdims=True)
        values = pool_ref[first:first + chunk, :, head_size:].reshape(chunk * page_tokens, head_size)
        chunk_num = jnp.dot(weights.astype(jnp.bfloat16), values, preferred_element_type=jnp.float32)
        if peak is None:
            num, den = chunk_num, chunk_den
        else:
            kept = jnp.exp2(peak - top)
            num, den = num * kept + chunk_num, den * kept + chunk_den
        peak = top
    per = heads * rows
    stats = pack_stats(peak, den)
    outs = list(out_refs) if len(out_refs[0].shape) == 2 else [out_refs[0].at[j] for j in range(slots)]
    for j, out_ref in enumerate(outs):
        out_ref[:, :head_size] = num[j * per:(j + 1) * per].astype(out_ref.dtype)
        out_ref[:, head_size:] = stats[j * per:(j + 1) * per].astype(out_ref.dtype)


def own_kernel(heads, rows, scale, len_ref, q_ref, tail_ref, fresh_ref, weight_ref, out_ref, q_rows, f_rows):
    del weight_ref
    reqs, drafts, _ = q_ref.shape
    tail = tail_ref.shape[1]
    head_size = tail_ref.shape[2] // 2
    spread_rows(q_rows, 0, q_ref, heads, head_size, rows)
    fresh_rows = f_rows.shape[0] // 2
    spread_rows(f_rows, 0, fresh_ref, 2, head_size, fresh_rows)
    queries = q_rows[...]
    contract = (((1,), (1,)), ((), ()))
    logits = lax.dot_general(
        queries, tail_ref[:, :, :head_size].reshape(reqs * tail, head_size),
        contract, preferred_element_type=jnp.float32,
    )
    total = heads * rows
    row = iota((total, tail), 0) % rows
    lane = iota((total, tail), 1)
    parts = []
    for r in range(reqs):
        live = (row // drafts == r) & (lane < len_ref[r])
        parts.append(jnp.where(live, logits[:, r * tail:(r + 1) * tail] * scale, FLOOR))
    fresh = lax.dot_general(
        queries, f_rows[0:fresh_rows, :], contract, preferred_element_type=jnp.float32
    )
    row = iota((total, fresh_rows), 0) % rows
    key = iota((total, fresh_rows), 1)
    live = (row // drafts == key // drafts) & (key % drafts <= row % drafts)
    fresh = jnp.where(live, fresh * scale, FLOOR)
    logits = jnp.concatenate(parts, axis=1)
    peak = jnp.maximum(
        jnp.max(logits, axis=1, keepdims=True), jnp.max(fresh, axis=1, keepdims=True)
    )
    peak = rounded_peak(peak)
    weights = jnp.exp2(logits - peak)
    fresh = jnp.exp2(fresh - peak)
    den = jnp.sum(weights, axis=1, keepdims=True) + jnp.sum(fresh, axis=1, keepdims=True)
    num = jnp.dot(
        weights.astype(jnp.bfloat16), tail_ref[:, :, head_size:].reshape(reqs * tail, head_size),
        preferred_element_type=jnp.float32,
    )
    num = num + jnp.dot(
        fresh.astype(jnp.bfloat16), f_rows[fresh_rows:2 * fresh_rows, :], preferred_element_type=jnp.float32
    )
    out_ref[:, :head_size] = num
    out_ref[:, head_size:] = pack_stats(peak, den)


def summed_parts(blocks, head_size):
    nums = [b[:, :head_size].astype(jnp.float32) for b in blocks]
    stats = [unpack_stats(b[:, head_size:]) for b in blocks]
    peak = functools.reduce(jnp.maximum, [s[0] for s in stats])
    factors = [jnp.exp2(s[0] - peak) for s in stats]
    num = sum(n * f for n, f in zip(nums, factors))
    den = sum(s[1] * f for s, f in zip(stats, factors))
    return num, peak, den


def project(num, den, weight_ref, out_ref, heads, rows):
    reqs, drafts, _ = out_ref.shape
    attention = num / den
    head_size = attention.shape[1]
    value = sum(
        jnp.dot(
            attention[c * rows:(c + 1) * rows, :].astype(jnp.bfloat16), weight_ref[c * head_size:(c + 1) * head_size, :],
            preferred_element_type=jnp.float32,
        )
        for c in range(heads)
    ).astype(out_ref.dtype)
    for r in range(reqs):
        out_ref[r] = value[r * drafts:(r + 1) * drafts, :]


def combine_kernel(heads, rows, head_size, *refs):
    *block_refs, weight_ref, out_ref = refs
    num, _, den = summed_parts([b[...] for b in block_refs], head_size)
    project(num, den, weight_ref, out_ref, heads, rows)


def combine_many_kernel(heads, rows, head_size, own_ref, many_ref, weight_ref, out_ref):
    def one(j, carry):
        num, peak, den = carry
        block = many_ref[j]
        next_peak, next_den = unpack_stats(block[:, head_size:])
        top = jnp.maximum(peak, next_peak)
        old, new = jnp.exp2(peak - top), jnp.exp2(next_peak - top)
        return num * old + block[:, :head_size].astype(jnp.float32) * new, top, den * old + next_den * new

    own = own_ref[...]
    carry = (own[:, :head_size], *unpack_stats(own[:, head_size:]))
    num, _, den = lax.fori_loop(0, many_ref.shape[0], one, carry)
    project(num, den, weight_ref, out_ref, heads, rows)


def final_kernel(*refs):
    *part_refs, hidden_ref, gain_ref, score_ref, out_ref, scores_ref = refs
    reqs, drafts, width = hidden_ref.shape
    mix = gain_ref[...] * score_ref[...]
    lane = iota((1, LANES), 1)
    scores = jnp.zeros((1, LANES), jnp.float32)
    for r in range(reqs):
        total = sum(p[r].astype(jnp.float32) for p in part_refs)
        value = (hidden_ref[r].astype(jnp.float32) + total).astype(out_ref.dtype)
        out_ref[r] = value
        last = value.astype(jnp.float32)[drafts - 1:drafts, :]
        square = jnp.sum(last * last, axis=1, keepdims=True) / width
        score = jnp.sum(last * mix, axis=1, keepdims=True) * lax.rsqrt(square + 1e-06)
        scores = jnp.where(lane == r, score, scores)
    scores_ref[...] = scores[0, :reqs]


def body(sizes, prefix_pool, slot_page, prompt_len, request_ids, tail_len, tail_cache, queries, new_kv, hidden,
         out_weight, norm_gain, score_weight):
    blk, kv = sizes
    pool = prefix_pool[0]
    page_count, page_tokens, head_pair = pool.shape
    head_size = head_pair // 2
    local, drafts, head_width = queries.shape
    heads = head_width // head_size
    rows = local * drafts
    if heads * rows % 8:
        rows = round_up(rows, 16)
    per = heads * rows
    keys = page_count * page_tokens
    width = hidden.shape[2]
    scale = head_size ** (-0.5) * LOG2E
    paired = blk in (2, 4, 8)
    half = blk // 2
    partners = [0] + [j for j in ORDER_A if j < half]
    masks = [0] + [2 * j + 1 for j in partners[1:]]

    def swap(x, axis, size, mask):
        return lax.ppermute(x, axis, [(i, i ^ mask) for i in range(size)])

    def device_of(j, me):
        return me ^ masks[j] if paired else j

    slots = half if paired else blk
    pools = [pool]
    if paired:
        pools.append(swap(pool, "blk", blk, 1))
        far_pages = swap(slot_page, "blk", blk, 1)

    in_hbm = functools.partial(pltpu.with_memory_space_constraint, memory_space=pltpu.HBM)
    low, high, near_keys, near_queries = pl.pallas_call(
        functools.partial(layout_kernel, device_of, slots, local, rows, heads, drafts, page_tokens),
        out_shape=(
            jax.ShapeDtypeStruct((slots * per, LANES), jnp.int32),
            jax.ShapeDtypeStruct((slots * per, LANES), jnp.int32),
            jax.ShapeDtypeStruct((8, keys), jnp.int32),
            jax.ShapeDtypeStruct(queries.shape, queries.dtype),
        ),
        in_specs=[ANY] * 4,
        out_specs=(VMEM,) * 3 + (ANY,),
        scratch_shapes=[
            pltpu.SMEM(request_ids.shape, jnp.int32),
            pltpu.SMEM(prompt_len.shape, jnp.int32),
            pltpu.SMEM(slot_page.shape, jnp.int32),
            pltpu.SMEM(prompt_len.shape, jnp.int32),
            pltpu.SemaphoreType.DMA((4,)),
        ],
        compiler_params=vmem(8),
        cost_estimate=cost(4 * 10**9, 2 * slots * per * LANES * 4),
        name="key_ranges",
    )(*map(in_hbm, (request_ids, prompt_len, slot_page, queries)))
    flipped = pl.pallas_call(
        functools.partial(flip_kernel, page_tokens),
        out_shape=(jax.ShapeDtypeStruct((8, keys), jnp.int32),) * (len(pools) - 1)
        + (jax.ShapeDtypeStruct((head_size, keys), pool.dtype),) * len(pools),
        in_specs=[SMEM] * (len(pools) - 1) + [VMEM] * len(pools),
        out_specs=(VMEM,) * (2 * len(pools) - 1),
        compiler_params=vmem(12),
        cost_estimate=cost(10**9, 4 * pool.size * len(pools)),
        name="flip_keys",
    )(*([far_pages] if paired else []), *pools)
    key_lists, flips = [near_keys, *flipped[:-len(pools)]], flipped[-len(pools):]

    own = pl.pallas_call(
        functools.partial(own_kernel, heads, rows, scale),
        out_shape=jax.ShapeDtypeStruct((per, head_size + LANES), jnp.float32),
        in_specs=[SMEM] + [VMEM] * 4,
        out_specs=VMEM,
        scratch_shapes=[
            pltpu.VMEM((per, head_size), jnp.bfloat16),
            pltpu.VMEM((2 * round_up(local * drafts, 16), head_size), jnp.bfloat16),
        ],
        compiler_params=vmem(8),
        cost_estimate=cost(4 * per * local * tail_cache.shape[2] * head_size, 2 * tail_cache.size),
        name="own_keys",
    )(tail_len, queries, tail_cache[0], new_kv[0], out_weight)

    block_shape = jax.ShapeDtypeStruct((per, head_size + LANES), jnp.bfloat16)
    scratch = [pltpu.VMEM((min(slots, 4) * per, head_size), jnp.bfloat16)]
    price = cost(4 * slots * per * keys * len(pools) * head_size, 2 * pool.size * len(pools))

    def prefix_column(blocks, first_slot):
        count = len(blocks)
        return pl.pallas_call(
            functools.partial(prefix_kernel, heads, rows, scale, count, count, first_slot),
            out_shape=(block_shape,) * count,
            in_specs=[VMEM] * (count + 2 + 3 * len(pools)),
            out_specs=(VMEM,) * count,
            scratch_shapes=[pltpu.VMEM((count * per, head_size), jnp.bfloat16)],
            compiler_params=vmem(24),
            cost_estimate=cost(price.flops // slots * count, price.bytes_accessed),
            name="prefix_keys",
        )(*blocks, low, high, *key_lists, *flips, *pools)

    def prefix_many(block):
        step = min(slots, 4)
        return pl.pallas_call(
            functools.partial(prefix_kernel, heads, rows, scale, 1, 1, 0),
            out_shape=jax.ShapeDtypeStruct((slots,) + block_shape.shape, jnp.bfloat16),
            grid=(slots // step,),
            in_specs=[
                pl.BlockSpec((step, local, drafts, head_width), lambda i: (i, 0, 0, 0)),
                pl.BlockSpec((step * per, LANES), lambda i: (i, 0)),
                pl.BlockSpec((step * per, LANES), lambda i: (i, 0)),
                pl.BlockSpec((8, keys), lambda i: (0, 0)),
                pl.BlockSpec((head_size, keys), lambda i: (0, 0)),
                pl.BlockSpec((page_count, page_tokens, head_pair), lambda i: (0, 0, 0)),
            ],
            out_specs=pl.BlockSpec((step,) + block_shape.shape, lambda i: (i, 0, 0)),
            scratch_shapes=scratch,
            compiler_params=vmem(24),
            cost_estimate=price,
            name="prefix_keys",
        )(block, low, high, *key_lists, *flips, *pools)

    partial_shape = jax.ShapeDtypeStruct((local, drafts, width), jnp.bfloat16)
    if paired:
        column = [near_queries] + [swap(queries, "blk", blk, mask) for mask in masks[1:]]
        sums = [None, *prefix_column(column[1:], 1)] if half > 1 else [None]
        sums[0] = prefix_column(column[:1], 0)[0]
        blocks = [sums[0]] + [
            swap(sums[partners.index(j)], "blk", blk, 2 * j + 1) for j in ORDER_B if j < half
        ]
        share = pl.pallas_call(
            functools.partial(combine_kernel, heads, rows, head_size),
            out_shape=partial_shape,
            in_specs=[VMEM] * (half + 2),
            out_specs=VMEM,
            compiler_params=vmem(12),
            cost_estimate=cost(2 * per * head_size * width, 2 * out_weight.size),
            name="combine_project",
        )(own, *blocks, out_weight)
    else:
        gathered = lax.all_gather(queries, "blk", axis=0)
        blocks = lax.all_to_all(prefix_many(gathered), "blk", 0, 0)
        share = pl.pallas_call(
            functools.partial(combine_many_kernel, heads, rows, head_size),
            out_shape=partial_shape,
            in_specs=[VMEM] * 3,
            out_specs=VMEM,
            compiler_params=vmem(12),
            cost_estimate=cost(2 * per * head_size * width, 2 * out_weight.size),
            name="combine_project",
        )(own, blocks, out_weight)
    if kv in (2, 4):
        shares = [share] + [swap(share, "kv", kv, j) for j in ORDER_C if j < kv]
    else:
        shares = [lax.psum(share, "kv")]
    hidden_out, scores = pl.pallas_call(
        final_kernel,
        out_shape=(
            jax.ShapeDtypeStruct(hidden.shape, hidden.dtype),
            jax.ShapeDtypeStruct((local,), jnp.float32),
        ),
        in_specs=[VMEM] * (len(shares) + 3),
        out_specs=(VMEM, VMEM),
        compiler_params=vmem(8),
        cost_estimate=cost(1, 2 * hidden.size * 6),
        name="residual_scores",
    )(*shares, hidden, norm_gain.reshape(1, width), score_weight.reshape(1, width))
    return hidden_out, scores


def solution(mesh):
    in_specs = (
        P("kv", "blk", None, None),
        P("blk"),
        P(),
        P(),
        P("blk"),
        P("kv", "blk", None, None),
        P("blk", None, "kv"),
        P("kv", "blk", None, None),
        P("blk", None, None),
        P("kv", None),
        P(),
        P(),
    )
    out_specs = (P("blk", None, None), P("blk"))
    sizes = (mesh.shape["blk"], mesh.shape["kv"])
    return jax.shard_map(
        functools.partial(body, sizes), mesh=mesh, in_specs=in_specs, out_specs=out_specs, check_vma=False
    )
```

```python
import functools

import jax
import jax.numpy as jnp
from jax import lax
from jax.experimental import pallas as pl
from jax.experimental.pallas import tpu as pltpu
from jax.sharding import PartitionSpec as P

SAMPLES = 16
CHUNK = 8
ORDER_A = (2, 3, 1)
ORDER_B = (3, 1, 2)
ORDER_C = (1, 2, 3)
LANES = 128
FLOOR = -(2.0**100)
LOG2E = 1.4426950408889634
ANY = pl.BlockSpec(memory_space=pl.ANY)
VMEM = pl.BlockSpec(memory_space=pltpu.VMEM)
SMEM = pl.BlockSpec(memory_space=pltpu.SMEM)


def round_up(value, unit):
    return (value + unit - 1) // unit * unit


def cost(flops, size):
    return pl.CostEstimate(flops=flops, bytes_accessed=size, transcendentals=0)


def vmem(mebibytes):
    return pltpu.CompilerParams(vmem_limit_bytes=mebibytes * 1024 * 1024)


def iota(shape, dim):
    return lax.broadcasted_iota(jnp.int32, shape, dim)


def rounded_peak(peak):
    return peak.astype(jnp.bfloat16).astype(jnp.float32)


def pack_stats(peak, den):
    high = den.astype(jnp.bfloat16).astype(jnp.float32)
    lane = iota((peak.shape[0], LANES), 1)
    stats = jnp.where(lane == 0, peak, jnp.where(lane == 1, high, den - high))
    return jnp.where(lane < 3, stats, 0.0)


def unpack_stats(stats):
    stats = stats.astype(jnp.float32)
    return stats[:, 0:1], stats[:, 1:2] + stats[:, 2:3]


def spread_rows(dest, base, block, heads, head_size, rows):
    reqs, drafts, _ = block.shape
    pad = rows - reqs * drafts
    for c in range(heads):
        cols = pl.ds(c * head_size, head_size)
        for r in range(reqs):
            dest[pl.ds(base + c * rows + r * drafts, drafts), :] = block[r, :, cols]
        if pad:
            dest[pl.ds(base + c * rows + reqs * drafts, pad), :] = jnp.zeros((pad, head_size), dest.dtype)


def write_keys(page_ref, key_ref, page_tokens):
    lane = iota((8, page_tokens), 1)
    for s in range(page_ref.shape[0]):
        key_ref[:, pl.ds(s * page_tokens, page_tokens)] = lane + page_ref[s] * page_tokens


def layout_kernel(device_of, slots, local, rows, heads, drafts, page_tokens,
                  ids_hbm, len_hbm, page_hbm, q_ref,
                  low_ref, high_ref, key_ref, q_out_ref,
                  ids_ref, len_ref, page_ref, start_ref, sems):
    pairs = [(ids_hbm, ids_ref), (len_hbm, len_ref), (page_hbm, page_ref), (q_ref, q_out_ref)]
    copies = [pltpu.make_async_copy(a, b, sems.at[i]) for i, (a, b) in enumerate(pairs)]
    for copy in copies:
        copy.start()
    me = lax.axis_index("blk")
    prompts = len_ref.shape[0]
    shift = SAMPLES.bit_length() - 1
    for copy in copies[:3]:
        copy.wait()

    def place(p, start):
        start_ref[p] = start
        return start + lax.div(len_ref[p] + page_tokens - 1, page_tokens) * page_tokens

    lax.fori_loop(0, prompts, place, jnp.int32(0), unroll=prompts <= 4)
    request = iota((heads * rows, LANES), 0) % rows // drafts

    def one(j, _):
        device = device_of(j, me)
        low = jnp.zeros((heads * rows, LANES), jnp.int32)
        high = low
        for r in range(local):
            prompt = lax.shift_right_logical(ids_ref[device * local + r], shift)
            start = start_ref[prompt]
            low = jnp.where(request == r, start, low)
            high = jnp.where(request == r, start + len_ref[prompt], high)
        place_at = pl.ds(j * heads * rows, heads * rows)
        low_ref[place_at, :] = low
        high_ref[place_at, :] = high
        return 0

    if slots <= 8:
        for j in range(slots):
            one(j, 0)
    else:
        lax.fori_loop(0, slots, one, 0)
    write_keys(page_ref, key_ref, page_tokens)
    for copy in copies[3:]:
        copy.wait()


def flip_kernel(page_tokens, *refs):
    pools = 2 if len(refs) == 6 else 1
    page_refs, pool_refs, key_refs, flip_refs = refs[:pools - 1], refs[pools - 1:2 * pools - 1], refs[2 * pools - 1:-pools], refs[-pools:]
    for page_ref, key_ref in zip(page_refs, key_refs):
        write_keys(page_ref, key_ref, page_tokens)
    for pool_ref, flip_ref in zip(pool_refs, flip_refs):
        pages, tokens, head_pair = pool_ref.shape
        keys = pool_ref[:, :, :head_pair // 2].reshape(pages * tokens, head_pair // 2)
        flip_ref[...] = keys.T


def prefix_kernel(heads, rows, scale, sources, parts_out, first_slot, *refs):
    q_refs, refs = refs[:sources], refs[sources:]
    (low_ref, high_ref), refs = refs[:2], refs[2:]
    both_refs, out_refs, q_rows = refs[:-parts_out - 1], refs[-parts_out - 1:-1], refs[-1]
    count = len(both_refs) // 3
    key_refs, flip_refs, pool_refs = both_refs[:count], both_refs[count:2 * count], both_refs[2 * count:]
    blocks = list(q_refs) if len(q_refs[0].shape) == 3 else [q_refs[0].at[j] for j in range(q_refs[0].shape[0])]
    slots = len(blocks)
    pages, page_tokens, head_pair = pool_refs[0].shape
    head_size = head_pair // 2
    for j, block in enumerate(blocks):
        spread_rows(q_rows, j * heads * rows, block, heads, head_size, rows)
    ranges = pl.ds(first_slot * heads * rows, slots * heads * rows)
    low, high = low_ref[ranges, :], high_ref[ranges, :]
    queries = q_rows[...]
    chunk = CHUNK if pages % CHUNK == 0 else pages
    masked = []
    for key_ref, flip_ref, pool_ref in zip(key_refs, flip_refs, pool_refs):
        for first in range(0, pages, chunk):
            at = first * page_tokens
            logits = jnp.dot(queries, flip_ref[:, at:at + chunk * page_tokens], preferred_element_type=jnp.float32)
            parts = []
            for k in range(0, chunk * page_tokens, LANES):
                key = key_ref[0:1, at + k:at + k + LANES]
                live = (key >= low) & (key < high)
                parts.append(jnp.where(live, logits[:, k:k + LANES] * scale, FLOOR))
            masked.append((pool_ref, first, jnp.concatenate(parts, axis=1)))
    num = den = peak = None
    for pool_ref, first, logits in masked:
        top = rounded_peak(jnp.max(logits, axis=1, keepdims=True))
        if peak is not None:
            top = jnp.maximum(top, peak)
        weights = jnp.exp2(logits - top)
        chunk_den = jnp.sum(weights, axis=1, keepdims=True)
        values = pool_ref[first:first + chunk, :, head_size:].reshape(chunk * page_tokens, head_size)
        chunk_num = jnp.dot(weights.astype(jnp.bfloat16), values, preferred_element_type=jnp.float32)
        if peak is None:
            num, den = chunk_num, chunk_den
        else:
            kept = jnp.exp2(peak - top)
            num, den = num * kept + chunk_num, den * kept + chunk_den
        peak = top
    per = heads * rows
    stats = pack_stats(peak, den)
    outs = list(out_refs) if len(out_refs[0].shape) == 2 else [out_refs[0].at[j] for j in range(slots)]
    for j, out_ref in enumerate(outs):
        out_ref[:, :head_size] = num[j * per:(j + 1) * per].astype(out_ref.dtype)
        out_ref[:, head_size:] = stats[j * per:(j + 1) * per].astype(out_ref.dtype)


def own_kernel(heads, rows, scale, len_ref, q_ref, tail_ref, fresh_ref, weight_ref, out_ref, q_rows, f_rows):
    del weight_ref
    reqs, drafts, _ = q_ref.shape
    tail = tail_ref.shape[1]
    head_size = tail_ref.shape[2] // 2
    spread_rows(q_rows, 0, q_ref, heads, head_size, rows)
    fresh_rows = f_rows.shape[0] // 2
    spread_rows(f_rows, 0, fresh_ref, 2, head_size, fresh_rows)
    queries = q_rows[...]
    contract = (((1,), (1,)), ((), ()))
    logits = lax.dot_general(
        queries, tail_ref[:, :, :head_size].reshape(reqs * tail, head_size),
        contract, preferred_element_type=jnp.float32,
    )
    total = heads * rows
    row = iota((total, tail), 0) % rows
    lane = iota((total, tail), 1)
    parts = []
    for r in range(reqs):
        live = (row // drafts == r) & (lane < len_ref[r])
        parts.append(jnp.where(live, logits[:, r * tail:(r + 1) * tail] * scale, FLOOR))
    fresh = lax.dot_general(
        queries, f_rows[0:fresh_rows, :], contract, preferred_element_type=jnp.float32
    )
    row = iota((total, fresh_rows), 0) % rows
    key = iota((total, fresh_rows), 1)
    live = (row // drafts == key // drafts) & (key % drafts <= row % drafts)
    fresh = jnp.where(live, fresh * scale, FLOOR)
    logits = jnp.concatenate(parts, axis=1)
    peak = jnp.maximum(
        jnp.max(logits, axis=1, keepdims=True), jnp.max(fresh, axis=1, keepdims=True)
    )
    peak = rounded_peak(peak)
    weights = jnp.exp2(logits - peak)
    fresh = jnp.exp2(fresh - peak)
    den = jnp.sum(weights, axis=1, keepdims=True) + jnp.sum(fresh, axis=1, keepdims=True)
    num = jnp.dot(
        weights.astype(jnp.bfloat16), tail_ref[:, :, head_size:].reshape(reqs * tail, head_size),
        preferred_element_type=jnp.float32,
    )
    num = num + jnp.dot(
        fresh.astype(jnp.bfloat16), f_rows[fresh_rows:2 * fresh_rows, :], preferred_element_type=jnp.float32
    )
    out_ref[:, :head_size] = num
    out_ref[:, head_size:] = pack_stats(peak, den)


def summed_parts(blocks, head_size):
    nums = [b[:, :head_size].astype(jnp.float32) for b in blocks]
    stats = [unpack_stats(b[:, head_size:]) for b in blocks]
    peak = functools.reduce(jnp.maximum, [s[0] for s in stats])
    factors = [jnp.exp2(s[0] - peak) for s in stats]
    num = sum(n * f for n, f in zip(nums, factors))
    den = sum(s[1] * f for s, f in zip(stats, factors))
    return num, peak, den


def project(num, den, weight_ref, out_ref, heads, rows):
    reqs, drafts, _ = out_ref.shape
    attention = num / den
    head_size = attention.shape[1]
    value = sum(
        jnp.dot(
            attention[c * rows:(c + 1) * rows, :].astype(jnp.bfloat16), weight_ref[c * head_size:(c + 1) * head_size, :],
            preferred_element_type=jnp.float32,
        )
        for c in range(heads)
    ).astype(out_ref.dtype)
    for r in range(reqs):
        out_ref[r] = value[r * drafts:(r + 1) * drafts, :]


def combine_kernel(heads, rows, head_size, *refs):
    *block_refs, weight_ref, out_ref = refs
    num, _, den = summed_parts([b[...] for b in block_refs], head_size)
    project(num, den, weight_ref, out_ref, heads, rows)


def combine_many_kernel(heads, rows, head_size, own_ref, many_ref, weight_ref, out_ref):
    def one(j, carry):
        num, peak, den = carry
        block = many_ref[j]
        next_peak, next_den = unpack_stats(block[:, head_size:])
        top = jnp.maximum(peak, next_peak)
        old, new = jnp.exp2(peak - top), jnp.exp2(next_peak - top)
        return num * old + block[:, :head_size].astype(jnp.float32) * new, top, den * old + next_den * new

    own = own_ref[...]
    carry = (own[:, :head_size], *unpack_stats(own[:, head_size:]))
    num, _, den = lax.fori_loop(0, many_ref.shape[0], one, carry)
    project(num, den, weight_ref, out_ref, heads, rows)


def final_kernel(*refs):
    *part_refs, hidden_ref, gain_ref, score_ref, out_ref, scores_ref = refs
    reqs, drafts, width = hidden_ref.shape
    mix = gain_ref[...] * score_ref[...]
    lane = iota((1, LANES), 1)
    scores = jnp.zeros((1, LANES), jnp.float32)
    for r in range(reqs):
        total = sum(p[r].astype(jnp.float32) for p in part_refs)
        value = (hidden_ref[r].astype(jnp.float32) + total).astype(out_ref.dtype)
        out_ref[r] = value
        last = value.astype(jnp.float32)[drafts - 1:drafts, :]
        square = jnp.sum(last * last, axis=1, keepdims=True) / width
        score = jnp.sum(last * mix, axis=1, keepdims=True) * lax.rsqrt(square + 1e-06)
        scores = jnp.where(lane == r, score, scores)
    scores_ref[...] = scores[0, :reqs]


def body(sizes, prefix_pool, slot_page, prompt_len, request_ids, tail_len, tail_cache, queries, new_kv, hidden,
         out_weight, norm_gain, score_weight):
    blk, kv = sizes
    pool = prefix_pool[0]
    page_count, page_tokens, head_pair = pool.shape
    head_size = head_pair // 2
    local, drafts, head_width = queries.shape
    heads = head_width // head_size
    rows = local * drafts
    if heads * rows % 8:
        rows = round_up(rows, 16)
    per = heads * rows
    keys = page_count * page_tokens
    width = hidden.shape[2]
    scale = head_size ** (-0.5) * LOG2E
    paired = blk in (2, 4, 8)
    half = blk // 2
    partners = [0] + [j for j in ORDER_A if j < half]
    masks = [0] + [2 * j + 1 for j in partners[1:]]

    def swap(x, axis, size, mask):
        return lax.ppermute(x, axis, [(i, i ^ mask) for i in range(size)])

    def device_of(j, me):
        return me ^ masks[j] if paired else j

    slots = half if paired else blk
    pools = [pool]
    if paired:
        pools.append(swap(pool, "blk", blk, 1))
        far_pages = swap(slot_page, "blk", blk, 1)

    in_hbm = functools.partial(pltpu.with_memory_space_constraint, memory_space=pltpu.HBM)
    low, high, near_keys, near_queries = pl.pallas_call(
        functools.partial(layout_kernel, device_of, slots, local, rows, heads, drafts, page_tokens),
        out_shape=(
            jax.ShapeDtypeStruct((slots * per, LANES), jnp.int32),
            jax.ShapeDtypeStruct((slots * per, LANES), jnp.int32),
            jax.ShapeDtypeStruct((8, keys), jnp.int32),
            jax.ShapeDtypeStruct(queries.shape, queries.dtype),
        ),
        in_specs=[ANY] * 4,
        out_specs=(VMEM,) * 3 + (ANY,),
        scratch_shapes=[
            pltpu.SMEM(request_ids.shape, jnp.int32),
            pltpu.SMEM(prompt_len.shape, jnp.int32),
            pltpu.SMEM(slot_page.shape, jnp.int32),
            pltpu.SMEM(prompt_len.shape, jnp.int32),
            pltpu.SemaphoreType.DMA((4,)),
        ],
        compiler_params=vmem(8),
        cost_estimate=cost(4 * 10**9, 2 * slots * per * LANES * 4),
        name="key_ranges",
    )(*map(in_hbm, (request_ids, prompt_len, slot_page, queries)))
    flipped = pl.pallas_call(
        functools.partial(flip_kernel, page_tokens),
        out_shape=(jax.ShapeDtypeStruct((8, keys), jnp.int32),) * (len(pools) - 1)
        + (jax.ShapeDtypeStruct((head_size, keys), pool.dtype),) * len(pools),
        in_specs=[SMEM] * (len(pools) - 1) + [VMEM] * len(pools),
        out_specs=(VMEM,) * (2 * len(pools) - 1),
        compiler_params=vmem(12),
        cost_estimate=cost(10**9, 4 * pool.size * len(pools)),
        name="flip_keys",
    )(*([far_pages] if paired else []), *pools)
    key_lists, flips = [near_keys, *flipped[:-len(pools)]], flipped[-len(pools):]

    own = pl.pallas_call(
        functools.partial(own_kernel, heads, rows, scale),
        out_shape=jax.ShapeDtypeStruct((per, head_size + LANES), jnp.float32),
        in_specs=[SMEM] + [VMEM] * 4,
        out_specs=VMEM,
        scratch_shapes=[
            pltpu.VMEM((per, head_size), jnp.bfloat16),
            pltpu.VMEM((2 * round_up(local * drafts, 16), head_size), jnp.bfloat16),
        ],
        compiler_params=vmem(8),
        cost_estimate=cost(4 * per * local * tail_cache.shape[2] * head_size, 2 * tail_cache.size),
        name="own_keys",
    )(tail_len, queries, tail_cache[0], new_kv[0], out_weight)

    block_shape = jax.ShapeDtypeStruct((per, head_size + LANES), jnp.bfloat16)
    scratch = [pltpu.VMEM((min(slots, 4) * per, head_size), jnp.bfloat16)]
    price = cost(4 * slots * per * keys * len(pools) * head_size, 2 * pool.size * len(pools))

    def prefix_column(blocks, first_slot):
        count = len(blocks)
        return pl.pallas_call(
            functools.partial(prefix_kernel, heads, rows, scale, count, count, first_slot),
            out_shape=(block_shape,) * count,
            in_specs=[VMEM] * (count + 2 + 3 * len(pools)),
            out_specs=(VMEM,) * count,
            scratch_shapes=[pltpu.VMEM((count * per, head_size), jnp.bfloat16)],
            compiler_params=vmem(24),
            cost_estimate=cost(price.flops // slots * count, price.bytes_accessed),
            name="prefix_keys",
        )(*blocks, low, high, *key_lists, *flips, *pools)

    def prefix_many(block):
        step = min(slots, 4)
        return pl.pallas_call(
            functools.partial(prefix_kernel, heads, rows, scale, 1, 1, 0),
            out_shape=jax.ShapeDtypeStruct((slots,) + block_shape.shape, jnp.bfloat16),
            grid=(slots // step,),
            in_specs=[
                pl.BlockSpec((step, local, drafts, head_width), lambda i: (i, 0, 0, 0)),
                pl.BlockSpec((step * per, LANES), lambda i: (i, 0)),
                pl.BlockSpec((step * per, LANES), lambda i: (i, 0)),
                pl.BlockSpec((8, keys), lambda i: (0, 0)),
                pl.BlockSpec((head_size, keys), lambda i: (0, 0)),
                pl.BlockSpec((page_count, page_tokens, head_pair), lambda i: (0, 0, 0)),
            ],
            out_specs=pl.BlockSpec((step,) + block_shape.shape, lambda i: (i, 0, 0)),
            scratch_shapes=scratch,
            compiler_params=vmem(24),
            cost_estimate=price,
            name="prefix_keys",
        )(block, low, high, *key_lists, *flips, *pools)

    partial_shape = jax.ShapeDtypeStruct((local, drafts, width), jnp.bfloat16)
    if paired:
        column = [near_queries] + [swap(queries, "blk", blk, mask) for mask in masks[1:]]
        sums = [None, *prefix_column(column[1:], 1)] if half > 1 else [None]
        sums[0] = prefix_column(column[:1], 0)[0]
        blocks = [sums[0]] + [
            swap(sums[partners.index(j)], "blk", blk, 2 * j + 1) for j in ORDER_B if j < half
        ]
        share = pl.pallas_call(
            functools.partial(combine_kernel, heads, rows, head_size),
            out_shape=partial_shape,
            in_specs=[VMEM] * (half + 2),
            out_specs=VMEM,
            compiler_params=vmem(12),
            cost_estimate=cost(2 * per * head_size * width, 2 * out_weight.size),
            name="combine_project",
        )(own, *blocks, out_weight)
    else:
        gathered = lax.all_gather(queries, "blk", axis=0)
        blocks = lax.all_to_all(prefix_many(gathered), "blk", 0, 0)
        share = pl.pallas_call(
            functools.partial(combine_many_kernel, heads, rows, head_size),
            out_shape=partial_shape,
            in_specs=[VMEM] * 3,
            out_specs=VMEM,
            compiler_params=vmem(12),
            cost_estimate=cost(2 * per * head_size * width, 2 * out_weight.size),
            name="combine_project",
        )(own, blocks, out_weight)
    out_type = hidden.dtype
    if kv in (2, 4):
        arrived = {j: swap(share, "kv", kv, j) for j in ORDER_C if j < kv}
        last = arrived.pop(2 if kv == 4 else 1)
        early = hidden.astype(jnp.float32) + share.astype(jnp.float32)
        for value in arrived.values():
            early = early + value.astype(jnp.float32)
        hidden, shares = early, [last]
    else:
        shares = [lax.psum(share, "kv")]
    hidden_out, scores = pl.pallas_call(
        final_kernel,
        out_shape=(
            jax.ShapeDtypeStruct(hidden.shape, out_type),
            jax.ShapeDtypeStruct((local,), jnp.float32),
        ),
        in_specs=[VMEM] * (len(shares) + 3),
        out_specs=(VMEM, VMEM),
        compiler_params=vmem(8),
        cost_estimate=cost(1, 2 * hidden.size * 6),
        name="residual_scores",
    )(*shares, hidden, norm_gain.reshape(1, width), score_weight.reshape(1, width))
    return hidden_out, scores


def solution(mesh):
    in_specs = (
        P("kv", "blk", None, None),
        P("blk"),
        P(),
        P(),
        P("blk"),
        P("kv", "blk", None, None),
        P("blk", None, "kv"),
        P("kv", "blk", None, None),
        P("blk", None, None),
        P("kv", None),
        P(),
        P(),
    )
    out_specs = (P("blk", None, None), P("blk"))
    sizes = (mesh.shape["blk"], mesh.shape["kv"])
    return jax.shard_map(
        functools.partial(body, sizes), mesh=mesh, in_specs=in_specs, out_specs=out_specs, check_vma=False
    )
```

```python
import functools

import jax
import jax.numpy as jnp
from jax import lax
from jax.experimental import pallas as pl
from jax.experimental.pallas import tpu as pltpu
from jax.sharding import PartitionSpec as P

SAMPLES = 16
CHUNK = 8
ORDER_A = (2, 3, 1)
ORDER_B = (3, 1, 2)
ORDER_C = (1, 2, 3)
LANES = 128
FLOOR = -(2.0**100)
LOG2E = 1.4426950408889634
ANY = pl.BlockSpec(memory_space=pl.ANY)
VMEM = pl.BlockSpec(memory_space=pltpu.VMEM)
SMEM = pl.BlockSpec(memory_space=pltpu.SMEM)


def round_up(value, unit):
    return (value + unit - 1) // unit * unit


def cost(flops, size):
    return pl.CostEstimate(flops=flops, bytes_accessed=size, transcendentals=0)


def vmem(mebibytes):
    return pltpu.CompilerParams(vmem_limit_bytes=mebibytes * 1024 * 1024)


def iota(shape, dim):
    return lax.broadcasted_iota(jnp.int32, shape, dim)


def rounded_peak(peak):
    return peak.astype(jnp.bfloat16).astype(jnp.float32)


def pack_stats(peak, den):
    high = den.astype(jnp.bfloat16).astype(jnp.float32)
    lane = iota((peak.shape[0], LANES), 1)
    stats = jnp.where(lane == 0, peak, jnp.where(lane == 1, high, den - high))
    return jnp.where(lane < 3, stats, 0.0)


def unpack_stats(stats):
    stats = stats.astype(jnp.float32)
    return stats[:, 0:1], stats[:, 1:2] + stats[:, 2:3]


def spread_rows(dest, base, block, heads, head_size, rows):
    reqs, drafts, _ = block.shape
    pad = rows - reqs * drafts
    for c in range(heads):
        cols = pl.ds(c * head_size, head_size)
        for r in range(reqs):
            dest[pl.ds(base + c * rows + r * drafts, drafts), :] = block[r, :, cols]
        if pad:
            dest[pl.ds(base + c * rows + reqs * drafts, pad), :] = jnp.zeros((pad, head_size), dest.dtype)


def write_keys(page_ref, key_ref, page_tokens):
    lane = iota((8, page_tokens), 1)
    for s in range(page_ref.shape[0]):
        key_ref[:, pl.ds(s * page_tokens, page_tokens)] = lane + page_ref[s] * page_tokens


def layout_kernel(device_of, slots, local, rows, heads, drafts, page_tokens,
                  ids_hbm, len_hbm, page_hbm, q_ref,
                  low_ref, high_ref, key_ref, q_out_ref,
                  ids_ref, len_ref, page_ref, start_ref, sems):
    pairs = [(ids_hbm, ids_ref), (len_hbm, len_ref), (page_hbm, page_ref), (q_ref, q_out_ref)]
    copies = [pltpu.make_async_copy(a, b, sems.at[i]) for i, (a, b) in enumerate(pairs)]
    for copy in copies:
        copy.start()
    me = lax.axis_index("blk")
    prompts = len_ref.shape[0]
    shift = SAMPLES.bit_length() - 1
    for copy in copies[:3]:
        copy.wait()

    def place(p, start):
        start_ref[p] = start
        return start + lax.div(len_ref[p] + page_tokens - 1, page_tokens) * page_tokens

    lax.fori_loop(0, prompts, place, jnp.int32(0), unroll=prompts <= 4)
    request = iota((heads * rows, LANES), 0) % rows // drafts

    def one(j, _):
        device = device_of(j, me)
        low = jnp.zeros((heads * rows, LANES), jnp.int32)
        high = low
        for r in range(local):
            prompt = lax.shift_right_logical(ids_ref[device * local + r], shift)
            start = start_ref[prompt]
            low = jnp.where(request == r, start, low)
            high = jnp.where(request == r, start + len_ref[prompt], high)
        place_at = pl.ds(j * heads * rows, heads * rows)
        low_ref[place_at, :] = low
        high_ref[place_at, :] = high
        return 0

    if slots <= 8:
        for j in range(slots):
            one(j, 0)
    else:
        lax.fori_loop(0, slots, one, 0)
    write_keys(page_ref, key_ref, page_tokens)
    for copy in copies[3:]:
        copy.wait()


def flip_kernel(page_tokens, *refs):
    pools = 2 if len(refs) == 6 else 1
    page_refs, pool_refs, key_refs, flip_refs = refs[:pools - 1], refs[pools - 1:2 * pools - 1], refs[2 * pools - 1:-pools], refs[-pools:]
    for page_ref, key_ref in zip(page_refs, key_refs):
        write_keys(page_ref, key_ref, page_tokens)
    for pool_ref, flip_ref in zip(pool_refs, flip_refs):
        pages, tokens, head_pair = pool_ref.shape
        keys = pool_ref[:, :, :head_pair // 2].reshape(pages * tokens, head_pair // 2)
        flip_ref[...] = keys.T


def prefix_kernel(heads, rows, scale, sources, parts_out, first_slot, *refs):
    q_refs, refs = refs[:sources], refs[sources:]
    (low_ref, high_ref), refs = refs[:2], refs[2:]
    both_refs, out_refs, q_rows = refs[:-parts_out - 1], refs[-parts_out - 1:-1], refs[-1]
    count = len(both_refs) // 3
    key_refs, flip_refs, pool_refs = both_refs[:count], both_refs[count:2 * count], both_refs[2 * count:]
    blocks = list(q_refs) if len(q_refs[0].shape) == 3 else [q_refs[0].at[j] for j in range(q_refs[0].shape[0])]
    slots = len(blocks)
    pages, page_tokens, head_pair = pool_refs[0].shape
    head_size = head_pair // 2
    for j, block in enumerate(blocks):
        spread_rows(q_rows, j * heads * rows, block, heads, head_size, rows)
    ranges = pl.ds(first_slot * heads * rows, slots * heads * rows)
    low, high = low_ref[ranges, :], high_ref[ranges, :]
    span = (high - low).astype(jnp.uint32)
    queries = q_rows[...]
    chunk = CHUNK if pages % CHUNK == 0 else pages
    masked = []
    for key_ref, flip_ref, pool_ref in zip(key_refs, flip_refs, pool_refs):
        for first in range(0, pages, chunk):
            at = first * page_tokens
            logits = jnp.dot(queries, flip_ref[:, at:at + chunk * page_tokens], preferred_element_type=jnp.float32)
            parts = []
            for k in range(0, chunk * page_tokens, LANES):
                key = key_ref[0:1, at + k:at + k + LANES]
                live = (key - low).astype(jnp.uint32) < span
                parts.append(jnp.where(live, logits[:, k:k + LANES] * scale, FLOOR))
            masked.append((pool_ref, first, jnp.concatenate(parts, axis=1)))
    num = den = peak = None
    for pool_ref, first, logits in masked:
        top = rounded_peak(jnp.max(logits, axis=1, keepdims=True))
        if peak is not None:
            top = jnp.maximum(top, peak)
        weights = jnp.exp2(logits - top)
        chunk_den = jnp.sum(weights, axis=1, keepdims=True)
        values = pool_ref[first:first + chunk, :, head_size:].reshape(chunk * page_tokens, head_size)
        chunk_num = jnp.dot(weights.astype(jnp.bfloat16), values, preferred_element_type=jnp.float32)
        if peak is None:
            num, den = chunk_num, chunk_den
        else:
            kept = jnp.exp2(peak - top)
            num, den = num * kept + chunk_num, den * kept + chunk_den
        peak = top
    per = heads * rows
    stats = pack_stats(peak, den)
    outs = list(out_refs) if len(out_refs[0].shape) == 2 else [out_refs[0].at[j] for j in range(slots)]
    for j, out_ref in enumerate(outs):
        out_ref[:, :head_size] = num[j * per:(j + 1) * per].astype(out_ref.dtype)
        out_ref[:, head_size:] = stats[j * per:(j + 1) * per].astype(out_ref.dtype)


def own_kernel(heads, rows, scale, len_ref, q_ref, tail_ref, fresh_ref, weight_ref, out_ref, q_rows, f_rows):
    del weight_ref
    reqs, drafts, _ = q_ref.shape
    tail = tail_ref.shape[1]
    head_size = tail_ref.shape[2] // 2
    spread_rows(q_rows, 0, q_ref, heads, head_size, rows)
    fresh_rows = f_rows.shape[0] // 2
    spread_rows(f_rows, 0, fresh_ref, 2, head_size, fresh_rows)
    queries = q_rows[...]
    contract = (((1,), (1,)), ((), ()))
    logits = lax.dot_general(
        queries, tail_ref[:, :, :head_size].reshape(reqs * tail, head_size),
        contract, preferred_element_type=jnp.float32,
    )
    total = heads * rows
    row = iota((total, tail), 0) % rows
    lane = iota((total, tail), 1)
    parts = []
    for r in range(reqs):
        live = (row // drafts == r) & (lane < len_ref[r])
        parts.append(jnp.where(live, logits[:, r * tail:(r + 1) * tail] * scale, FLOOR))
    fresh = lax.dot_general(
        queries, f_rows[0:fresh_rows, :], contract, preferred_element_type=jnp.float32
    )
    row = iota((total, fresh_rows), 0) % rows
    key = iota((total, fresh_rows), 1)
    live = (row // drafts == key // drafts) & (key % drafts <= row % drafts)
    fresh = jnp.where(live, fresh * scale, FLOOR)
    logits = jnp.concatenate(parts, axis=1)
    peak = jnp.maximum(
        jnp.max(logits, axis=1, keepdims=True), jnp.max(fresh, axis=1, keepdims=True)
    )
    peak = rounded_peak(peak)
    weights = jnp.exp2(logits - peak)
    fresh = jnp.exp2(fresh - peak)
    den = jnp.sum(weights, axis=1, keepdims=True) + jnp.sum(fresh, axis=1, keepdims=True)
    num = jnp.dot(
        weights.astype(jnp.bfloat16), tail_ref[:, :, head_size:].reshape(reqs * tail, head_size),
        preferred_element_type=jnp.float32,
    )
    num = num + jnp.dot(
        fresh.astype(jnp.bfloat16), f_rows[fresh_rows:2 * fresh_rows, :], preferred_element_type=jnp.float32
    )
    out_ref[:, :head_size] = num
    out_ref[:, head_size:] = pack_stats(peak, den)


def summed_parts(blocks, head_size):
    nums = [b[:, :head_size].astype(jnp.float32) for b in blocks]
    stats = [unpack_stats(b[:, head_size:]) for b in blocks]
    peak = functools.reduce(jnp.maximum, [s[0] for s in stats])
    factors = [jnp.exp2(s[0] - peak) for s in stats]
    num = sum(n * f for n, f in zip(nums, factors))
    den = sum(s[1] * f for s, f in zip(stats, factors))
    return num, peak, den


def project(num, den, weight_ref, out_ref, heads, rows):
    reqs, drafts, _ = out_ref.shape
    attention = num / den
    head_size = attention.shape[1]
    value = sum(
        jnp.dot(
            attention[c * rows:(c + 1) * rows, :].astype(jnp.bfloat16), weight_ref[c * head_size:(c + 1) * head_size, :],
            preferred_element_type=jnp.float32,
        )
        for c in range(heads)
    ).astype(out_ref.dtype)
    for r in range(reqs):
        out_ref[r] = value[r * drafts:(r + 1) * drafts, :]


def combine_kernel(heads, rows, head_size, *refs):
    *block_refs, weight_ref, out_ref = refs
    num, _, den = summed_parts([b[...] for b in block_refs], head_size)
    project(num, den, weight_ref, out_ref, heads, rows)


def combine_many_kernel(heads, rows, head_size, own_ref, many_ref, weight_ref, out_ref):
    def one(j, carry):
        num, peak, den = carry
        block = many_ref[j]
        next_peak, next_den = unpack_stats(block[:, head_size:])
        top = jnp.maximum(peak, next_peak)
        old, new = jnp.exp2(peak - top), jnp.exp2(next_peak - top)
        return num * old + block[:, :head_size].astype(jnp.float32) * new, top, den * old + next_den * new

    own = own_ref[...]
    carry = (own[:, :head_size], *unpack_stats(own[:, head_size:]))
    num, _, den = lax.fori_loop(0, many_ref.shape[0], one, carry)
    project(num, den, weight_ref, out_ref, heads, rows)


def final_kernel(*refs):
    *part_refs, hidden_ref, gain_ref, score_ref, out_ref, scores_ref = refs
    reqs, drafts, width = hidden_ref.shape
    mix = gain_ref[...] * score_ref[...]
    lane = iota((1, LANES), 1)
    scores = jnp.zeros((1, LANES), jnp.float32)
    for r in range(reqs):
        total = sum(p[r].astype(jnp.float32) for p in part_refs)
        value = (hidden_ref[r].astype(jnp.float32) + total).astype(out_ref.dtype)
        out_ref[r] = value
        last = value.astype(jnp.float32)[drafts - 1:drafts, :]
        square = jnp.sum(last * last, axis=1, keepdims=True) / width
        score = jnp.sum(last * mix, axis=1, keepdims=True) * lax.rsqrt(square + 1e-06)
        scores = jnp.where(lane == r, score, scores)
    scores_ref[...] = scores[0, :reqs]


def body(sizes, prefix_pool, slot_page, prompt_len, request_ids, tail_len, tail_cache, queries, new_kv, hidden,
         out_weight, norm_gain, score_weight):
    blk, kv = sizes
    pool = prefix_pool[0]
    page_count, page_tokens, head_pair = pool.shape
    head_size = head_pair // 2
    local, drafts, head_width = queries.shape
    heads = head_width // head_size
    rows = local * drafts
    if heads * rows % 8:
        rows = round_up(rows, 16)
    per = heads * rows
    keys = page_count * page_tokens
    width = hidden.shape[2]
    scale = head_size ** (-0.5) * LOG2E
    paired = blk in (2, 4, 8)
    half = blk // 2
    partners = [0] + [j for j in ORDER_A if j < half]
    masks = [0] + [2 * j + 1 for j in partners[1:]]

    def swap(x, axis, size, mask):
        return lax.ppermute(x, axis, [(i, i ^ mask) for i in range(size)])

    def device_of(j, me):
        return me ^ masks[j] if paired else j

    slots = half if paired else blk
    pools = [pool]
    if paired:
        pools.append(swap(pool, "blk", blk, 1))
        far_pages = swap(slot_page, "blk", blk, 1)

    in_hbm = functools.partial(pltpu.with_memory_space_constraint, memory_space=pltpu.HBM)
    low, high, near_keys, near_queries = pl.pallas_call(
        functools.partial(layout_kernel, device_of, slots, local, rows, heads, drafts, page_tokens),
        out_shape=(
            jax.ShapeDtypeStruct((slots * per, LANES), jnp.int32),
            jax.ShapeDtypeStruct((slots * per, LANES), jnp.int32),
            jax.ShapeDtypeStruct((8, keys), jnp.int32),
            jax.ShapeDtypeStruct(queries.shape, queries.dtype),
        ),
        in_specs=[ANY] * 4,
        out_specs=(VMEM,) * 3 + (ANY,),
        scratch_shapes=[
            pltpu.SMEM(request_ids.shape, jnp.int32),
            pltpu.SMEM(prompt_len.shape, jnp.int32),
            pltpu.SMEM(slot_page.shape, jnp.int32),
            pltpu.SMEM(prompt_len.shape, jnp.int32),
            pltpu.SemaphoreType.DMA((4,)),
        ],
        compiler_params=vmem(8),
        cost_estimate=cost(4 * 10**9, 2 * slots * per * LANES * 4),
        name="key_ranges",
    )(*map(in_hbm, (request_ids, prompt_len, slot_page, queries)))
    flipped = pl.pallas_call(
        functools.partial(flip_kernel, page_tokens),
        out_shape=(jax.ShapeDtypeStruct((8, keys), jnp.int32),) * (len(pools) - 1)
        + (jax.ShapeDtypeStruct((head_size, keys), pool.dtype),) * len(pools),
        in_specs=[SMEM] * (len(pools) - 1) + [VMEM] * len(pools),
        out_specs=(VMEM,) * (2 * len(pools) - 1),
        compiler_params=vmem(12),
        cost_estimate=cost(10**9, 4 * pool.size * len(pools)),
        name="flip_keys",
    )(*([far_pages] if paired else []), *pools)
    key_lists, flips = [near_keys, *flipped[:-len(pools)]], flipped[-len(pools):]

    own = pl.pallas_call(
        functools.partial(own_kernel, heads, rows, scale),
        out_shape=jax.ShapeDtypeStruct((per, head_size + LANES), jnp.float32),
        in_specs=[SMEM] + [VMEM] * 4,
        out_specs=VMEM,
        scratch_shapes=[
            pltpu.VMEM((per, head_size), jnp.bfloat16),
            pltpu.VMEM((2 * round_up(local * drafts, 16), head_size), jnp.bfloat16),
        ],
        compiler_params=vmem(8),
        cost_estimate=cost(4 * per * local * tail_cache.shape[2] * head_size, 2 * tail_cache.size),
        name="own_keys",
    )(tail_len, queries, tail_cache[0], new_kv[0], out_weight)

    block_shape = jax.ShapeDtypeStruct((per, head_size + LANES), jnp.bfloat16)
    scratch = [pltpu.VMEM((min(slots, 4) * per, head_size), jnp.bfloat16)]
    price = cost(4 * slots * per * keys * len(pools) * head_size, 2 * pool.size * len(pools))

    def prefix_column(blocks, first_slot):
        count = len(blocks)
        return pl.pallas_call(
            functools.partial(prefix_kernel, heads, rows, scale, count, count, first_slot),
            out_shape=(block_shape,) * count,
            in_specs=[VMEM] * (count + 2 + 3 * len(pools)),
            out_specs=(VMEM,) * count,
            scratch_shapes=[pltpu.VMEM((count * per, head_size), jnp.bfloat16)],
            compiler_params=vmem(24),
            cost_estimate=cost(price.flops // slots * count, price.bytes_accessed),
            name="prefix_keys",
        )(*blocks, low, high, *key_lists, *flips, *pools)

    def prefix_many(block):
        step = min(slots, 4)
        return pl.pallas_call(
            functools.partial(prefix_kernel, heads, rows, scale, 1, 1, 0),
            out_shape=jax.ShapeDtypeStruct((slots,) + block_shape.shape, jnp.bfloat16),
            grid=(slots // step,),
            in_specs=[
                pl.BlockSpec((step, local, drafts, head_width), lambda i: (i, 0, 0, 0)),
                pl.BlockSpec((step * per, LANES), lambda i: (i, 0)),
                pl.BlockSpec((step * per, LANES), lambda i: (i, 0)),
                pl.BlockSpec((8, keys), lambda i: (0, 0)),
                pl.BlockSpec((head_size, keys), lambda i: (0, 0)),
                pl.BlockSpec((page_count, page_tokens, head_pair), lambda i: (0, 0, 0)),
            ],
            out_specs=pl.BlockSpec((step,) + block_shape.shape, lambda i: (i, 0, 0)),
            scratch_shapes=scratch,
            compiler_params=vmem(24),
            cost_estimate=price,
            name="prefix_keys",
        )(block, low, high, *key_lists, *flips, *pools)

    partial_shape = jax.ShapeDtypeStruct((local, drafts, width), jnp.bfloat16)
    if paired:
        column = [near_queries] + [swap(queries, "blk", blk, mask) for mask in masks[1:]]
        sums = [None, *prefix_column(column[1:], 1)] if half > 1 else [None]
        sums[0] = prefix_column(column[:1], 0)[0]
        blocks = [sums[0]] + [
            swap(sums[partners.index(j)], "blk", blk, 2 * j + 1) for j in ORDER_B if j < half
        ]
        share = pl.pallas_call(
            functools.partial(combine_kernel, heads, rows, head_size),
            out_shape=partial_shape,
            in_specs=[VMEM] * (half + 2),
            out_specs=VMEM,
            compiler_params=vmem(12),
            cost_estimate=cost(2 * per * head_size * width, 2 * out_weight.size),
            name="combine_project",
        )(own, *blocks, out_weight)
    else:
        gathered = lax.all_gather(queries, "blk", axis=0)
        blocks = lax.all_to_all(prefix_many(gathered), "blk", 0, 0)
        share = pl.pallas_call(
            functools.partial(combine_many_kernel, heads, rows, head_size),
            out_shape=partial_shape,
            in_specs=[VMEM] * 3,
            out_specs=VMEM,
            compiler_params=vmem(12),
            cost_estimate=cost(2 * per * head_size * width, 2 * out_weight.size),
            name="combine_project",
        )(own, blocks, out_weight)
    if kv in (2, 4):
        shares = [share] + [swap(share, "kv", kv, j) for j in ORDER_C if j < kv]
    else:
        shares = [lax.psum(share, "kv")]
    hidden_out, scores = pl.pallas_call(
        final_kernel,
        out_shape=(
            jax.ShapeDtypeStruct(hidden.shape, hidden.dtype),
            jax.ShapeDtypeStruct((local,), jnp.float32),
        ),
        in_specs=[VMEM] * (len(shares) + 3),
        out_specs=(VMEM, VMEM),
        compiler_params=vmem(8),
        cost_estimate=cost(1, 2 * hidden.size * 6),
        name="residual_scores",
    )(*shares, hidden, norm_gain.reshape(1, width), score_weight.reshape(1, width))
    return hidden_out, scores


def solution(mesh):
    in_specs = (
        P("kv", "blk", None, None),
        P("blk"),
        P(),
        P(),
        P("blk"),
        P("kv", "blk", None, None),
        P("blk", None, "kv"),
        P("kv", "blk", None, None),
        P("blk", None, None),
        P("kv", None),
        P(),
        P(),
    )
    out_specs = (P("blk", None, None), P("blk"))
    sizes = (mesh.shape["blk"], mesh.shape["kv"])
    return jax.shard_map(
        functools.partial(body, sizes), mesh=mesh, in_specs=in_specs, out_specs=out_specs, check_vma=False
    )
```

```python
import functools

import jax
import jax.numpy as jnp
from jax import lax
from jax.experimental import pallas as pl
from jax.experimental.pallas import tpu as pltpu
from jax.sharding import PartitionSpec as P

SAMPLES = 16
CHUNK = 8
ORDER_A = (2, 3, 1)
ORDER_B = (3, 1, 2)
ORDER_C = (1, 2, 3)
LANES = 128
FLOOR = -(2.0**100)
LOG2E = 1.4426950408889634
ANY = pl.BlockSpec(memory_space=pl.ANY)
VMEM = pl.BlockSpec(memory_space=pltpu.VMEM)
SMEM = pl.BlockSpec(memory_space=pltpu.SMEM)


def round_up(value, unit):
    return (value + unit - 1) // unit * unit


def cost(flops, size):
    return pl.CostEstimate(flops=flops, bytes_accessed=size, transcendentals=0)


def vmem(mebibytes):
    return pltpu.CompilerParams(vmem_limit_bytes=mebibytes * 1024 * 1024)


def iota(shape, dim):
    return lax.broadcasted_iota(jnp.int32, shape, dim)


def rounded_peak(peak):
    return peak.astype(jnp.bfloat16).astype(jnp.float32)


def pack_stats(peak, den):
    high = den.astype(jnp.bfloat16).astype(jnp.float32)
    lane = iota((peak.shape[0], LANES), 1)
    stats = jnp.where(lane == 0, peak, jnp.where(lane == 1, high, den - high))
    return jnp.where(lane < 3, stats, 0.0)


def unpack_stats(stats):
    stats = stats.astype(jnp.float32)
    return stats[:, 0:1], stats[:, 1:2] + stats[:, 2:3]


def spread_rows(dest, base, block, heads, head_size, rows):
    reqs, drafts, _ = block.shape
    pad = rows - reqs * drafts
    for c in range(heads):
        cols = pl.ds(c * head_size, head_size)
        for r in range(reqs):
            dest[pl.ds(base + c * rows + r * drafts, drafts), :] = block[r, :, cols]
        if pad:
            dest[pl.ds(base + c * rows + reqs * drafts, pad), :] = jnp.zeros((pad, head_size), dest.dtype)


def write_keys(page_ref, key_ref, page_tokens):
    lane = iota((8, page_tokens), 1)
    for s in range(page_ref.shape[0]):
        key_ref[:, pl.ds(s * page_tokens, page_tokens)] = lane + page_ref[s] * page_tokens


def layout_kernel(device_of, slots, local, rows, heads, drafts, page_tokens,
                  ids_hbm, len_hbm, page_hbm, q_ref,
                  low_ref, high_ref, key_ref, q_out_ref,
                  ids_ref, len_ref, page_ref, start_ref, sems):
    pairs = [(ids_hbm, ids_ref), (len_hbm, len_ref), (page_hbm, page_ref), (q_ref, q_out_ref)]
    copies = [pltpu.make_async_copy(a, b, sems.at[i]) for i, (a, b) in enumerate(pairs)]
    for copy in copies:
        copy.start()
    me = lax.axis_index("blk")
    prompts = len_ref.shape[0]
    shift = SAMPLES.bit_length() - 1
    for copy in copies[:3]:
        copy.wait()

    def place(p, start):
        start_ref[p] = start
        return start + lax.div(len_ref[p] + page_tokens - 1, page_tokens) * page_tokens

    lax.fori_loop(0, prompts, place, jnp.int32(0), unroll=prompts <= 4)
    request = iota((heads * rows, LANES), 0) % rows // drafts

    def one(j, _):
        device = device_of(j, me)
        low = jnp.zeros((heads * rows, LANES), jnp.int32)
        high = low
        for r in range(local):
            prompt = lax.shift_right_logical(ids_ref[device * local + r], shift)
            start = start_ref[prompt]
            low = jnp.where(request == r, start, low)
            high = jnp.where(request == r, start + len_ref[prompt], high)
        place_at = pl.ds(j * heads * rows, heads * rows)
        low_ref[place_at, :] = low
        high_ref[place_at, :] = high
        return 0

    if slots <= 8:
        for j in range(slots):
            one(j, 0)
    else:
        lax.fori_loop(0, slots, one, 0)
    write_keys(page_ref, key_ref, page_tokens)
    for copy in copies[3:]:
        copy.wait()


def flip_kernel(page_tokens, *refs):
    pools = 2 if len(refs) == 6 else 1
    page_refs, pool_refs, key_refs, flip_refs = refs[:pools - 1], refs[pools - 1:2 * pools - 1], refs[2 * pools - 1:-pools], refs[-pools:]
    for page_ref, key_ref in zip(page_refs, key_refs):
        write_keys(page_ref, key_ref, page_tokens)
    for pool_ref, flip_ref in zip(pool_refs, flip_refs):
        pages, tokens, head_pair = pool_ref.shape
        keys = pool_ref[:, :, :head_pair // 2].reshape(pages * tokens, head_pair // 2)
        flip_ref[...] = keys.T


def prefix_kernel(heads, rows, scale, sources, parts_out, first_slot, *refs):
    q_refs, refs = refs[:sources], refs[sources:]
    (low_ref, high_ref), refs = refs[:2], refs[2:]
    both_refs, out_refs, q_rows = refs[:-parts_out - 1], refs[-parts_out - 1:-1], refs[-1]
    count = len(both_refs) // 3
    key_refs, flip_refs, pool_refs = both_refs[:count], both_refs[count:2 * count], both_refs[2 * count:]
    blocks = list(q_refs) if len(q_refs[0].shape) == 3 else [q_refs[0].at[j] for j in range(q_refs[0].shape[0])]
    slots = len(blocks)
    pages, page_tokens, head_pair = pool_refs[0].shape
    head_size = head_pair // 2
    for j, block in enumerate(blocks):
        spread_rows(q_rows, j * heads * rows, block, heads, head_size, rows)
    ranges = pl.ds(first_slot * heads * rows, slots * heads * rows)
    low, high = low_ref[ranges, :], high_ref[ranges, :]
    span = (high - low).astype(jnp.uint32)
    queries = q_rows[...]
    chunk = CHUNK if pages % CHUNK == 0 else pages
    masked = []
    for key_ref, flip_ref, pool_ref in zip(key_refs, flip_refs, pool_refs):
        for first in range(0, pages, chunk):
            at = first * page_tokens
            logits = jnp.dot(queries, flip_ref[:, at:at + chunk * page_tokens], preferred_element_type=jnp.float32)
            parts = []
            for k in range(0, chunk * page_tokens, LANES):
                key = key_ref[0:1, at + k:at + k + LANES]
                live = (key - low).astype(jnp.uint32) < span
                parts.append(jnp.where(live, logits[:, k:k + LANES] * scale, FLOOR))
            masked.append((pool_ref, first, jnp.concatenate(parts, axis=1)))
    num = den = peak = None
    for pool_ref, first, logits in masked:
        top = rounded_peak(jnp.max(logits, axis=1, keepdims=True))
        if peak is not None:
            top = jnp.maximum(top, peak)
        weights = jnp.exp2(logits - top)
        chunk_den = jnp.sum(weights, axis=1, keepdims=True)
        values = pool_ref[first:first + chunk, :, head_size:].reshape(chunk * page_tokens, head_size)
        chunk_num = jnp.dot(weights.astype(jnp.bfloat16), values, preferred_element_type=jnp.float32)
        if peak is None:
            num, den = chunk_num, chunk_den
        else:
            kept = jnp.exp2(peak - top)
            num, den = num * kept + chunk_num, den * kept + chunk_den
        peak = top
    per = heads * rows
    stats = pack_stats(peak, den)
    outs = list(out_refs) if len(out_refs[0].shape) == 2 else [out_refs[0].at[j] for j in range(slots)]
    for j, out_ref in enumerate(outs):
        out_ref[:, :head_size] = num[j * per:(j + 1) * per].astype(out_ref.dtype)
        out_ref[:, head_size:] = stats[j * per:(j + 1) * per].astype(out_ref.dtype)


def own_kernel(heads, rows, scale, len_ref, q_ref, tail_ref, fresh_ref, weight_ref, out_ref, q_rows, f_rows):
    del weight_ref
    reqs, drafts, _ = q_ref.shape
    tail = tail_ref.shape[1]
    head_size = tail_ref.shape[2] // 2
    spread_rows(q_rows, 0, q_ref, heads, head_size, rows)
    fresh_rows = f_rows.shape[0] // 2
    spread_rows(f_rows, 0, fresh_ref, 2, head_size, fresh_rows)
    queries = q_rows[...]
    contract = (((1,), (1,)), ((), ()))
    logits = lax.dot_general(
        queries, tail_ref[:, :, :head_size].reshape(reqs * tail, head_size),
        contract, preferred_element_type=jnp.float32,
    )
    total = heads * rows
    row = iota((total, tail), 0) % rows
    lane = iota((total, tail), 1)
    parts = []
    for r in range(reqs):
        live = (row // drafts == r) & (lane < len_ref[r])
        parts.append(jnp.where(live, logits[:, r * tail:(r + 1) * tail] * scale, FLOOR))
    fresh = lax.dot_general(
        queries, f_rows[0:fresh_rows, :], contract, preferred_element_type=jnp.float32
    )
    row = iota((total, fresh_rows), 0) % rows
    key = iota((total, fresh_rows), 1)
    live = (row // drafts == key // drafts) & (key % drafts <= row % drafts)
    fresh = jnp.where(live, fresh * scale, FLOOR)
    logits = jnp.concatenate(parts, axis=1)
    peak = jnp.maximum(
        jnp.max(logits, axis=1, keepdims=True), jnp.max(fresh, axis=1, keepdims=True)
    )
    peak = rounded_peak(peak)
    weights = jnp.exp2(logits - peak)
    fresh = jnp.exp2(fresh - peak)
    den = jnp.sum(weights, axis=1, keepdims=True) + jnp.sum(fresh, axis=1, keepdims=True)
    num = jnp.dot(
        weights.astype(jnp.bfloat16), tail_ref[:, :, head_size:].reshape(reqs * tail, head_size),
        preferred_element_type=jnp.float32,
    )
    num = num + jnp.dot(
        fresh.astype(jnp.bfloat16), f_rows[fresh_rows:2 * fresh_rows, :], preferred_element_type=jnp.float32
    )
    out_ref[:, :head_size] = num
    out_ref[:, head_size:] = pack_stats(peak, den)


def summed_parts(blocks, head_size):
    nums = [b[:, :head_size].astype(jnp.float32) for b in blocks]
    stats = [unpack_stats(b[:, head_size:]) for b in blocks]
    peak = functools.reduce(jnp.maximum, [s[0] for s in stats])
    factors = [jnp.exp2(s[0] - peak) for s in stats]
    num = sum(n * f for n, f in zip(nums, factors))
    den = sum(s[1] * f for s, f in zip(stats, factors))
    return num, peak, den


def project(num, den, weight_ref, out_ref, heads, rows):
    reqs, drafts, _ = out_ref.shape
    attention = num / den
    head_size = attention.shape[1]
    value = sum(
        jnp.dot(
            attention[c * rows:(c + 1) * rows, :].astype(jnp.bfloat16), weight_ref[c * head_size:(c + 1) * head_size, :],
            preferred_element_type=jnp.float32,
        )
        for c in range(heads)
    ).astype(out_ref.dtype)
    for r in range(reqs):
        out_ref[r] = value[r * drafts:(r + 1) * drafts, :]


def combine_kernel(heads, rows, head_size, *refs):
    *block_refs, weight_ref, out_ref = refs
    num, _, den = summed_parts([b[...] for b in block_refs], head_size)
    project(num, den, weight_ref, out_ref, heads, rows)


def combine_many_kernel(heads, rows, head_size, own_ref, many_ref, weight_ref, out_ref):
    def one(j, carry):
        num, peak, den = carry
        block = many_ref[j]
        next_peak, next_den = unpack_stats(block[:, head_size:])
        top = jnp.maximum(peak, next_peak)
        old, new = jnp.exp2(peak - top), jnp.exp2(next_peak - top)
        return num * old + block[:, :head_size].astype(jnp.float32) * new, top, den * old + next_den * new

    own = own_ref[...]
    carry = (own[:, :head_size], *unpack_stats(own[:, head_size:]))
    num, _, den = lax.fori_loop(0, many_ref.shape[0], one, carry)
    project(num, den, weight_ref, out_ref, heads, rows)


def final_kernel(*refs):
    *part_refs, hidden_ref, gain_ref, score_ref, out_ref, scores_ref = refs
    reqs, drafts, width = hidden_ref.shape
    mix = gain_ref[...] * score_ref[...]
    lane = iota((1, LANES), 1)
    scores = jnp.zeros((1, LANES), jnp.float32)
    for r in range(reqs):
        total = sum(p[r].astype(jnp.float32) for p in part_refs)
        value = (hidden_ref[r].astype(jnp.float32) + total).astype(out_ref.dtype)
        out_ref[r] = value
        last = value.astype(jnp.float32)[drafts - 1:drafts, :]
        square = jnp.sum(last * last, axis=1, keepdims=True) / width
        score = jnp.sum(last * mix, axis=1, keepdims=True) * lax.rsqrt(square + 1e-06)
        scores = jnp.where(lane == r, score, scores)
    scores_ref[...] = scores[0, :reqs]


def body(sizes, prefix_pool, slot_page, prompt_len, request_ids, tail_len, tail_cache, queries, new_kv, hidden,
         out_weight, norm_gain, score_weight):
    blk, kv = sizes
    pool = prefix_pool[0]
    page_count, page_tokens, head_pair = pool.shape
    head_size = head_pair // 2
    local, drafts, head_width = queries.shape
    heads = head_width // head_size
    rows = local * drafts
    if heads * rows % 8:
        rows = round_up(rows, 16)
    per = heads * rows
    keys = page_count * page_tokens
    width = hidden.shape[2]
    scale = head_size ** (-0.5) * LOG2E
    paired = blk in (2, 4, 8)
    half = blk // 2
    partners = [0] + [j for j in ORDER_A if j < half]
    masks = [0] + [2 * j + 1 for j in partners[1:]]

    def swap(x, axis, size, mask):
        return lax.ppermute(x, axis, [(i, i ^ mask) for i in range(size)])

    def device_of(j, me):
        return me ^ masks[j] if paired else j

    slots = half if paired else blk
    pools = [pool]
    if paired:
        pools.append(swap(pool, "blk", blk, 1))
        far_pages = swap(slot_page, "blk", blk, 1)

    in_hbm = functools.partial(pltpu.with_memory_space_constraint, memory_space=pltpu.HBM)
    low, high, near_keys, near_queries = pl.pallas_call(
        functools.partial(layout_kernel, device_of, slots, local, rows, heads, drafts, page_tokens),
        out_shape=(
            jax.ShapeDtypeStruct((slots * per, LANES), jnp.int32),
            jax.ShapeDtypeStruct((slots * per, LANES), jnp.int32),
            jax.ShapeDtypeStruct((8, keys), jnp.int32),
            jax.ShapeDtypeStruct(queries.shape, queries.dtype),
        ),
        in_specs=[ANY] * 4,
        out_specs=(VMEM,) * 3 + (ANY,),
        scratch_shapes=[
            pltpu.SMEM(request_ids.shape, jnp.int32),
            pltpu.SMEM(prompt_len.shape, jnp.int32),
            pltpu.SMEM(slot_page.shape, jnp.int32),
            pltpu.SMEM(prompt_len.shape, jnp.int32),
            pltpu.SemaphoreType.DMA((4,)),
        ],
        compiler_params=vmem(8),
        cost_estimate=cost(4 * 10**9, 2 * slots * per * LANES * 4),
        name="key_ranges",
    )(*map(in_hbm, (request_ids, prompt_len, slot_page, queries)))
    flipped = pl.pallas_call(
        functools.partial(flip_kernel, page_tokens),
        out_shape=(jax.ShapeDtypeStruct((8, keys), jnp.int32),) * (len(pools) - 1)
        + (jax.ShapeDtypeStruct((head_size, keys), pool.dtype),) * len(pools),
        in_specs=[SMEM] * (len(pools) - 1) + [VMEM] * len(pools),
        out_specs=(VMEM,) * (2 * len(pools) - 1),
        compiler_params=vmem(12),
        cost_estimate=cost(10**9, 4 * pool.size * len(pools)),
        name="flip_keys",
    )(*([far_pages] if paired else []), *pools)
    key_lists, flips = [near_keys, *flipped[:-len(pools)]], flipped[-len(pools):]

    own = pl.pallas_call(
        functools.partial(own_kernel, heads, rows, scale),
        out_shape=jax.ShapeDtypeStruct((per, head_size + LANES), jnp.float32),
        in_specs=[SMEM] + [VMEM] * 4,
        out_specs=VMEM,
        scratch_shapes=[
            pltpu.VMEM((per, head_size), jnp.bfloat16),
            pltpu.VMEM((2 * round_up(local * drafts, 16), head_size), jnp.bfloat16),
        ],
        compiler_params=vmem(8),
        cost_estimate=cost(4 * per * local * tail_cache.shape[2] * head_size, 2 * tail_cache.size),
        name="own_keys",
    )(tail_len, queries, tail_cache[0], new_kv[0], out_weight)

    block_shape = jax.ShapeDtypeStruct((per, head_size + LANES), jnp.bfloat16)
    scratch = [pltpu.VMEM((min(slots, 4) * per, head_size), jnp.bfloat16)]
    price = cost(4 * slots * per * keys * len(pools) * head_size, 2 * pool.size * len(pools))

    def prefix_column(blocks, first_slot):
        count = len(blocks)
        return pl.pallas_call(
            functools.partial(prefix_kernel, heads, rows, scale, count, count, first_slot),
            out_shape=(block_shape,) * count,
            in_specs=[VMEM] * (count + 2 + 3 * len(pools)),
            out_specs=(VMEM,) * count,
            scratch_shapes=[pltpu.VMEM((count * per, head_size), jnp.bfloat16)],
            compiler_params=vmem(24),
            cost_estimate=cost(price.flops // slots * count, price.bytes_accessed),
            name="prefix_keys",
        )(*blocks, low, high, *key_lists, *flips, *pools)

    def prefix_many(block):
        step = min(slots, 4)
        return pl.pallas_call(
            functools.partial(prefix_kernel, heads, rows, scale, 1, 1, 0),
            out_shape=jax.ShapeDtypeStruct((slots,) + block_shape.shape, jnp.bfloat16),
            grid=(slots // step,),
            in_specs=[
                pl.BlockSpec((step, local, drafts, head_width), lambda i: (i, 0, 0, 0)),
                pl.BlockSpec((step * per, LANES), lambda i: (i, 0)),
                pl.BlockSpec((step * per, LANES), lambda i: (i, 0)),
                pl.BlockSpec((8, keys), lambda i: (0, 0)),
                pl.BlockSpec((head_size, keys), lambda i: (0, 0)),
                pl.BlockSpec((page_count, page_tokens, head_pair), lambda i: (0, 0, 0)),
            ],
            out_specs=pl.BlockSpec((step,) + block_shape.shape, lambda i: (i, 0, 0)),
            scratch_shapes=scratch,
            compiler_params=vmem(24),
            cost_estimate=price,
            name="prefix_keys",
        )(block, low, high, *key_lists, *flips, *pools)

    partial_shape = jax.ShapeDtypeStruct((local, drafts, width), jnp.bfloat16)
    if paired:
        column = [near_queries] + [swap(queries, "blk", blk, mask) for mask in masks[1:]]
        sums = [None, *prefix_column(column[1:], 1)] if half > 1 else [None]
        sums[0] = prefix_column(column[:1], 0)[0]
        blocks = [sums[0]] + [
            swap(sums[partners.index(j)], "blk", blk, 2 * j + 1) for j in ORDER_B if j < half
        ]
        share = pl.pallas_call(
            functools.partial(combine_kernel, heads, rows, head_size),
            out_shape=partial_shape,
            in_specs=[VMEM] * (half + 2),
            out_specs=VMEM,
            compiler_params=vmem(12),
            cost_estimate=cost(2 * per * head_size * width, 2 * out_weight.size),
            name="combine_project",
        )(own, *blocks, out_weight)
    else:
        gathered = lax.all_gather(queries, "blk", axis=0)
        blocks = lax.all_to_all(prefix_many(gathered), "blk", 0, 0)
        share = pl.pallas_call(
            functools.partial(combine_many_kernel, heads, rows, head_size),
            out_shape=partial_shape,
            in_specs=[VMEM] * 3,
            out_specs=VMEM,
            compiler_params=vmem(12),
            cost_estimate=cost(2 * per * head_size * width, 2 * out_weight.size),
            name="combine_project",
        )(own, blocks, out_weight)
    out_type = hidden.dtype
    if kv in (2, 4):
        arrived = {j: swap(share, "kv", kv, j) for j in ORDER_C if j < kv}
        last = arrived.pop(2 if kv == 4 else 1)
        early = hidden.astype(jnp.float32) + share.astype(jnp.float32)
        for value in arrived.values():
            early = early + value.astype(jnp.float32)
        hidden, shares = early, [last]
    else:
        shares = [lax.psum(share, "kv")]
    hidden_out, scores = pl.pallas_call(
        final_kernel,
        out_shape=(
            jax.ShapeDtypeStruct(hidden.shape, out_type),
            jax.ShapeDtypeStruct((local,), jnp.float32),
        ),
        in_specs=[VMEM] * (len(shares) + 3),
        out_specs=(VMEM, VMEM),
        compiler_params=vmem(8),
        cost_estimate=cost(1, 2 * hidden.size * 6),
        name="residual_scores",
    )(*shares, hidden, norm_gain.reshape(1, width), score_weight.reshape(1, width))
    return hidden_out, scores


def solution(mesh):
    in_specs = (
        P("kv", "blk", None, None),
        P("blk"),
        P(),
        P(),
        P("blk"),
        P("kv", "blk", None, None),
        P("blk", None, "kv"),
        P("kv", "blk", None, None),
        P("blk", None, None),
        P("kv", None),
        P(),
        P(),
    )
    out_specs = (P("blk", None, None), P("blk"))
    sizes = (mesh.shape["blk"], mesh.shape["kv"])
    return jax.shard_map(
        functools.partial(body, sizes), mesh=mesh, in_specs=in_specs, out_specs=out_specs, check_vma=False
    )
```
